768 devices in a mesh: dp: 48 (over z_hi, y, core), fsdp: 16 (over x, z_lo).
Axes of the slice: x: 4, y: 8, z: 12 (z_hi: 3, z_lo: 4; z = z_hi * 4 + z_lo), core: 2. Of those that a mesh axis runs over, the one named last changes fastest.
Arguments:
- queries: bfloat16 [18432, 4096], P('dp', 'fsdp'), may hold values from -16 to 16
- key_rows: bfloat16 [18432, 4096], P('dp', 'fsdp'), may hold values from -16 to 16
- value_rows: bfloat16 [18432, 4096], P('dp', 'fsdp'), may hold values from -6 to 6
- image_ids: int32 [18432], P('dp'), may hold values from 0 to 18304, as said below
- send_slot: int32 [18432], P('dp'), may hold values from 0 to 511, as said below
- out_weight: bfloat16 [4096, 6144], P('fsdp'), may hold values from -0.09375 to 0.09375
- grad_out: bfloat16 [24576, 6144], P('dp'), may hold values from -0.59765625 to 0.59765625
Outputs:
- grad_query: bfloat16 [18432, 4096], P('dp', 'fsdp')
- grad_key: bfloat16 [18432, 4096], P('dp', 'fsdp')
- grad_value: bfloat16 [18432, 4096], P('dp', 'fsdp')
- grad_weight: float32 [4096, 6144], P('fsdp', 'dp')
The draws below stay inside these ranges and needn't reach their ends.
Inputs may be any that keep to these rules, and one draw needn't show every extreme that they name: `send_slot`: each rank moves at most one image, of exactly 128 rows, to the next rank along dp (the last rank to the first); its rows take slots 384 to 511 in order; every other row keeps its own position in its rank; some rank moves an image in every draw. `image_ids`: images are runs of consecutive rows of one rank made of 1 to 3 whole aligned blocks of 128 rows; the id is the global index of the image's first row.
All inputs are finite; a program needn't handle non-finite values.
Results may differ from the reference program's by a relative error of at most 0.0074.
Values may be sent and summed in bfloat16 or wider, within the bound.
No kernel may reach another device: no remote copies, remote signals or barrier semaphores. Data moves between devices by JAX's collectives and lax.ppermute only.
A program may use at most 64 MiB of HBM per device.

```python
import jax
import jax.numpy as jnp
from jax import lax

D = 6144
HD = 128
HEAD_DEV = 2
PIECE = 128
ROWS = 384
SLOT_DEV = 512
HEADS = 32
TOKENS = 18432
SLOTS = 24576
N_DP = 48
N_FSDP = 16


def layout(key):
    pattern_key, force_key, pick_key = jax.random.split(key, 3)
    sender = jnp.arange(N_DP, dtype=jnp.int32)
    forced = jax.random.randint(force_key, (), 0, N_DP)
    pattern = jax.random.randint(pattern_key, (N_DP,), 0, 4)
    pattern = jnp.where(sender == forced, pattern % 3, pattern).astype(jnp.int32)
    pattern = jnp.where(sender == N_DP - 1, 2 * (pattern % 2), pattern).astype(jnp.int32)
    start_table = jnp.array([[1, 1, 1], [1, 1, 0], [1, 0, 1], [1, 0, 0]], jnp.int32)
    moved_table = jnp.array([0, 0, 2, -1], jnp.int32)
    picked = jax.random.randint(pick_key, (N_DP,), 0, 3).astype(jnp.int32)
    moved = jnp.where(pattern == 0, picked, moved_table[pattern])
    starts = start_table[pattern]
    unit_pos = jnp.arange(3, dtype=jnp.int32)
    first_unit = lax.cummax(jnp.where(starts == 1, unit_pos[None, :], -1), axis=1)
    row_pos = jnp.arange(ROWS, dtype=jnp.int32)
    row_unit = row_pos // PIECE
    ids_out = sender[:, None] * ROWS + first_unit[:, row_unit] * PIECE
    slots_out = jnp.where(row_unit[None, :] == moved[:, None], ROWS + row_pos[None, :] % PIECE, row_pos[None, :])
    return (slots_out.reshape(TOKENS).astype(jnp.int32), ids_out.reshape(TOKENS).astype(jnp.int32))


def draw_send_slot(key, part):
    return layout(key)[0]


def draw_image_ids(key, part):
    return layout(key)[1]


def draw_queries(key, part):
    key = jax.random.fold_in(key, 11)
    array_shape = (TOKENS, HEADS * HD)
    return jax.random.normal(key, array_shape, jnp.float32).astype(jnp.bfloat16)


def draw_key_rows(key, part):
    key = jax.random.fold_in(key, 23)
    array_shape = (TOKENS, HEADS * HD)
    return jax.random.normal(key, array_shape, jnp.float32).astype(jnp.bfloat16)


def strengthened(values, rng, source, target, parts, factor):
    owner, partner = [(jnp.arange(values.shape[dim]) // (values.shape[dim] // parts)).reshape([-1 if axis == dim else 1 for axis in range(values.ndim)]) for dim in (source, target)]
    chosen = jax.random.permutation(rng, parts)[partner]
    strong = (owner == chosen) | (owner == (partner + parts // 2) % parts)
    return jnp.where(strong, factor * values, values)


def block_levels(own_key, shape, cuts, least, largest):
    gain, own = 1.0, jax.random.fold_in(own_key, 6)
    for dim, shards_of in cuts:
        draws = jnp.exp(jax.random.uniform(jax.random.fold_in(own, dim), (shards_of,), jnp.float32, least / len(cuts), largest / len(cuts)))
        gain = gain * jnp.repeat(draws, shape[dim] // shards_of).reshape([-1 if axis == dim else 1 for axis in range(len(shape))])
    return gain


def noise(stream_key, extent, spread, most, shards=(), kind=jnp.bfloat16):
    gain = block_levels(stream_key, extent, shards, -0.22, 0.18) if shards else 1.0
    result = jax.random.normal(stream_key, extent, jnp.float32) * spread * gain
    return jnp.minimum(jnp.maximum(result, -most), most).astype(kind)


def heavy_noise(stream_key, extent, spread, limit, shards, heavy, kind=jnp.bfloat16):
    entries = spread * jax.random.normal(stream_key, extent, jnp.float32)
    if shards:
        entries = entries * block_levels(stream_key, extent, shards, -0.22, 0.18)
    return jnp.clip(strengthened(entries, jax.random.fold_in(stream_key, 3), *heavy), -limit, limit).astype(kind)


def setup_inputs(seed: int = 0) -> dict:
    streams_of = jax.random.split(jax.random.key(seed), 8)
    queries = draw_queries(jax.random.fold_in(streams_of[7], 71), 0)
    key_rows = draw_key_rows(jax.random.fold_in(streams_of[7], 71), 0)
    value_rows = noise(streams_of[2], (TOKENS, HEADS * HD), 1.0, 6.0, ((0, 48), (1, 16)))
    image_ids = draw_image_ids(jax.random.fold_in(streams_of[7], 71), 0)
    send_slot = draw_send_slot(jax.random.fold_in(streams_of[7], 71), 0)
    out_weight = noise(streams_of[5], (HEADS * HD, D), (HEADS * HD) ** -0.5, 0.09375, ((0, 16),))
    grad_out = heavy_noise(streams_of[6], (SLOTS, D), 0.1, 0.59765625, ((0, 48),), (0, 1, 48, 3.25))
    return dict(queries=queries, key_rows=key_rows, value_rows=value_rows, image_ids=image_ids, send_slot=send_slot, out_weight=out_weight, grad_out=grad_out)


def rounded(values):
    return lax.optimization_barrier(values.astype(jnp.bfloat16)).astype(jnp.float32)


def attend(query_blk, key_blk, value_blk, labels, grad_blk):
    score_scale = HD ** -0.5
    query_f = query_blk.astype(jnp.float32)
    key_f = key_blk.astype(jnp.float32)
    value_f = value_blk.astype(jnp.float32)
    scores = jnp.einsum("qhd,khd->hqk", query_f, key_f) * score_scale
    same_image = labels[:, None] == labels[None, :]
    scores = jnp.where(same_image[None], scores, -jnp.inf)
    row_top = jnp.max(scores, axis=-1, keepdims=True)
    expo = jnp.exp(scores - row_top)
    weights = expo / jnp.sum(expo, axis=-1, keepdims=True)
    prob_round = rounded(weights)
    context = jnp.einsum("hqk,khd->qhd", prob_round, value_f).astype(jnp.bfloat16)
    grad_heads = grad_blk.astype(jnp.float32)
    value_back = jnp.einsum("hqk,qhd->khd", prob_round, grad_heads).astype(jnp.bfloat16)
    grad_prob = jnp.einsum("qhd,khd->hqk", grad_heads, value_f)
    inner_sum = jnp.sum(weights * grad_prob, axis=-1, keepdims=True)
    grad_score = rounded(weights * (grad_prob - inner_sum))
    query_back = (jnp.einsum("hqk,khd->qhd", grad_score, key_f) * score_scale).astype(jnp.bfloat16)
    key_back = (jnp.einsum("hqk,qhd->khd", grad_score, query_f) * score_scale).astype(jnp.bfloat16)
    return context, query_back, key_back, value_back


def reference(queries, key_rows, value_rows, image_ids, send_slot, out_weight, grad_out):
    slot_dev = SLOT_DEV
    slot_total = N_DP * slot_dev
    head_count = HEAD_DEV * N_FSDP
    feat_width = head_count * HD
    sender = jnp.arange(N_DP * ROWS, dtype=jnp.int32) // ROWS
    receiver = jnp.where(send_slot < ROWS, sender, (sender + 1) % N_DP).astype(jnp.int32)
    target = (receiver * slot_dev + send_slot).astype(jnp.int32)

    def place_rows(rows_in):
        return jnp.zeros((slot_total, feat_width), rows_in.dtype).at[target].set(rows_in)

    query_slot = place_rows(queries)
    key_slot = place_rows(key_rows)
    value_slot = place_rows(value_rows)
    slot_image = jnp.full((slot_total,), -1, jnp.int32).at[target].set(image_ids)
    grad_context = jnp.dot(grad_out, out_weight.T, preferred_element_type=jnp.float32).astype(jnp.bfloat16)

    def per_device(index):
        begin = (index * slot_dev).astype(jnp.int32)

        def take_block(array_in):
            return lax.dynamic_slice_in_dim(array_in, begin, slot_dev, 0)

        def heads_of(array_in):
            return take_block(array_in).reshape(slot_dev, head_count, HD)

        return attend(heads_of(query_slot), heads_of(key_slot), heads_of(value_slot),
                      take_block(slot_image), heads_of(grad_context))

    results = lax.map(per_device, jnp.arange(N_DP, dtype=jnp.int32))
    context, query_back, key_back, value_back = [part_out.reshape(slot_total, feat_width) for part_out in results]
    grad_weight = jnp.dot(context.T, grad_out, preferred_element_type=jnp.float32)
    return query_back[target], key_back[target], value_back[target], grad_weight
```

```python
import functools

import jax
import jax.numpy as jnp
from jax import lax
from jax.experimental import pallas as pl
from jax.experimental.pallas import tpu as pltpu
from jax.sharding import PartitionSpec as P

HD = 128
UNIT = 128
NZ, NY, NC = 3, 8, 2
FIRST = (4, 3, 5)
SECOND = (2, 6, 1, 7, 0)
SMEM = pl.BlockSpec(memory_space=pltpu.SMEM)
VMEM = pl.BlockSpec(memory_space=pltpu.VMEM)
PARAMS = pltpu.CompilerParams(vmem_limit_bytes=48 * 1024 * 1024)


def dot(a, b, dims):
    return lax.dot_general(a, b, (dims, ((), ())), preferred_element_type=jnp.float32)


def block_masks(ids_ref, units):
    lane_unit = lax.broadcasted_iota(jnp.int32, (1, units * UNIT), 1) // UNIT
    lane_ids = jnp.full((1, units * UNIT), ids_ref[0], jnp.int32)
    for u in range(1, units):
        lane_ids = jnp.where(lane_unit == u, ids_ref[u * UNIT], lane_ids)
    return [lane_ids == ids_ref[u * UNIT] for u in range(units)]


def softmax(scores):
    expo = jnp.exp(scores - jnp.max(scores, axis=-1, keepdims=True))
    return expo / jnp.sum(expo, axis=-1, keepdims=True)


def unit_weights(q, k, mask):
    return softmax(jnp.where(mask, dot(q, k, ((1,), (1,))) * HD**-0.5, -jnp.inf))


def moved_unit(slot_ref, units):
    unit = jnp.int32(0)
    for u in range(1, units):
        unit = jnp.where(slot_ref[u * UNIT] >= units * UNIT, u, unit)
    return unit


def moved_kernel(units, slot_ref, q_ref, k_ref, v_ref, out_ref):
    moves = slot_ref[moved_unit(slot_ref, units) * UNIT] >= units * UNIT
    for h in range(q_ref.shape[1] // HD):
        cols = pl.ds(h * HD, HD)
        w = softmax(dot(q_ref[:, cols], k_ref[:, cols], ((1,), (1,))) * HD**-0.5)
        ctx = dot(v_ref[:, cols].T, w.astype(jnp.bfloat16), ((1,), (1,)))
        out_ref[cols, :] = jnp.where(moves, ctx, 0.0).astype(jnp.bfloat16)


def moved_context(send_slot, q, k, v):
    units, width = q.shape[0] // UNIT, q.shape[1]
    block = pl.BlockSpec((UNIT, width), lambda i, slot: (moved_unit(slot, units), 0))
    return pl.pallas_call(
        functools.partial(moved_kernel, units),
        grid_spec=pltpu.PrefetchScalarGridSpec(
            num_scalar_prefetch=1,
            grid=(1,),
            in_specs=[block] * 3,
            out_specs=pl.BlockSpec((width, UNIT), lambda i, slot: (0, 0)),
        ),
        out_shape=jax.ShapeDtypeStruct((width, UNIT), jnp.bfloat16),
    )(send_slot, q, k, v)


def context_kernel(ids_ref, slot_ref, q_ref, k_ref, v_ref, out_ref):
    units = q_ref.shape[0] // UNIT
    masks = block_masks(ids_ref, units)
    for h in range(q_ref.shape[1] // HD):
        cols = pl.ds(h * HD, HD)
        v_t = v_ref[:, cols].T
        for u in range(units):
            rows = pl.ds(u * UNIT, UNIT)
            w = unit_weights(q_ref[rows, cols], k_ref[:, cols], masks[u])
            ctx = dot(v_t, w.astype(jnp.bfloat16), ((1,), (1,)))
            stays = slot_ref[u * UNIT] < units * UNIT
            out_ref[cols, rows] = jnp.where(stays, ctx, 0.0).astype(jnp.bfloat16)


def staying_context(image_ids, send_slot, q, k, v):
    return pl.pallas_call(
        context_kernel,
        in_specs=[SMEM, SMEM, VMEM, VMEM, VMEM],
        out_specs=VMEM,
        out_shape=jax.ShapeDtypeStruct(q.shape[::-1], jnp.bfloat16),
        compiler_params=PARAMS,
    )(image_ids, send_slot, q, k, v)


def partial_kernel(picks, stay_ref, came_ref, g_ref, *out_refs):
    me = lax.axis_index("dp")
    z, y, c = me // (NY * NC), (me // NC) % NY, me % NC
    ctx_t = jnp.concatenate([stay_ref[...], came_ref[...]], axis=1)
    width = ctx_t.shape[0]
    for out_ref, (distances, other) in zip(out_refs, picks, strict=True):
        core = 1 - c if other else c
        for n, distance in enumerate(distances):
            dest = [((z + i) % NZ * NY + (y + distance) % NY) * NC + core for i in range(NZ)]
            g = jnp.concatenate([g_ref[:, pl.ds(pl.multiple_of(d * UNIT, UNIT), UNIT)] for d in dest], axis=1)
            part = dot(ctx_t, g, ((1,), (0,))).astype(jnp.bfloat16)
            for i in range(NZ):
                out_ref[pl.ds((n * NZ + i) * width, width), :] = part[:, i * UNIT : (i + 1) * UNIT]


def partial_grad(picks, stay, came, grad_out):
    rows = [len(distances) * NZ * stay.shape[0] for distances, _ in picks]
    return pl.pallas_call(
        functools.partial(partial_kernel, picks),
        in_specs=[VMEM] * 3,
        out_specs=[VMEM] * len(rows),
        out_shape=[jax.ShapeDtypeStruct((r, UNIT), jnp.bfloat16) for r in rows],
        compiler_params=PARAMS,
    )(stay, came, grad_out)


def grad_context_kernel(g_ref, w_ref, out_ref, acc_ref):
    @pl.when(pl.program_id(0) == 0)
    def _():
        acc_ref[...] = jnp.zeros_like(acc_ref)

    acc_ref[...] += dot(g_ref[...], w_ref[...], ((1,), (1,)))

    @pl.when(pl.program_id(0) == pl.num_programs(0) - 1)
    def _():
        out_ref[...] = acc_ref[...].astype(jnp.bfloat16)


def grad_context(grad_out, out_weight):
    rows, depth = grad_out.shape
    width = out_weight.shape[0]
    step = 1024
    return pl.pallas_call(
        grad_context_kernel,
        grid=(depth // step,),
        in_specs=[
            pl.BlockSpec((rows, step), lambda i: (0, i)),
            pl.BlockSpec((width, step), lambda i: (0, i)),
        ],
        out_specs=pl.BlockSpec((rows, width), lambda i: (0, 0)),
        out_shape=jax.ShapeDtypeStruct((rows, width), jnp.bfloat16),
        scratch_shapes=[pltpu.VMEM((rows, width), jnp.float32)],
        compiler_params=PARAMS,
    )(grad_out, out_weight)


def backward_kernel(ids_ref, slot_ref, q_ref, k_ref, v_ref, g_ref, back_ref, dq_ref, dk_ref, dv_ref):
    units = q_ref.shape[0] // UNIT
    masks = block_masks(ids_ref, units)
    for h in range(q_ref.shape[1] // HD):
        cols = pl.ds(h * HD, HD)
        k, v = k_ref[:, cols], v_ref[:, cols]
        dk = jnp.zeros(k.shape, jnp.float32)
        dv = jnp.zeros(v.shape, jnp.float32)
        for u in range(units):
            rows = pl.ds(u * UNIT, UNIT)
            q = q_ref[rows, cols]
            w = unit_weights(q, k, masks[u])
            stays = slot_ref[u * UNIT] < units * UNIT
            g = jnp.where(stays, g_ref[rows, cols].astype(jnp.float32), back_ref[:, cols].astype(jnp.float32))
            g = g.astype(jnp.bfloat16)
            dv += dot(w.astype(jnp.bfloat16), g, ((0,), (0,)))
            dw = dot(g, v, ((1,), (1,)))
            ds = (w * (dw - jnp.sum(w * dw, axis=-1, keepdims=True))).astype(jnp.bfloat16)
            dq_ref[rows, cols] = (dot(ds, k, ((1,), (0,))) * HD**-0.5).astype(jnp.bfloat16)
            dk += dot(ds, q, ((0,), (0,)))
        dk_ref[:, cols] = (dk * HD**-0.5).astype(jnp.bfloat16)
        dv_ref[:, cols] = dv.astype(jnp.bfloat16)


def backward(image_ids, send_slot, q, k, v, g, back):
    return pl.pallas_call(
        backward_kernel,
        in_specs=[SMEM, SMEM] + [VMEM] * 5,
        out_specs=[VMEM] * 3,
        out_shape=[jax.ShapeDtypeStruct(q.shape, jnp.bfloat16)] * 3,
        compiler_params=PARAMS,
    )(image_ids, send_slot, q, k, v, g, back)


PLACES = [(z, y, c) for z in range(NZ) for y in range(NY) for c in range(NC)]


def index(z, y, c):
    return (z % NZ * NY + y % NY) * NC + c


def send(block, to):
    return lax.ppermute(block, "dp", [(index(*p), index(*to(*p))) for p in PLACES])


def along_y(step):
    return lambda z, y, c: (z, y + step, c)


def apart_y(z, y, c):
    return (z, y + 1 - 2 * c, c)


def along_z(step):
    return lambda z, y, c: (z + step, y, c)


def sibling(z, y, c):
    return (z, y, 1 - c)


def total(*terms):
    return sum(t.astype(jnp.float32) for t in terms)


def rounded_total(*terms):
    return total(*terms).astype(jnp.bfloat16)


def local(queries, key_rows, value_rows, image_ids, send_slot, out_weight, grad_out):
    row_count, width = queries.shape
    ranks = lax.axis_size("dp")
    core = lax.axis_index("dp") % NC

    leaving = moved_context(send_slot, queries, key_rows, value_rows)
    came = lax.ppermute(leaving, "dp", [(i, (i + 1) % ranks) for i in range(ranks)])
    stay = staying_context(image_ids, send_slot, queries, key_rows, value_rows)

    (given1,) = partial_grad([(FIRST, True)], stay, came, grad_out)
    got1 = send(given1, sibling)
    given2, = partial_grad([(SECOND, True)], stay, came, grad_out)
    got2 = send(given2, sibling)
    (own,) = partial_grad([(FIRST + SECOND, False)], stay, came, grad_out)

    size = NZ * width
    mine = {d: own[i * size : (i + 1) * size] for i, d in enumerate(FIRST + SECOND)}
    theirs = {d: got1[i * size : (i + 1) * size] for i, d in enumerate(FIRST)}
    theirs |= {d: got2[i * size : (i + 1) * size] for i, d in enumerate(SECOND)}

    half = send(rounded_total(mine[4], theirs[4]), apart_y)
    none = jnp.zeros_like(half)
    up = rounded_total(mine[3], theirs[3], jnp.where(core == 0, half, none))
    down = rounded_total(mine[5], theirs[5], jnp.where(core == 1, half, none))
    up, down = send(up, along_y(1)), send(down, along_y(-1))
    up, down = rounded_total(mine[2], theirs[2], up), rounded_total(mine[6], theirs[6], down)
    up, down = send(up, along_y(1)), send(down, along_y(-1))
    up, down = rounded_total(mine[1], theirs[1], up), rounded_total(mine[7], theirs[7], down)
    up, down = send(up, along_y(1)), send(down, along_y(-1))
    ring = total(mine[0], theirs[0], up, down)
    above = send(ring[width : 2 * width].astype(jnp.bfloat16), along_z(1))
    below = send(ring[2 * width :].astype(jnp.bfloat16), along_z(-1))
    grad_weight = total(ring[:width], above, below)

    grad_ctx = grad_context(grad_out, out_weight)
    back = lax.ppermute(grad_ctx[row_count:], "dp", [((i + 1) % ranks, i) for i in range(ranks)])
    grads = backward(image_ids, send_slot, queries, key_rows, value_rows, grad_ctx, back)
    return (*grads, grad_weight)


def solution(mesh):
    placed = (
        P("dp", "fsdp"),
        P("dp", "fsdp"),
        P("dp", "fsdp"),
        P("dp"),
        P("dp"),
        P("fsdp", None),
        P("dp", None),
    )
    return jax.shard_map(
        local,
        mesh=mesh,
        in_specs=placed,
        out_specs=(P("dp", "fsdp"), P("dp", "fsdp"), P("dp", "fsdp"), P("fsdp", "dp")),
        check_vma=False,
    )
```

```python
import functools

import jax
import jax.numpy as jnp
from jax import lax
from jax.experimental import pallas as pl
from jax.experimental.pallas import tpu as pltpu
from jax.sharding import PartitionSpec as P

HD = 128
UNIT = 128
NZ, NY, NC = 3, 8, 2
ORDER = (4, 3, 5, 2, 6, 1, 7, 0)
SMEM = pl.BlockSpec(memory_space=pltpu.SMEM)
VMEM = pl.BlockSpec(memory_space=pltpu.VMEM)
PARAMS = pltpu.CompilerParams(vmem_limit_bytes=16 * 1024 * 1024)


def dot(a, b, dims):
    return lax.dot_general(a, b, (dims, ((), ())), preferred_element_type=jnp.float32)


def block_masks(ids_ref, units):
    lane_unit = lax.broadcasted_iota(jnp.int32, (1, units * UNIT), 1) // UNIT
    lane_ids = jnp.full((1, units * UNIT), ids_ref[0], jnp.int32)
    for u in range(1, units):
        lane_ids = jnp.where(lane_unit == u, ids_ref[u * UNIT], lane_ids)
    return [lane_ids == ids_ref[u * UNIT] for u in range(units)]


def softmax(scores):
    expo = jnp.exp(scores - jnp.max(scores, axis=-1, keepdims=True))
    return expo / jnp.sum(expo, axis=-1, keepdims=True)


def unit_weights(q, k, mask):
    return softmax(jnp.where(mask, dot(q, k, ((1,), (1,))) * HD**-0.5, -jnp.inf))


def context_kernel(ids_hbm, slot_hbm, q_hbm, k_hbm, v_hbm, g_hbm, w_hbm, stay_ref, leave_ref, g_ref, w_ref,
                   ids_ref, slot_ref, q_ref, k_ref, v_ref, sems):
    pairs = [(ids_hbm, ids_ref), (slot_hbm, slot_ref), (q_hbm, q_ref), (k_hbm, k_ref), (v_hbm, v_ref),
             (g_hbm, g_ref), (w_hbm, w_ref)]
    copies = [pltpu.make_async_copy(src, dst, sems.at[i]) for i, (src, dst) in enumerate(pairs)]
    for copy in copies:
        copy.start()
    for copy in copies[:5]:
        copy.wait()
    units = q_ref.shape[0] // UNIT
    masks = block_masks(ids_ref, units)
    for h in range(q_ref.shape[1] // HD):
        cols = pl.ds(h * HD, HD)
        v_t = v_ref[:, cols].T
        leave = jnp.zeros((HD, UNIT), jnp.float32)
        for u in range(units):
            rows = pl.ds(u * UNIT, UNIT)
            w = unit_weights(q_ref[rows, cols], k_ref[:, cols], masks[u])
            ctx = dot(v_t, w.astype(jnp.bfloat16), ((1,), (1,)))
            stays = slot_ref[u * UNIT] < units * UNIT
            stay_ref[cols, rows] = jnp.where(stays, ctx, 0.0).astype(jnp.bfloat16)
            leave = jnp.where(stays, leave, ctx)
        leave_ref[cols, :] = leave.astype(jnp.bfloat16)
    for copy in copies[5:]:
        copy.wait()


def whole(shape):
    return pl.BlockSpec(shape, lambda i: (0,) * len(shape))


def contexts(image_ids, send_slot, q, k, v, grad_out, out_weight):
    rows, width = q.shape
    shapes = [(width, rows), (width, UNIT), grad_out.shape, out_weight.shape]
    return pl.pallas_call(
        context_kernel,
        in_specs=[pl.BlockSpec(memory_space=pltpu.HBM)] * 7,
        out_specs=[VMEM] * 4,
        out_shape=[jax.ShapeDtypeStruct(shape, jnp.bfloat16) for shape in shapes],
        scratch_shapes=[pltpu.SMEM(image_ids.shape, jnp.int32), pltpu.SMEM(send_slot.shape, jnp.int32)]
        + [pltpu.VMEM(q.shape, jnp.bfloat16)] * 3
        + [pltpu.SemaphoreType.DMA((7,))],
        compiler_params=PARAMS,
    )(*[pltpu.with_memory_space_constraint(x, pltpu.HBM) for x in (image_ids, send_slot, q, k, v, grad_out, out_weight)])


def partial_kernel(other, stay_ref, came_ref, g_ref, out_ref):
    me = lax.axis_index("dp")
    z, y, c = me // (NY * NC), (me // NC) % NY, me % NC
    core = 1 - c if other else c
    ctx_t = jnp.concatenate([stay_ref[...], came_ref[...]], axis=1)
    width = ctx_t.shape[0]
    for n, distance in enumerate(ORDER):
        dest = [((z + i) % NZ * NY + (y + distance) % NY) * NC + core for i in range(NZ)]
        g = jnp.concatenate([g_ref[:, pl.ds(pl.multiple_of(d * UNIT, UNIT), UNIT)] for d in dest], axis=1)
        part = dot(ctx_t, g, ((1,), (0,))).astype(jnp.bfloat16)
        for i in range(NZ):
            out_ref[pl.ds((n * NZ + i) * width, width), :] = part[:, i * UNIT : (i + 1) * UNIT]


def partial_grad(other, stay, came, grad_out):
    shape = (NY * NZ * stay.shape[0], UNIT)
    return pl.pallas_call(
        functools.partial(partial_kernel, other),
        in_specs=[VMEM, VMEM, VMEM],
        out_specs=VMEM,
        out_shape=jax.ShapeDtypeStruct(shape, jnp.bfloat16),
        compiler_params=PARAMS,
    )(stay, came, grad_out)


def grad_context_kernel(g_ref, w_ref, out_ref):
    step = 1024
    acc = jnp.zeros(out_ref.shape, jnp.float32)
    for i in range(0, g_ref.shape[1], step):
        acc += dot(g_ref[:, i : i + step], w_ref[:, i : i + step], ((1,), (1,)))
    out_ref[...] = acc.astype(jnp.bfloat16)


def grad_context(grad_out, out_weight):
    shape = (grad_out.shape[0], out_weight.shape[0])
    return pl.pallas_call(
        grad_context_kernel,
        in_specs=[VMEM] * 2,
        out_specs=VMEM,
        out_shape=jax.ShapeDtypeStruct(shape, jnp.bfloat16),
        compiler_params=PARAMS,
    )(grad_out, out_weight)


def backward_kernel(ids_ref, slot_ref, q_ref, k_ref, v_ref, g_ref, back_ref, dq_ref, dk_ref, dv_ref):
    units = q_ref.shape[0] // UNIT
    masks = block_masks(ids_ref, units)
    for h in range(q_ref.shape[1] // HD):
        cols = pl.ds(h * HD, HD)
        k, v = k_ref[:, cols], v_ref[:, cols]
        dk = jnp.zeros(k.shape, jnp.float32)
        dv = jnp.zeros(v.shape, jnp.float32)
        for u in range(units):
            rows = pl.ds(u * UNIT, UNIT)
            q = q_ref[rows, cols]
            w = unit_weights(q, k, masks[u])
            stays = slot_ref[u * UNIT] < units * UNIT
            g = jnp.where(stays, g_ref[rows, cols].astype(jnp.float32), back_ref[:, cols].astype(jnp.float32))
            g = g.astype(jnp.bfloat16)
            dv += dot(w.astype(jnp.bfloat16), g, ((0,), (0,)))
            dw = dot(g, v, ((1,), (1,)))
            ds = (w * (dw - jnp.sum(w * dw, axis=-1, keepdims=True))).astype(jnp.bfloat16)
            dq_ref[rows, cols] = (dot(ds, k, ((1,), (0,))) * HD**-0.5).astype(jnp.bfloat16)
            dk += dot(ds, q, ((0,), (0,)))
        dk_ref[:, cols] = (dk * HD**-0.5).astype(jnp.bfloat16)
        dv_ref[:, cols] = dv.astype(jnp.bfloat16)


def backward(image_ids, send_slot, q, k, v, g, back):
    return pl.pallas_call(
        backward_kernel,
        grid=(1,),
        in_specs=[SMEM, SMEM] + [whole(q.shape)] * 3 + [whole(g.shape), whole(back.shape)],
        out_specs=[whole(q.shape)] * 3,
        out_shape=[jax.ShapeDtypeStruct(q.shape, jnp.bfloat16)] * 3,
    )(image_ids, send_slot, q, k, v, g, back)


PLACES = [(z, y, c) for z in range(NZ) for y in range(NY) for c in range(NC)]


def index(z, y, c):
    return (z % NZ * NY + y % NY) * NC + c


def send(block, to):
    return lax.ppermute(block, "dp", [(index(*p), index(*to(*p))) for p in PLACES])


def along_y(step):
    return lambda z, y, c: (z, y + step, c)


def apart_y(step):
    return lambda z, y, c: (z, y + step * (1 - 2 * c), c)


def along_z(step):
    return lambda z, y, c: (z + step, y, c)


def sibling(z, y, c):
    return (z, y, 1 - c)


def total(*terms):
    return sum(t.astype(jnp.float32) for t in terms)


def rounded_total(*terms):
    return total(*terms).astype(jnp.bfloat16)


def local(queries, key_rows, value_rows, image_ids, send_slot, out_weight, grad_out):
    row_count, width = queries.shape
    ranks = lax.axis_size("dp")
    core = lax.axis_index("dp") % NC

    stay, leave, g_near, w_near = contexts(
        image_ids, send_slot, queries, key_rows, value_rows, grad_out, out_weight
    )
    came = lax.ppermute(leave, "dp", [(i, (i + 1) % ranks) for i in range(ranks)])
    grad_ctx = grad_context(g_near, w_near)
    stay, grad_ctx = lax.optimization_barrier((stay, grad_ctx))

    given = partial_grad(True, stay, came, g_near)
    got = send(given, sibling)
    own = partial_grad(False, stay, came, g_near)

    size = NZ * width
    mine = {d: own[i * size : (i + 1) * size] for i, d in enumerate(ORDER)}
    theirs = {d: got[i * size : (i + 1) * size] for i, d in enumerate(ORDER)}
    part = {d: rounded_total(mine[d], theirs[d]) for d in (4, 3, 5, 1, 7)}

    far = send(part[4], apart_y(2))
    up, down = send(part[3], along_y(1)), send(part[5], along_y(-1))
    near_up, near_down = send(part[1], along_y(1)), send(part[7], along_y(-1))
    none = jnp.zeros_like(far)
    up = rounded_total(mine[2], theirs[2], up, jnp.where(core == 0, far, none))
    down = rounded_total(mine[6], theirs[6], down, jnp.where(core == 1, far, none))
    up, down = send(up, along_y(2)), send(down, along_y(-2))
    ring = total(mine[0], theirs[0], near_up, near_down, up, down)
    above = send(ring[width : 2 * width].astype(jnp.bfloat16), along_z(1))
    below = send(ring[2 * width :].astype(jnp.bfloat16), along_z(-1))
    grad_weight = total(ring[:width], above, below)

    back = lax.ppermute(grad_ctx[row_count:], "dp", [((i + 1) % ranks, i) for i in range(ranks)])
    grads = backward(image_ids, send_slot, queries, key_rows, value_rows, grad_ctx, back)
    return (*grads, grad_weight)


def solution(mesh):
    placed = (
        P("dp", "fsdp"),
        P("dp", "fsdp"),
        P("dp", "fsdp"),
        P("dp"),
        P("dp"),
        P("fsdp", None),
        P("dp", None),
    )
    return jax.shard_map(
        local,
        mesh=mesh,
        in_specs=placed,
        out_specs=(P("dp", "fsdp"), P("dp", "fsdp"), P("dp", "fsdp"), P("fsdp", "dp")),
        check_vma=False,
    )
```

```python
import functools

import jax
import jax.numpy as jnp
from jax import lax
from jax.experimental import pallas as pl
from jax.experimental.pallas import tpu as pltpu
from jax.sharding import PartitionSpec as P

HD = 128
UNIT = 128
NZ, NY, NC = 3, 8, 2
ORDER = (4, 3, 1, 5, 7, 2, 6, 0)
SMEM = pl.BlockSpec(memory_space=pltpu.SMEM)
VMEM = pl.BlockSpec(memory_space=pltpu.VMEM)
PARAMS = pltpu.CompilerParams(vmem_limit_bytes=16 * 1024 * 1024)


def dot(a, b, dims):
    return lax.dot_general(a, b, (dims, ((), ())), preferred_element_type=jnp.float32)


def block_masks(ids_ref, units):
    lane_unit = lax.broadcasted_iota(jnp.int32, (1, units * UNIT), 1) // UNIT
    lane_ids = jnp.full((1, units * UNIT), ids_ref[0], jnp.int32)
    for u in range(1, units):
        lane_ids = jnp.where(lane_unit == u, ids_ref[u * UNIT], lane_ids)
    return [lane_ids == ids_ref[u * UNIT] for u in range(units)]


def softmax(scores):
    expo = jnp.exp(scores - jnp.max(scores, axis=-1, keepdims=True))
    return expo / jnp.sum(expo, axis=-1, keepdims=True)


def unit_weights(q, k, mask):
    return softmax(jnp.where(mask, dot(q, k, ((1,), (1,))) * HD**-0.5, -jnp.inf))


def context_kernel(ids_hbm, slot_hbm, q_hbm, k_hbm, v_hbm, g_hbm, stay_ref, leave_ref, g_ref,
                   ids_ref, slot_ref, q_ref, k_ref, v_ref, sems):
    pairs = [(ids_hbm, ids_ref), (slot_hbm, slot_ref), (q_hbm, q_ref), (k_hbm, k_ref), (v_hbm, v_ref),
             (g_hbm, g_ref)]
    copies = [pltpu.make_async_copy(src, dst, sems.at[i]) for i, (src, dst) in enumerate(pairs)]
    for copy in copies:
        copy.start()
    for copy in copies[:5]:
        copy.wait()
    units = q_ref.shape[0] // UNIT
    masks = block_masks(ids_ref, units)
    for h in range(q_ref.shape[1] // HD):
        cols = pl.ds(h * HD, HD)
        v_t = v_ref[:, cols].T
        leave = jnp.zeros((HD, UNIT), jnp.float32)
        for u in range(units):
            rows = pl.ds(u * UNIT, UNIT)
            w = unit_weights(q_ref[rows, cols], k_ref[:, cols], masks[u])
            ctx = dot(v_t, w.astype(jnp.bfloat16), ((1,), (1,)))
            stays = slot_ref[u * UNIT] < units * UNIT
            stay_ref[cols, rows] = jnp.where(stays, ctx, 0.0).astype(jnp.bfloat16)
            leave = jnp.where(stays, leave, ctx)
        leave_ref[cols, :] = leave.astype(jnp.bfloat16)
    copies[5].wait()


def in_hbm(x):
    return pltpu.with_memory_space_constraint(x, pltpu.HBM)


def whole(shape):
    return pl.BlockSpec(shape, lambda i: (0,) * len(shape))


def contexts(image_ids, send_slot, q, k, v, grad_out):
    rows, width = q.shape
    shapes = [(width, rows), (width, UNIT), grad_out.shape]
    return pl.pallas_call(
        context_kernel,
        in_specs=[pl.BlockSpec(memory_space=pltpu.HBM)] * 6,
        out_specs=[VMEM] * 3,
        out_shape=[jax.ShapeDtypeStruct(shape, jnp.bfloat16) for shape in shapes],
        scratch_shapes=[pltpu.SMEM(image_ids.shape, jnp.int32), pltpu.SMEM(send_slot.shape, jnp.int32)]
        + [pltpu.VMEM(q.shape, jnp.bfloat16)] * 3
        + [pltpu.SemaphoreType.DMA((6,))],
        compiler_params=PARAMS,
    )(*[in_hbm(x) for x in (image_ids, send_slot, q, k, v, grad_out)])


def partial_kernel(other, stay_ref, came_ref, g_ref, out_ref):
    me = lax.axis_index("dp")
    z, y, c = me // (NY * NC), (me // NC) % NY, me % NC
    core = 1 - c if other else c
    ctx_t = jnp.concatenate([stay_ref[...], came_ref[...]], axis=1)
    width = ctx_t.shape[0]
    for n, distance in enumerate(ORDER):
        dest = [((z + i) % NZ * NY + (y + distance) % NY) * NC + core for i in range(NZ)]
        g = jnp.concatenate([g_ref[:, pl.ds(pl.multiple_of(d * UNIT, UNIT), UNIT)] for d in dest], axis=1)
        part = dot(ctx_t, g, ((1,), (0,))).astype(jnp.bfloat16)
        for i in range(NZ):
            out_ref[pl.ds((n * NZ + i) * width, width), :] = part[:, i * UNIT : (i + 1) * UNIT]


def partial_grad(other, stay, came, grad_out):
    shape = (NY * NZ * stay.shape[0], UNIT)
    return pl.pallas_call(
        functools.partial(partial_kernel, other),
        in_specs=[VMEM, VMEM, VMEM],
        out_specs=VMEM,
        out_shape=jax.ShapeDtypeStruct(shape, jnp.bfloat16),
        compiler_params=PARAMS,
    )(stay, came, grad_out)


def grad_context_kernel(g_ref, w_ref, out_ref, acc_ref):
    i = pl.program_id(0)
    step = w_ref.shape[1]
    part = dot(g_ref[:, pl.ds(pl.multiple_of(i * step, step), step)], w_ref[...], ((1,), (1,)))

    @pl.when(i == 0)
    def _():
        acc_ref[...] = part

    @pl.when(i > 0)
    def _():
        acc_ref[...] += part

    @pl.when(i == pl.num_programs(0) - 1)
    def _():
        out_ref[...] = acc_ref[...].astype(jnp.bfloat16)


def grad_context(grad_out, out_weight):
    shape = (grad_out.shape[0], out_weight.shape[0])
    step = 1536
    return pl.pallas_call(
        grad_context_kernel,
        grid=(grad_out.shape[1] // step,),
        in_specs=[VMEM, pl.BlockSpec((shape[1], step), lambda i: (0, i))],
        out_specs=VMEM,
        out_shape=jax.ShapeDtypeStruct(shape, jnp.bfloat16),
        scratch_shapes=[pltpu.VMEM(shape, jnp.float32)],
        compiler_params=PARAMS,
    )(grad_out, in_hbm(out_weight))


def backward_kernel(ids_ref, slot_ref, q_ref, k_ref, v_ref, g_ref, back_ref, dq_ref, dk_ref, dv_ref):
    units = q_ref.shape[0] // UNIT
    masks = block_masks(ids_ref, units)
    for h in range(q_ref.shape[1] // HD):
        cols = pl.ds(h * HD, HD)
        k, v = k_ref[:, cols], v_ref[:, cols]
        dk = jnp.zeros(k.shape, jnp.float32)
        dv = jnp.zeros(v.shape, jnp.float32)
        for u in range(units):
            rows = pl.ds(u * UNIT, UNIT)
            q = q_ref[rows, cols]
            w = unit_weights(q, k, masks[u])
            stays = slot_ref[u * UNIT] < units * UNIT
            g = jnp.where(stays, g_ref[rows, cols].astype(jnp.float32), back_ref[:, cols].astype(jnp.float32))
            g = g.astype(jnp.bfloat16)
            dv += dot(w.astype(jnp.bfloat16), g, ((0,), (0,)))
            dw = dot(g, v, ((1,), (1,)))
            ds = (w * (dw - jnp.sum(w * dw, axis=-1, keepdims=True))).astype(jnp.bfloat16)
            dq_ref[rows, cols] = (dot(ds, k, ((1,), (0,))) * HD**-0.5).astype(jnp.bfloat16)
            dk += dot(ds, q, ((0,), (0,)))
        dk_ref[:, cols] = (dk * HD**-0.5).astype(jnp.bfloat16)
        dv_ref[:, cols] = dv.astype(jnp.bfloat16)


def backward(image_ids, send_slot, q, k, v, g, back):
    return pl.pallas_call(
        backward_kernel,
        grid=(1,),
        in_specs=[SMEM, SMEM] + [whole(q.shape)] * 3 + [whole(g.shape), whole(back.shape)],
        out_specs=[whole(q.shape)] * 3,
        out_shape=[jax.ShapeDtypeStruct(q.shape, jnp.bfloat16)] * 3,
    )(image_ids, send_slot, q, k, v, g, back)


PLACES = [(z, y, c) for z in range(NZ) for y in range(NY) for c in range(NC)]


def index(z, y, c):
    return (z % NZ * NY + y % NY) * NC + c


def send(block, to):
    return lax.ppermute(block, "dp", [(index(*p), index(*to(*p))) for p in PLACES])


def along_y(step):
    return lambda z, y, c: (z, y + step, c)


def apart_y(step):
    return lambda z, y, c: (z, y + step * (1 - 2 * c), c)


def along_z(step):
    return lambda z, y, c: (z + step, y, c)


def sibling(z, y, c):
    return (z, y, 1 - c)


def total(*terms):
    return sum(t.astype(jnp.float32) for t in terms)


def rounded_total(*terms):
    return total(*terms).astype(jnp.bfloat16)


def local(queries, key_rows, value_rows, image_ids, send_slot, out_weight, grad_out):
    row_count, width = queries.shape
    ranks = lax.axis_size("dp")
    core = lax.axis_index("dp") % NC

    stay, leave, g_near = contexts(image_ids, send_slot, queries, key_rows, value_rows, grad_out)
    came = lax.ppermute(leave, "dp", [(i, (i + 1) % ranks) for i in range(ranks)])
    grad_ctx = grad_context(g_near, out_weight)
    stay, grad_ctx = lax.optimization_barrier((stay, grad_ctx))

    given = partial_grad(True, stay, came, g_near)
    given, tail = lax.optimization_barrier((given, grad_ctx[row_count:]))
    got = send(given, sibling)
    own = partial_grad(False, stay, came, g_near)
    back = lax.ppermute(tail, "dp", [((i + 1) % ranks, i) for i in range(ranks)])
    got, back = lax.optimization_barrier((got, back))

    def blocks(first, last):
        rows = slice(ORDER.index(first) * NZ * width, (ORDER.index(last) + 1) * NZ * width)
        return own[rows], got[rows]

    size = NZ * width
    far = send(rounded_total(*blocks(4, 4)), apart_y(2))
    up = send(rounded_total(*blocks(3, 1)), along_y(1))
    down = send(rounded_total(*blocks(5, 7)), along_y(-1))
    grads = backward(image_ids, send_slot, queries, key_rows, value_rows, grad_ctx, back)
    none = jnp.zeros_like(far)
    up2 = rounded_total(*blocks(2, 2), up[:size], jnp.where(core == 0, far, none))
    down2 = rounded_total(*blocks(6, 6), down[:size], jnp.where(core == 1, far, none))
    up2, down2, *grads = lax.optimization_barrier((up2, down2, *grads))
    up2, down2 = send(up2, along_y(2)), send(down2, along_y(-2))
    ring = total(*blocks(0, 0), up[size:], down[size:], up2, down2)
    above = send(ring[width : 2 * width].astype(jnp.bfloat16), along_z(1))
    below = send(ring[2 * width :].astype(jnp.bfloat16), along_z(-1))
    grad_weight = total(ring[:width], above, below)
    return (*grads, grad_weight)


def solution(mesh):
    placed = (
        P("dp", "fsdp"),
        P("dp", "fsdp"),
        P("dp", "fsdp"),
        P("dp"),
        P("dp"),
        P("fsdp", None),
        P("dp", None),
    )
    return jax.shard_map(
        local,
        mesh=mesh,
        in_specs=placed,
        out_specs=(P("dp", "fsdp"), P("dp", "fsdp"), P("dp", "fsdp"), P("fsdp", "dp")),
        check_vma=False,
    )
```

```python
import functools

import jax
import jax.numpy as jnp
from jax import lax
from jax.experimental import pallas as pl
from jax.experimental.pallas import tpu as pltpu
from jax.sharding import PartitionSpec as P

HD = 128
UNIT = 128
NZ, NY, NC = 3, 8, 2
SMEM = pl.BlockSpec(memory_space=pltpu.SMEM)
VMEM = pl.BlockSpec(memory_space=pltpu.VMEM)
PARAMS = pltpu.CompilerParams(vmem_limit_bytes=16 * 1024 * 1024)


def dot(a, b, dims):
    return lax.dot_general(a, b, (dims, ((), ())), preferred_element_type=jnp.float32)


def block_masks(ids_ref, units):
    lane_unit = lax.broadcasted_iota(jnp.int32, (1, units * UNIT), 1) // UNIT
    lane_ids = jnp.full((1, units * UNIT), ids_ref[0], jnp.int32)
    for u in range(1, units):
        lane_ids = jnp.where(lane_unit == u, ids_ref[u * UNIT], lane_ids)
    return [lane_ids == ids_ref[u * UNIT] for u in range(units)]


def softmax(scores):
    expo = jnp.exp(scores - jnp.max(scores, axis=-1, keepdims=True))
    return expo / jnp.sum(expo, axis=-1, keepdims=True)


def unit_weights(q, k, mask):
    return softmax(jnp.where(mask, dot(q, k, ((1,), (1,))) * HD**-0.5, -jnp.inf))


def context_kernel(ids_hbm, slot_hbm, q_hbm, k_hbm, v_hbm, g_hbm, stay_ref, leave_ref, g_ref,
                   ids_ref, slot_ref, q_ref, k_ref, v_ref, sems):
    pairs = [(ids_hbm, ids_ref), (slot_hbm, slot_ref), (q_hbm, q_ref), (k_hbm, k_ref), (v_hbm, v_ref),
             (g_hbm, g_ref)]
    copies = [pltpu.make_async_copy(src, dst, sems.at[i]) for i, (src, dst) in enumerate(pairs)]
    for copy in copies:
        copy.start()
    for copy in copies[:5]:
        copy.wait()
    units = q_ref.shape[0] // UNIT
    masks = block_masks(ids_ref, units)
    for h in range(q_ref.shape[1] // HD):
        cols = pl.ds(h * HD, HD)
        v_t = v_ref[:, cols].T
        leave = jnp.zeros((HD, UNIT), jnp.float32)
        for u in range(units):
            rows = pl.ds(u * UNIT, UNIT)
            w = unit_weights(q_ref[rows, cols], k_ref[:, cols], masks[u])
            ctx = dot(v_t, w.astype(jnp.bfloat16), ((1,), (1,)))
            stays = slot_ref[u * UNIT] < units * UNIT
            stay_ref[cols, rows] = jnp.where(stays, ctx, 0.0).astype(jnp.bfloat16)
            leave = jnp.where(stays, leave, ctx)
        leave_ref[cols, :] = leave.astype(jnp.bfloat16)
    copies[5].wait()


def in_hbm(x):
    return pltpu.with_memory_space_constraint(x, pltpu.HBM)


def whole(shape):
    return pl.BlockSpec(shape, lambda i: (0,) * len(shape))


def contexts(image_ids, send_slot, q, k, v, grad_out):
    rows, width = q.shape
    shapes = [(width, rows), (width, UNIT), grad_out.shape]
    return pl.pallas_call(
        context_kernel,
        in_specs=[pl.BlockSpec(memory_space=pltpu.HBM)] * 6,
        out_specs=[VMEM] * 3,
        out_shape=[jax.ShapeDtypeStruct(shape, jnp.bfloat16) for shape in shapes],
        scratch_shapes=[pltpu.SMEM(image_ids.shape, jnp.int32), pltpu.SMEM(send_slot.shape, jnp.int32)]
        + [pltpu.VMEM(q.shape, jnp.bfloat16)] * 3
        + [pltpu.SemaphoreType.DMA((6,))],
        compiler_params=PARAMS,
    )(*[in_hbm(x) for x in (image_ids, send_slot, q, k, v, grad_out)])


def partial_kernel(other, stay_ref, came_ref, g_ref, out_ref):
    me = lax.axis_index("dp")
    y, c = (me // NC) % NY, me % NC
    core = 1 - c if other else c
    ctx_t = jnp.concatenate([stay_ref[...], came_ref[...]], axis=1)
    width = ctx_t.shape[0]
    blocks = NY * NZ
    group = 4
    for n in range(0, blocks, group):
        dest = []
        for i in range(n, n + group):
            odd = (y + (i < blocks // 2)) % 2
            dest.append((i % (blocks // 2) * 2 + odd) * NC + core)
        g = jnp.concatenate([g_ref[:, pl.ds(pl.multiple_of(d * UNIT, UNIT), UNIT)] for d in dest], axis=1)
        part = dot(ctx_t, g, ((1,), (0,))).astype(jnp.bfloat16)
        for i in range(group):
            out_ref[pl.ds((n + i) * width, width), :] = part[:, i * UNIT : (i + 1) * UNIT]


def partial_grad(other, stay, came, grad_out):
    shape = (NY * NZ * stay.shape[0], UNIT)
    return pl.pallas_call(
        functools.partial(partial_kernel, other),
        in_specs=[VMEM, VMEM, VMEM],
        out_specs=VMEM,
        out_shape=jax.ShapeDtypeStruct(shape, jnp.bfloat16),
        compiler_params=PARAMS,
    )(stay, came, grad_out)


def grad_context_kernel(g_ref, w_ref, out_ref):
    step = 1024
    acc = jnp.zeros(out_ref.shape, jnp.float32)
    for i in range(0, g_ref.shape[1], step):
        acc += dot(g_ref[:, i : i + step], w_ref[:, i : i + step], ((1,), (1,)))
    out_ref[...] = acc.astype(jnp.bfloat16)


def grad_context(grad_out, out_weight):
    shape = (grad_out.shape[0], out_weight.shape[0])
    return pl.pallas_call(
        grad_context_kernel,
        in_specs=[VMEM] * 2,
        out_specs=VMEM,
        out_shape=jax.ShapeDtypeStruct(shape, jnp.bfloat16),
        compiler_params=PARAMS,
    )(grad_out, out_weight)


def backward_kernel(ids_ref, slot_ref, q_ref, k_ref, v_ref, g_ref, back_ref, dq_ref, dk_ref, dv_ref):
    units = q_ref.shape[0] // UNIT
    masks = block_masks(ids_ref, units)
    for h in range(q_ref.shape[1] // HD):
        cols = pl.ds(h * HD, HD)
        k, v = k_ref[:, cols], v_ref[:, cols]
        dk = jnp.zeros(k.shape, jnp.float32)
        dv = jnp.zeros(v.shape, jnp.float32)
        for u in range(units):
            rows = pl.ds(u * UNIT, UNIT)
            q = q_ref[rows, cols]
            w = unit_weights(q, k, masks[u])
            stays = slot_ref[u * UNIT] < units * UNIT
            g = jnp.where(stays, g_ref[rows, cols].astype(jnp.float32), back_ref[:, cols].astype(jnp.float32))
            g = g.astype(jnp.bfloat16)
            dv += dot(w.astype(jnp.bfloat16), g, ((0,), (0,)))
            dw = dot(g, v, ((1,), (1,)))
            ds = (w * (dw - jnp.sum(w * dw, axis=-1, keepdims=True))).astype(jnp.bfloat16)
            dq_ref[rows, cols] = (dot(ds, k, ((1,), (0,))) * HD**-0.5).astype(jnp.bfloat16)
            dk += dot(ds, q, ((0,), (0,)))
        dk_ref[:, cols] = (dk * HD**-0.5).astype(jnp.bfloat16)
        dv_ref[:, cols] = dv.astype(jnp.bfloat16)


def backward(image_ids, send_slot, q, k, v, g, back):
    return pl.pallas_call(
        backward_kernel,
        grid=(1,),
        in_specs=[SMEM, SMEM] + [whole(q.shape)] * 3 + [whole(g.shape), whole(back.shape)],
        out_specs=[whole(q.shape)] * 3,
        out_shape=[jax.ShapeDtypeStruct(q.shape, jnp.bfloat16)] * 3,
    )(image_ids, send_slot, q, k, v, g, back)


PLACES = [(z, y, c) for z in range(NZ) for y in range(NY) for c in range(NC)]


def index(z, y, c):
    return (z % NZ * NY + y % NY) * NC + c


def send(block, to):
    return lax.ppermute(block, "dp", [(index(*p), index(*to(*p))) for p in PLACES])


def paired(z, y, c):
    return (z, y + 1 - (y + c) % 2 * 2, c)


def same_parity():
    return [[index(z, y, c) for z in range(NZ) for y in range(odd, NY, 2)] for odd in range(2) for c in range(NC)]


def sibling(z, y, c):
    return (z, y, 1 - c)


def total(*terms):
    return sum(t.astype(jnp.float32) for t in terms)


def rounded_total(*terms):
    return total(*terms).astype(jnp.bfloat16)


def local(queries, key_rows, value_rows, image_ids, send_slot, out_weight, grad_out):
    row_count, width = queries.shape
    ranks = lax.axis_size("dp")
    stay, leave, g_near = contexts(image_ids, send_slot, queries, key_rows, value_rows, grad_out)
    came = lax.ppermute(leave, "dp", [(i, (i + 1) % ranks) for i in range(ranks)])

    given = partial_grad(True, stay, came, g_near)
    got = send(given, sibling)
    own = partial_grad(False, stay, came, g_near)

    half = NY * NZ * width // 2
    met = send(rounded_total(own[:half], got[:half]), paired)
    grad_ctx = grad_context(g_near, out_weight)
    back = lax.ppermute(grad_ctx[row_count:], "dp", [((i + 1) % ranks, i) for i in range(ranks)])
    met, back = lax.optimization_barrier((met, back))
    sums = rounded_total(own[half:], got[half:], met).reshape(-1, width, UNIT)
    sums = lax.all_to_all(sums, "dp", 0, 0, axis_index_groups=same_parity())
    grads = backward(image_ids, send_slot, queries, key_rows, value_rows, grad_ctx, back)
    grad_weight = jnp.sum(sums.astype(jnp.float32), axis=0)
    return (*grads, grad_weight)


def solution(mesh):
    placed = (
        P("dp", "fsdp"),
        P("dp", "fsdp"),
        P("dp", "fsdp"),
        P("dp"),
        P("dp"),
        P("fsdp", None),
        P("dp", None),
    )
    return jax.shard_map(
        local,
        mesh=mesh,
        in_specs=placed,
        out_specs=(P("dp", "fsdp"), P("dp", "fsdp"), P("dp", "fsdp"), P("fsdp", "dp")),
        check_vma=False,
    )
```

```python
import functools

import jax
import jax.numpy as jnp
from jax import lax
from jax.experimental import pallas as pl
from jax.experimental.pallas import tpu as pltpu
from jax.sharding import PartitionSpec as P

HD = 128
UNIT = 128
NZ, NY, NC = 3, 8, 2
VMEM = pl.BlockSpec(memory_space=pltpu.VMEM)
PARAMS = pltpu.CompilerParams(vmem_limit_bytes=16 * 1024 * 1024)


def dot(a, b, dims):
    return lax.dot_general(a, b, (dims, ((), ())), preferred_element_type=jnp.float32)


def softmax(scores):
    expo = jnp.exp(scores - jnp.max(scores, axis=-1, keepdims=True))
    return expo / jnp.sum(expo, axis=-1, keepdims=True)


def unit_weights(q, k, mask):
    return softmax(jnp.where(mask, dot(q, k, ((1,), (1,))) * HD**-0.5, -jnp.inf))


def leaving_kernel(ids_hbm, slot_hbm, q_hbm, k_hbm, v_hbm, leave_ref, same_ref, stays_ref, q_ref, k_ref, v_ref,
                   ids_ref, slot_ref, sems):
    pairs = [(ids_hbm, ids_ref), (slot_hbm, slot_ref), (q_hbm, q_ref), (k_hbm, k_ref), (v_hbm, v_ref)]
    copies = [pltpu.make_async_copy(src, dst, sems.at[i]) for i, (src, dst) in enumerate(pairs)]
    for copy in copies:
        copy.start()
    for copy in copies:
        copy.wait()
    rows, width = q_ref.shape
    units = rows // UNIT
    stays = [slot_ref[u * UNIT] < rows for u in range(units)]
    first = jnp.int32(0)
    for u in range(1, units):
        first = jnp.where(stays[u], first, u * UNIT)
    moves = slot_ref[first] >= rows
    moved = pl.ds(pl.multiple_of(first, UNIT), UNIT)
    for h in range(width // HD):
        cols = pl.ds(h * HD, HD)
        w = softmax(dot(q_ref[moved, cols], k_ref[moved, cols], ((1,), (1,))) * HD**-0.5)
        ctx = dot(v_ref[moved, cols].T, w.astype(jnp.bfloat16), ((1,), (1,)))
        leave_ref[cols, :] = jnp.where(moves, ctx, 0.0).astype(jnp.bfloat16)
    lane_unit = lax.broadcasted_iota(jnp.int32, (1, rows), 1) // UNIT
    lane_ids = jnp.full((1, rows), ids_ref[0], jnp.int32)
    for u in range(1, units):
        lane_ids = jnp.where(lane_unit == u, ids_ref[u * UNIT], lane_ids)
    for u in range(units):
        same_ref[pl.ds(u, 1), :] = (lane_ids == ids_ref[u * UNIT]).astype(jnp.int32)
        stays_ref[pl.ds(u, 1), :] = jnp.full((1, UNIT), stays[u].astype(jnp.int32), jnp.int32)


def leaving_context(image_ids, send_slot, q, k, v):
    rows, width = q.shape
    shapes = [
        jax.ShapeDtypeStruct((width, UNIT), jnp.bfloat16),
        jax.ShapeDtypeStruct((8, rows), jnp.int32),
        jax.ShapeDtypeStruct((8, UNIT), jnp.int32),
    ] + [jax.ShapeDtypeStruct(q.shape, jnp.bfloat16)] * 3
    return pl.pallas_call(
        leaving_kernel,
        in_specs=[pl.BlockSpec(memory_space=pltpu.HBM)] * 5,
        out_specs=[VMEM] * 6,
        out_shape=shapes,
        scratch_shapes=[
            pltpu.SMEM(image_ids.shape, jnp.int32),
            pltpu.SMEM(send_slot.shape, jnp.int32),
            pltpu.SemaphoreType.DMA((5,)),
        ],
        compiler_params=PARAMS,
    )(*[in_hbm(x) for x in (image_ids, send_slot, q, k, v)])


def context_kernel(same_ref, stays_ref, q_ref, k_ref, v_ref, g_hbm, stay_ref, g_ref, sem):
    copy = pltpu.make_async_copy(g_hbm, g_ref, sem)
    copy.start()
    for h in range(q_ref.shape[1] // HD):
        cols = pl.ds(h * HD, HD)
        v_t = v_ref[:, cols].T
        for u in range(q_ref.shape[0] // UNIT):
            rows = pl.ds(u * UNIT, UNIT)
            w = unit_weights(q_ref[rows, cols], k_ref[:, cols], same_ref[u : u + 1, :] != 0)
            ctx = dot(v_t, w.astype(jnp.bfloat16), ((1,), (1,)))
            stay_ref[cols, rows] = jnp.where(stays_ref[u : u + 1, :] != 0, ctx, 0.0).astype(jnp.bfloat16)
    copy.wait()


def staying_context(same, stays, q, k, v, grad_out):
    shapes = [q.shape[::-1], grad_out.shape]
    return pl.pallas_call(
        context_kernel,
        in_specs=[VMEM] * 5 + [pl.BlockSpec(memory_space=pltpu.HBM)],
        out_specs=[VMEM] * 2,
        out_shape=[jax.ShapeDtypeStruct(shape, jnp.bfloat16) for shape in shapes],
        scratch_shapes=[pltpu.SemaphoreType.DMA],
        compiler_params=PARAMS,
    )(same, stays, q, k, v, in_hbm(grad_out))


def in_hbm(x):
    return pltpu.with_memory_space_constraint(x, pltpu.HBM)


def partial_kernel(crossing, other, stay_ref, came_ref, g_ref, out_ref):
    me = lax.axis_index("dp")
    y, c = (me // NC) % NY, me % NC
    core = 1 - c if other else c
    odd = (y + crossing) % 2
    ctx_t = jnp.concatenate([stay_ref[...], came_ref[...]], axis=1)
    width = ctx_t.shape[0]
    group = 4
    for n in range(0, NY * NZ // 2, group):
        dest = [(i * 2 + odd) * NC + core for i in range(n, n + group)]
        g = jnp.concatenate([g_ref[:, pl.ds(pl.multiple_of(d * UNIT, UNIT), UNIT)] for d in dest], axis=1)
        part = dot(ctx_t, g, ((1,), (0,))).astype(jnp.bfloat16)
        for i in range(group):
            out_ref[pl.ds((n + i) * width, width), :] = part[:, i * UNIT : (i + 1) * UNIT]


def partial_grad(crossing, other, stay, came, grad_out):
    shape = (NY * NZ // 2 * stay.shape[0], UNIT)
    return pl.pallas_call(
        functools.partial(partial_kernel, crossing, other),
        in_specs=[VMEM, VMEM, VMEM],
        out_specs=VMEM,
        out_shape=jax.ShapeDtypeStruct(shape, jnp.bfloat16),
        compiler_params=PARAMS,
    )(stay, came, grad_out)


def grad_context_kernel(g_ref, w_ref, out_ref):
    step = 1024
    acc = jnp.zeros(out_ref.shape, jnp.float32)
    for i in range(0, g_ref.shape[1], step):
        acc += dot(g_ref[:, i : i + step], w_ref[:, i : i + step], ((1,), (1,)))
    out_ref[...] = acc.astype(jnp.bfloat16)


def grad_context(grad_out, out_weight):
    shape = (grad_out.shape[0], out_weight.shape[0])
    return pl.pallas_call(
        grad_context_kernel,
        in_specs=[VMEM] * 2,
        out_specs=VMEM,
        out_shape=jax.ShapeDtypeStruct(shape, jnp.bfloat16),
        compiler_params=PARAMS,
    )(grad_out, out_weight)


def backward_kernel(same_ref, stays_ref, q_ref, k_ref, v_ref, g_ref, back_ref, dq_ref, dk_ref, dv_ref):
    for h in range(q_ref.shape[1] // HD):
        cols = pl.ds(h * HD, HD)
        k, v = k_ref[:, cols], v_ref[:, cols]
        dk = jnp.zeros(k.shape, jnp.float32)
        dv = jnp.zeros(v.shape, jnp.float32)
        for u in range(q_ref.shape[0] // UNIT):
            rows = pl.ds(u * UNIT, UNIT)
            q = q_ref[rows, cols]
            w = unit_weights(q, k, same_ref[u : u + 1, :] != 0)
            stays = stays_ref[u : u + 1, :] != 0
            g = jnp.where(stays, g_ref[rows, cols].astype(jnp.float32), back_ref[:, cols].astype(jnp.float32))
            g = g.astype(jnp.bfloat16)
            dv += dot(w.astype(jnp.bfloat16), g, ((0,), (0,)))
            dw = dot(g, v, ((1,), (1,)))
            ds = (w * (dw - jnp.sum(w * dw, axis=-1, keepdims=True))).astype(jnp.bfloat16)
            dq_ref[rows, cols] = (dot(ds, k, ((1,), (0,))) * HD**-0.5).astype(jnp.bfloat16)
            dk += dot(ds, q, ((0,), (0,)))
        dk_ref[:, cols] = (dk * HD**-0.5).astype(jnp.bfloat16)
        dv_ref[:, cols] = dv.astype(jnp.bfloat16)


def backward(same, stays, q, k, v, g, back):
    return pl.pallas_call(
        backward_kernel,
        in_specs=[VMEM] * 7,
        out_specs=[VMEM] * 3,
        out_shape=[jax.ShapeDtypeStruct(q.shape, jnp.bfloat16)] * 3,
        compiler_params=PARAMS,
    )(same, stays, q, k, v, g, back)


PLACES = [(z, y, c) for z in range(NZ) for y in range(NY) for c in range(NC)]


def index(z, y, c):
    return (z % NZ * NY + y % NY) * NC + c


def send(block, to):
    return lax.ppermute(block, "dp", [(index(*p), index(*to(*p))) for p in PLACES])


def paired(z, y, c):
    return (z, y + 1 - (y + c) % 2 * 2, c)


def same_parity():
    return [[index(z, y, c) for z in range(NZ) for y in range(odd, NY, 2)] for odd in range(2) for c in range(NC)]


def sibling(z, y, c):
    return (z, y, 1 - c)


def total(*terms):
    return sum(t.astype(jnp.float32) for t in terms)


def rounded_total(*terms):
    return total(*terms).astype(jnp.bfloat16)


def local(queries, key_rows, value_rows, image_ids, send_slot, out_weight, grad_out):
    row_count, width = queries.shape
    ranks = lax.axis_size("dp")
    leave, same, stays, q, k, v = leaving_context(image_ids, send_slot, queries, key_rows, value_rows)
    came = lax.ppermute(leave, "dp", [(i, (i + 1) % ranks) for i in range(ranks)])
    stay, g_near = staying_context(same, stays, q, k, v, grad_out)

    got = send(partial_grad(True, True, stay, came, g_near), sibling)
    own = partial_grad(True, False, stay, came, g_near)
    first, stay = lax.optimization_barrier((rounded_total(own, got), stay))
    met = send(first, paired)

    got = send(partial_grad(False, True, stay, came, g_near), sibling)
    own = partial_grad(False, False, stay, came, g_near)
    grad_ctx = grad_context(g_near, out_weight)
    sums = rounded_total(own, got, met).reshape(-1, width, UNIT)
    sums, grad_ctx = lax.optimization_barrier((sums, grad_ctx))
    sums = lax.all_to_all(sums, "dp", 0, 0, axis_index_groups=same_parity())

    back = lax.ppermute(grad_ctx[row_count:], "dp", [((i + 1) % ranks, i) for i in range(ranks)])
    grads = backward(same, stays, q, k, v, grad_ctx, back)
    grad_weight = jnp.sum(sums.astype(jnp.float32), axis=0)
    return (*grads, grad_weight)


def solution(mesh):
    placed = (
        P("dp", "fsdp"),
        P("dp", "fsdp"),
        P("dp", "fsdp"),
        P("dp"),
        P("dp"),
        P("fsdp", None),
        P("dp", None),
    )
    return jax.shard_map(
        local,
        mesh=mesh,
        in_specs=placed,
        out_specs=(P("dp", "fsdp"), P("dp", "fsdp"), P("dp", "fsdp"), P("fsdp", "dp")),
        check_vma=False,
    )
```

```python
import functools

import jax
import jax.numpy as jnp
from jax import lax
from jax.experimental import pallas as pl
from jax.experimental.pallas import tpu as pltpu
from jax.sharding import PartitionSpec as P

HD = 128
UNIT = 128
NZ, NY, NC = 3, 8, 2
VMEM = pl.BlockSpec(memory_space=pltpu.VMEM)
PARAMS = pltpu.CompilerParams(vmem_limit_bytes=16 * 1024 * 1024)


def dot(a, b, dims):
    return lax.dot_general(a, b, (dims, ((), ())), preferred_element_type=jnp.float32)


def softmax(scores):
    expo = jnp.exp(scores - jnp.max(scores, axis=-1, keepdims=True))
    return expo / jnp.sum(expo, axis=-1, keepdims=True)


def unit_weights(q, k, mask):
    return softmax(jnp.where(mask, dot(q, k, ((1,), (1,))) * HD**-0.5, -jnp.inf))


def leaving_kernel(ids_hbm, slot_hbm, q_hbm, k_hbm, v_hbm, leave_ref, same_ref, stays_ref, q_ref, k_ref, v_ref,
                   ids_ref, slot_ref, sems):
    pairs = [(ids_hbm, ids_ref), (slot_hbm, slot_ref), (q_hbm, q_ref), (k_hbm, k_ref), (v_hbm, v_ref)]
    copies = [pltpu.make_async_copy(src, dst, sems.at[i]) for i, (src, dst) in enumerate(pairs)]
    for copy in copies:
        copy.start()
    for copy in copies:
        copy.wait()
    rows, width = q_ref.shape
    units = rows // UNIT
    stays = [slot_ref[u * UNIT] < rows for u in range(units)]
    first = jnp.int32(0)
    for u in range(1, units):
        first = jnp.where(stays[u], first, u * UNIT)
    moves = slot_ref[first] >= rows
    moved = pl.ds(pl.multiple_of(first, UNIT), UNIT)
    for h in range(width // HD):
        cols = pl.ds(h * HD, HD)
        w = softmax(dot(q_ref[moved, cols], k_ref[moved, cols], ((1,), (1,))) * HD**-0.5)
        ctx = dot(v_ref[moved, cols].T, w.astype(jnp.bfloat16), ((1,), (1,)))
        leave_ref[cols, :] = jnp.where(moves, ctx, 0.0).astype(jnp.bfloat16)
    lane_unit = lax.broadcasted_iota(jnp.int32, (1, rows), 1) // UNIT
    lane_ids = jnp.full((1, rows), ids_ref[0], jnp.int32)
    for u in range(1, units):
        lane_ids = jnp.where(lane_unit == u, ids_ref[u * UNIT], lane_ids)
    for u in range(units):
        same_ref[pl.ds(u, 1), :] = (lane_ids == ids_ref[u * UNIT]).astype(jnp.int32)
        stays_ref[pl.ds(u, 1), :] = jnp.full((1, UNIT), stays[u].astype(jnp.int32), jnp.int32)


def leaving_context(image_ids, send_slot, q, k, v):
    rows, width = q.shape
    shapes = [
        jax.ShapeDtypeStruct((width, UNIT), jnp.bfloat16),
        jax.ShapeDtypeStruct((8, rows), jnp.int32),
        jax.ShapeDtypeStruct((8, UNIT), jnp.int32),
    ] + [jax.ShapeDtypeStruct(q.shape, jnp.bfloat16)] * 3
    return pl.pallas_call(
        leaving_kernel,
        in_specs=[pl.BlockSpec(memory_space=pltpu.HBM)] * 5,
        out_specs=[VMEM] * 6,
        out_shape=shapes,
        scratch_shapes=[
            pltpu.SMEM(image_ids.shape, jnp.int32),
            pltpu.SMEM(send_slot.shape, jnp.int32),
            pltpu.SemaphoreType.DMA((5,)),
        ],
        compiler_params=PARAMS,
    )(*[in_hbm(x) for x in (image_ids, send_slot, q, k, v)])


def context_kernel(same_ref, stays_ref, q_ref, k_ref, v_ref, g_hbm, stay_ref, g_ref, sem):
    copy = pltpu.make_async_copy(g_hbm, g_ref, sem)
    copy.start()
    for h in range(q_ref.shape[1] // HD):
        cols = pl.ds(h * HD, HD)
        v_t = v_ref[:, cols].T
        for u in range(q_ref.shape[0] // UNIT):
            rows = pl.ds(u * UNIT, UNIT)
            w = unit_weights(q_ref[rows, cols], k_ref[:, cols], same_ref[u : u + 1, :] != 0)
            ctx = dot(v_t, w.astype(jnp.bfloat16), ((1,), (1,)))
            stay_ref[cols, rows] = jnp.where(stays_ref[u : u + 1, :] != 0, ctx, 0.0).astype(jnp.bfloat16)
    copy.wait()


def staying_context(same, stays, q, k, v, grad_out):
    shapes = [q.shape[::-1], grad_out.shape]
    return pl.pallas_call(
        context_kernel,
        in_specs=[VMEM] * 5 + [pl.BlockSpec(memory_space=pltpu.HBM)],
        out_specs=[VMEM] * 2,
        out_shape=[jax.ShapeDtypeStruct(shape, jnp.bfloat16) for shape in shapes],
        scratch_shapes=[pltpu.SemaphoreType.DMA],
        compiler_params=PARAMS,
    )(same, stays, q, k, v, in_hbm(grad_out))


def in_hbm(x):
    return pltpu.with_memory_space_constraint(x, pltpu.HBM)


def partial_kernel(crossing, other, stay_ref, came_ref, g_ref, out_ref):
    me = lax.axis_index("dp")
    z, y, c = me // (NY * NC), (me // NC) % NY, me % NC
    core = 1 - c if other else c
    odd = (y + crossing) % 2
    places = [((z + i) % NZ, j * 2 + odd) for j in range(NY // 2) for i in range(1, NZ)]
    places += [(z, j * 2 + odd) for j in range(NY // 2)]
    ctx_t = jnp.concatenate([stay_ref[...], came_ref[...]], axis=1)
    width = ctx_t.shape[0]
    group = 4
    for n in range(0, len(places), group):
        dest = [(z_to * NY + y_to) * NC + core for z_to, y_to in places[n : n + group]]
        g = jnp.concatenate([g_ref[:, pl.ds(pl.multiple_of(d * UNIT, UNIT), UNIT)] for d in dest], axis=1)
        part = dot(ctx_t, g, ((1,), (0,))).astype(jnp.bfloat16)
        for i in range(group):
            out_ref[pl.ds((n + i) * width, width), :] = part[:, i * UNIT : (i + 1) * UNIT]


def partial_grad(crossing, other, stay, came, grad_out):
    shape = (NY * NZ // 2 * stay.shape[0], UNIT)
    return pl.pallas_call(
        functools.partial(partial_kernel, crossing, other),
        in_specs=[VMEM, VMEM, VMEM],
        out_specs=VMEM,
        out_shape=jax.ShapeDtypeStruct(shape, jnp.bfloat16),
        compiler_params=PARAMS,
    )(stay, came, grad_out)


def grad_context_kernel(g_ref, w_ref, out_ref):
    step = 1024
    acc = jnp.zeros(out_ref.shape, jnp.float32)
    for i in range(0, g_ref.shape[1], step):
        acc += dot(g_ref[:, i : i + step], w_ref[:, i : i + step], ((1,), (1,)))
    out_ref[...] = acc.astype(jnp.bfloat16)


def grad_context(grad_out, out_weight):
    shape = (grad_out.shape[0], out_weight.shape[0])
    return pl.pallas_call(
        grad_context_kernel,
        in_specs=[VMEM] * 2,
        out_specs=VMEM,
        out_shape=jax.ShapeDtypeStruct(shape, jnp.bfloat16),
        compiler_params=PARAMS,
    )(grad_out, out_weight)


def backward_kernel(same_ref, stays_ref, q_ref, k_ref, v_ref, g_ref, back_ref, dq_ref, dk_ref, dv_ref):
    for h in range(q_ref.shape[1] // HD):
        cols = pl.ds(h * HD, HD)
        k, v = k_ref[:, cols], v_ref[:, cols]
        dk = jnp.zeros(k.shape, jnp.float32)
        dv = jnp.zeros(v.shape, jnp.float32)
        for u in range(q_ref.shape[0] // UNIT):
            rows = pl.ds(u * UNIT, UNIT)
            q = q_ref[rows, cols]
            w = unit_weights(q, k, same_ref[u : u + 1, :] != 0)
            stays = stays_ref[u : u + 1, :] != 0
            g = jnp.where(stays, g_ref[rows, cols].astype(jnp.float32), back_ref[:, cols].astype(jnp.float32))
            g = g.astype(jnp.bfloat16)
            dv += dot(w.astype(jnp.bfloat16), g, ((0,), (0,)))
            dw = dot(g, v, ((1,), (1,)))
            ds = (w * (dw - jnp.sum(w * dw, axis=-1, keepdims=True))).astype(jnp.bfloat16)
            dq_ref[rows, cols] = (dot(ds, k, ((1,), (0,))) * HD**-0.5).astype(jnp.bfloat16)
            dk += dot(ds, q, ((0,), (0,)))
        dk_ref[:, cols] = (dk * HD**-0.5).astype(jnp.bfloat16)
        dv_ref[:, cols] = dv.astype(jnp.bfloat16)


def backward(same, stays, q, k, v, g, back):
    return pl.pallas_call(
        backward_kernel,
        in_specs=[VMEM] * 7,
        out_specs=[VMEM] * 3,
        out_shape=[jax.ShapeDtypeStruct(q.shape, jnp.bfloat16)] * 3,
        compiler_params=PARAMS,
    )(same, stays, q, k, v, g, back)


PLACES = [(z, y, c) for z in range(NZ) for y in range(NY) for c in range(NC)]


def index(z, y, c):
    return (z % NZ * NY + y % NY) * NC + c


def send(block, to):
    return lax.ppermute(block, "dp", [(index(*p), index(*to(*p))) for p in PLACES])


def paired(z, y, c):
    return (z, y + 1 - (y + c) % 2 * 2, c)


def same_parity():
    return [[index(z, y, c) for y in range(odd, NY, 2)] for z in range(NZ) for odd in range(2) for c in range(NC)]


def along_z(step):
    return lambda z, y, c: (z + step, y, c)


def sibling(z, y, c):
    return (z, y, 1 - c)


def total(*terms):
    return sum(t.astype(jnp.float32) for t in terms)


def rounded_total(*terms):
    return total(*terms).astype(jnp.bfloat16)


def local(queries, key_rows, value_rows, image_ids, send_slot, out_weight, grad_out):
    row_count, width = queries.shape
    ranks = lax.axis_size("dp")
    leave, same, stays, q, k, v = leaving_context(image_ids, send_slot, queries, key_rows, value_rows)
    came = lax.ppermute(leave, "dp", [(i, (i + 1) % ranks) for i in range(ranks)])
    stay, g_near = staying_context(same, stays, q, k, v, grad_out)
    grad_ctx = grad_context(g_near, out_weight)
    stay, tail = lax.optimization_barrier((stay, grad_ctx[row_count:]))
    back = lax.ppermute(tail, "dp", [((i + 1) % ranks, i) for i in range(ranks)])

    got = send(partial_grad(True, True, stay, came, g_near), sibling)
    own = partial_grad(True, False, stay, came, g_near)
    got, back = lax.optimization_barrier((got, back))
    first, stay = lax.optimization_barrier((rounded_total(own, got), stay))
    met = send(first, paired)

    got = send(partial_grad(False, True, stay, came, g_near), sibling)
    own = partial_grad(False, False, stay, came, g_near)
    far = (NZ - 1) * (NY // 2) * width
    away = rounded_total(own[:far], got[:far], met[:far]).reshape(NY // 2, -1, UNIT)
    here = rounded_total(own[far:], got[far:], met[far:]).reshape(NY // 2, -1, UNIT)
    away, here = lax.optimization_barrier((away, here))
    away = lax.all_to_all(away, "dp", 0, 0, axis_index_groups=same_parity())
    away, here = lax.optimization_barrier((rounded_total(*away), here))
    here = lax.all_to_all(here, "dp", 0, 0, axis_index_groups=same_parity())
    above, below = send(away[:width], along_z(1)), send(away[width:], along_z(-1))
    grads = backward(same, stays, q, k, v, grad_ctx, back)
    grad_weight = total(*here, above, below)
    return (*grads, grad_weight)


def solution(mesh):
    placed = (
        P("dp", "fsdp"),
        P("dp", "fsdp"),
        P("dp", "fsdp"),
        P("dp"),
        P("dp"),
        P("fsdp", None),
        P("dp", None),
    )
    return jax.shard_map(
        local,
        mesh=mesh,
        in_specs=placed,
        out_specs=(P("dp", "fsdp"), P("dp", "fsdp"), P("dp", "fsdp"), P("fsdp", "dp")),
        check_vma=False,
    )
```

```python
import functools

import jax
import jax.numpy as jnp
from jax import lax
from jax.experimental import pallas as pl
from jax.experimental.pallas import tpu as pltpu
from jax.sharding import PartitionSpec as P

HD = 128
UNIT = 128
NZ, NY, NC = 3, 8, 2
VMEM = pl.BlockSpec(memory_space=pltpu.VMEM)
PARAMS = pltpu.CompilerParams(vmem_limit_bytes=16 * 1024 * 1024)


def dot(a, b, dims):
    return lax.dot_general(a, b, (dims, ((), ())), preferred_element_type=jnp.float32)


def softmax(scores):
    expo = jnp.exp(scores - jnp.max(scores, axis=-1, keepdims=True))
    return expo / jnp.sum(expo, axis=-1, keepdims=True)


def unit_weights(q, k, mask):
    return softmax(jnp.where(mask, dot(q, k, ((1,), (1,))) * HD**-0.5, -jnp.inf))


def leaving_kernel(ids_hbm, slot_hbm, q_hbm, k_hbm, v_hbm, leave_ref, same_ref, stays_ref, q_ref, k_ref, v_ref,
                   ids_ref, slot_ref, sems):
    pairs = [(ids_hbm, ids_ref), (slot_hbm, slot_ref), (q_hbm, q_ref), (k_hbm, k_ref), (v_hbm, v_ref)]
    copies = [pltpu.make_async_copy(src, dst, sems.at[i]) for i, (src, dst) in enumerate(pairs)]
    for copy in copies:
        copy.start()
    for copy in copies:
        copy.wait()
    rows, width = q_ref.shape
    units = rows // UNIT
    stays = [slot_ref[u * UNIT] < rows for u in range(units)]
    first = jnp.int32(0)
    for u in range(1, units):
        first = jnp.where(stays[u], first, u * UNIT)
    moves = slot_ref[first] >= rows
    moved = pl.ds(pl.multiple_of(first, UNIT), UNIT)
    for h in range(width // HD):
        cols = pl.ds(h * HD, HD)
        w = softmax(dot(q_ref[moved, cols], k_ref[moved, cols], ((1,), (1,))) * HD**-0.5)
        ctx = dot(v_ref[moved, cols].T, w.astype(jnp.bfloat16), ((1,), (1,)))
        leave_ref[cols, :] = jnp.where(moves, ctx, 0.0).astype(jnp.bfloat16)
    lane_unit = lax.broadcasted_iota(jnp.int32, (1, rows), 1) // UNIT
    lane_ids = jnp.full((1, rows), ids_ref[0], jnp.int32)
    for u in range(1, units):
        lane_ids = jnp.where(lane_unit == u, ids_ref[u * UNIT], lane_ids)
    for u in range(units):
        same_ref[pl.ds(u, 1), :] = (lane_ids == ids_ref[u * UNIT]).astype(jnp.int32)
        stays_ref[pl.ds(u, 1), :] = jnp.full((1, UNIT), stays[u].astype(jnp.int32), jnp.int32)


def leaving_context(image_ids, send_slot, q, k, v):
    rows, width = q.shape
    shapes = [
        jax.ShapeDtypeStruct((width, UNIT), jnp.bfloat16),
        jax.ShapeDtypeStruct((8, rows), jnp.int32),
        jax.ShapeDtypeStruct((8, UNIT), jnp.int32),
    ] + [jax.ShapeDtypeStruct(q.shape, jnp.bfloat16)] * 3
    return pl.pallas_call(
        leaving_kernel,
        in_specs=[pl.BlockSpec(memory_space=pltpu.HBM)] * 5,
        out_specs=[VMEM] * 6,
        out_shape=shapes,
        scratch_shapes=[
            pltpu.SMEM(image_ids.shape, jnp.int32),
            pltpu.SMEM(send_slot.shape, jnp.int32),
            pltpu.SemaphoreType.DMA((5,)),
        ],
        compiler_params=PARAMS,
    )(*[in_hbm(x) for x in (image_ids, send_slot, q, k, v)])


def context_kernel(same_ref, stays_ref, q_ref, k_ref, v_ref, g_hbm, stay_ref, g_ref, sem):
    copy = pltpu.make_async_copy(g_hbm, g_ref, sem)
    copy.start()
    for h in range(q_ref.shape[1] // HD):
        cols = pl.ds(h * HD, HD)
        v_t = v_ref[:, cols].T
        for u in range(q_ref.shape[0] // UNIT):
            rows = pl.ds(u * UNIT, UNIT)
            w = unit_weights(q_ref[rows, cols], k_ref[:, cols], same_ref[u : u + 1, :] != 0)
            ctx = dot(v_t, w.astype(jnp.bfloat16), ((1,), (1,)))
            stay_ref[cols, rows] = jnp.where(stays_ref[u : u + 1, :] != 0, ctx, 0.0).astype(jnp.bfloat16)
    copy.wait()


def staying_context(same, stays, q, k, v, grad_out):
    shapes = [q.shape[::-1], grad_out.shape]
    return pl.pallas_call(
        context_kernel,
        in_specs=[VMEM] * 5 + [pl.BlockSpec(memory_space=pltpu.HBM)],
        out_specs=[VMEM] * 2,
        out_shape=[jax.ShapeDtypeStruct(shape, jnp.bfloat16) for shape in shapes],
        scratch_shapes=[pltpu.SemaphoreType.DMA],
        compiler_params=PARAMS,
    )(same, stays, q, k, v, in_hbm(grad_out))


def in_hbm(x):
    return pltpu.with_memory_space_constraint(x, pltpu.HBM)


def partial_kernel(crossing, other, stay_ref, came_ref, g_ref, out_ref):
    me = lax.axis_index("dp")
    y, c = (me // NC) % NY, me % NC
    core = 1 - c if other else c
    odd = (y + crossing) % 2
    places = [(i, j * 2 + odd) for j in range(NY // 2) for i in range(NZ)]
    ctx_t = jnp.concatenate([stay_ref[...], came_ref[...]], axis=1)
    width = ctx_t.shape[0]
    group = 4
    for n in range(0, len(places), group):
        dest = [(z_to * NY + y_to) * NC + core for z_to, y_to in places[n : n + group]]
        g = jnp.concatenate([g_ref[:, pl.ds(pl.multiple_of(d * UNIT, UNIT), UNIT)] for d in dest], axis=1)
        part = dot(ctx_t, g, ((1,), (0,))).astype(jnp.bfloat16)
        for i in range(group):
            out_ref[pl.ds((n + i) * width, width), :] = part[:, i * UNIT : (i + 1) * UNIT]


def partial_grad(crossing, other, stay, came, grad_out):
    shape = (NY * NZ // 2 * stay.shape[0], UNIT)
    return pl.pallas_call(
        functools.partial(partial_kernel, crossing, other),
        in_specs=[VMEM, VMEM, VMEM],
        out_specs=VMEM,
        out_shape=jax.ShapeDtypeStruct(shape, jnp.bfloat16),
        compiler_params=PARAMS,
    )(stay, came, grad_out)


def grad_context_kernel(g_ref, w_ref, out_ref):
    step = 1024
    acc = jnp.zeros(out_ref.shape, jnp.float32)
    for i in range(0, g_ref.shape[1], step):
        acc += dot(g_ref[:, i : i + step], w_ref[:, i : i + step], ((1,), (1,)))
    out_ref[...] = acc.astype(jnp.bfloat16)


def grad_context(grad_out, out_weight):
    shape = (grad_out.shape[0], out_weight.shape[0])
    return pl.pallas_call(
        grad_context_kernel,
        in_specs=[VMEM] * 2,
        out_specs=VMEM,
        out_shape=jax.ShapeDtypeStruct(shape, jnp.bfloat16),
        compiler_params=PARAMS,
    )(grad_out, out_weight)


def backward_kernel(same_ref, stays_ref, q_ref, k_ref, v_ref, g_ref, back_ref, dq_ref, dk_ref, dv_ref):
    for h in range(q_ref.shape[1] // HD):
        cols = pl.ds(h * HD, HD)
        k, v = k_ref[:, cols], v_ref[:, cols]
        dk = jnp.zeros(k.shape, jnp.float32)
        dv = jnp.zeros(v.shape, jnp.float32)
        for u in range(q_ref.shape[0] // UNIT):
            rows = pl.ds(u * UNIT, UNIT)
            q = q_ref[rows, cols]
            w = unit_weights(q, k, same_ref[u : u + 1, :] != 0)
            stays = stays_ref[u : u + 1, :] != 0
            g = jnp.where(stays, g_ref[rows, cols].astype(jnp.float32), back_ref[:, cols].astype(jnp.float32))
            g = g.astype(jnp.bfloat16)
            dv += dot(w.astype(jnp.bfloat16), g, ((0,), (0,)))
            dw = dot(g, v, ((1,), (1,)))
            ds = (w * (dw - jnp.sum(w * dw, axis=-1, keepdims=True))).astype(jnp.bfloat16)
            dq_ref[rows, cols] = (dot(ds, k, ((1,), (0,))) * HD**-0.5).astype(jnp.bfloat16)
            dk += dot(ds, q, ((0,), (0,)))
        dk_ref[:, cols] = (dk * HD**-0.5).astype(jnp.bfloat16)
        dv_ref[:, cols] = dv.astype(jnp.bfloat16)


def backward(same, stays, q, k, v, g, back):
    return pl.pallas_call(
        backward_kernel,
        in_specs=[VMEM] * 7,
        out_specs=[VMEM] * 3,
        out_shape=[jax.ShapeDtypeStruct(q.shape, jnp.bfloat16)] * 3,
        compiler_params=PARAMS,
    )(same, stays, q, k, v, g, back)


PLACES = [(z, y, c) for z in range(NZ) for y in range(NY) for c in range(NC)]


def index(z, y, c):
    return (z % NZ * NY + y % NY) * NC + c


def send(block, to):
    return lax.ppermute(block, "dp", [(index(*p), index(*to(*p))) for p in PLACES])


def paired(z, y, c):
    return (z, y + 1 - (y + c) % 2 * 2, c)


def same_parity():
    return [[index(z, y, c) for y in range(odd, NY, 2)] for z in range(NZ) for odd in range(2) for c in range(NC)]


def same_place():
    return [[index(z, y, c) for z in range(NZ)] for y in range(NY) for c in range(NC)]


def sibling(z, y, c):
    return (z, y, 1 - c)


def total(*terms):
    return sum(t.astype(jnp.float32) for t in terms)


def rounded_total(*terms):
    return total(*terms).astype(jnp.bfloat16)


def local(queries, key_rows, value_rows, image_ids, send_slot, out_weight, grad_out):
    row_count, width = queries.shape
    ranks = lax.axis_size("dp")
    leave, same, stays, q, k, v = leaving_context(image_ids, send_slot, queries, key_rows, value_rows)
    came = lax.ppermute(leave, "dp", [(i, (i + 1) % ranks) for i in range(ranks)])
    stay, g_near = staying_context(same, stays, q, k, v, grad_out)
    grad_ctx = grad_context(g_near, out_weight)

    got = send(partial_grad(True, True, stay, came, g_near), sibling)
    own = partial_grad(True, False, stay, came, g_near)
    first, stay = lax.optimization_barrier((rounded_total(own, got), stay))
    met = send(first, paired)

    got = send(partial_grad(False, True, stay, came, g_near), sibling)
    own = partial_grad(False, False, stay, came, g_near)
    sums = rounded_total(own, got, met).reshape(NY // 2, -1, UNIT)
    sums, tail = lax.optimization_barrier((sums, grad_ctx[row_count:]))
    sums = lax.all_to_all(sums, "dp", 0, 0, axis_index_groups=same_parity())
    back = lax.ppermute(tail, "dp", [((i + 1) % ranks, i) for i in range(ranks)])
    sums, back = lax.optimization_barrier((sums, back))
    grads = backward(same, stays, q, k, v, grad_ctx, back)
    sums = rounded_total(*sums).reshape(NZ, -1, UNIT)
    sums = lax.all_to_all(sums, "dp", 0, 0, axis_index_groups=same_place())
    grad_weight = total(*sums)
    return (*grads, grad_weight)


def solution(mesh):
    placed = (
        P("dp", "fsdp"),
        P("dp", "fsdp"),
        P("dp", "fsdp"),
        P("dp"),
        P("dp"),
        P("fsdp", None),
        P("dp", None),
    )
    return jax.shard_map(
        local,
        mesh=mesh,
        in_specs=placed,
        out_specs=(P("dp", "fsdp"), P("dp", "fsdp"), P("dp", "fsdp"), P("fsdp", "dp")),
        check_vma=False,
    )
```

```python
import functools

import jax
import jax.numpy as jnp
from jax import lax
from jax.experimental import pallas as pl
from jax.experimental.pallas import tpu as pltpu
from jax.sharding import PartitionSpec as P

HD = 128
UNIT = 128
NZ, NY, NC = 3, 8, 2
ORDER = (4, 3, 5, 2, 6, 1, 7, 0)
VMEM = pl.BlockSpec(memory_space=pltpu.VMEM)
PARAMS = pltpu.CompilerParams(vmem_limit_bytes=8 * 1024 * 1024)


def dot(a, b, dims):
    return lax.dot_general(a, b, (dims, ((), ())), preferred_element_type=jnp.float32)


def softmax(scores):
    expo = jnp.exp(scores - jnp.max(scores, axis=-1, keepdims=True))
    return expo / jnp.sum(expo, axis=-1, keepdims=True)


def unit_weights(q, k, mask):
    return softmax(jnp.where(mask, dot(q, k, ((1,), (1,))) * HD**-0.5, -jnp.inf))


def leaving_kernel(ids_hbm, slot_hbm, q_hbm, k_hbm, v_hbm, leave_ref, same_ref, stays_ref, q_ref, k_ref, v_ref,
                   ids_ref, slot_ref, sems):
    pairs = [(ids_hbm, ids_ref), (slot_hbm, slot_ref), (q_hbm, q_ref), (k_hbm, k_ref), (v_hbm, v_ref)]
    copies = [pltpu.make_async_copy(src, dst, sems.at[i]) for i, (src, dst) in enumerate(pairs)]
    for copy in copies:
        copy.start()
    for copy in copies:
        copy.wait()
    rows, width = q_ref.shape
    units = rows // UNIT
    stays = [slot_ref[u * UNIT] < rows for u in range(units)]
    first = jnp.int32(0)
    for u in range(1, units):
        first = jnp.where(stays[u], first, u * UNIT)
    moves = slot_ref[first] >= rows
    moved = pl.ds(pl.multiple_of(first, UNIT), UNIT)
    for h in range(width // HD):
        cols = pl.ds(h * HD, HD)
        w = softmax(dot(q_ref[moved, cols], k_ref[moved, cols], ((1,), (1,))) * HD**-0.5)
        ctx = dot(v_ref[moved, cols].T, w.astype(jnp.bfloat16), ((1,), (1,)))
        leave_ref[cols, :] = jnp.where(moves, ctx, 0.0).astype(jnp.bfloat16)
    lane_unit = lax.broadcasted_iota(jnp.int32, (1, rows), 1) // UNIT
    lane_ids = jnp.full((1, rows), ids_ref[0], jnp.int32)
    for u in range(1, units):
        lane_ids = jnp.where(lane_unit == u, ids_ref[u * UNIT], lane_ids)
    for u in range(units):
        same_ref[pl.ds(u, 1), :] = (lane_ids == ids_ref[u * UNIT]).astype(jnp.int32)
        stays_ref[pl.ds(u, 1), :] = jnp.full((1, UNIT), stays[u].astype(jnp.int32), jnp.int32)


def leaving_context(image_ids, send_slot, q, k, v):
    rows, width = q.shape
    shapes = [
        jax.ShapeDtypeStruct((width, UNIT), jnp.bfloat16),
        jax.ShapeDtypeStruct((8, rows), jnp.int32),
        jax.ShapeDtypeStruct((8, UNIT), jnp.int32),
    ] + [jax.ShapeDtypeStruct(q.shape, jnp.bfloat16)] * 3
    return pl.pallas_call(
        leaving_kernel,
        in_specs=[pl.BlockSpec(memory_space=pltpu.HBM)] * 5,
        out_specs=[VMEM] * 6,
        out_shape=shapes,
        scratch_shapes=[
            pltpu.SMEM(image_ids.shape, jnp.int32),
            pltpu.SMEM(send_slot.shape, jnp.int32),
            pltpu.SemaphoreType.DMA((5,)),
        ],
        compiler_params=PARAMS,
    )(*[in_hbm(x) for x in (image_ids, send_slot, q, k, v)])


def context_kernel(same_ref, stays_ref, q_ref, k_ref, v_ref, g_hbm, stay_ref, g_ref, sem):
    copy = pltpu.make_async_copy(g_hbm, g_ref, sem)
    copy.start()
    for h in range(q_ref.shape[1] // HD):
        cols = pl.ds(h * HD, HD)
        v_t = v_ref[:, cols].T
        for u in range(q_ref.shape[0] // UNIT):
            rows = pl.ds(u * UNIT, UNIT)
            w = unit_weights(q_ref[rows, cols], k_ref[:, cols], same_ref[u : u + 1, :] != 0)
            ctx = dot(v_t, w.astype(jnp.bfloat16), ((1,), (1,)))
            stay_ref[cols, rows] = jnp.where(stays_ref[u : u + 1, :] != 0, ctx, 0.0).astype(jnp.bfloat16)
    copy.wait()


def staying_context(same, stays, q, k, v, grad_out):
    shapes = [q.shape[::-1], grad_out.shape]
    return pl.pallas_call(
        context_kernel,
        in_specs=[VMEM] * 5 + [pl.BlockSpec(memory_space=pltpu.HBM)],
        out_specs=[VMEM] * 2,
        out_shape=[jax.ShapeDtypeStruct(shape, jnp.bfloat16) for shape in shapes],
        scratch_shapes=[pltpu.SemaphoreType.DMA],
        compiler_params=PARAMS,
    )(same, stays, q, k, v, in_hbm(grad_out))


def in_hbm(x):
    return pltpu.with_memory_space_constraint(x, pltpu.HBM)


def partial_kernel(other, stay_ref, came_ref, g_ref, out_ref):
    me = lax.axis_index("dp")
    y, c = (me // NC) % NY, me % NC
    core = 1 - c if other else c
    ctx_t = jnp.concatenate([stay_ref[...], came_ref[...]], axis=1)
    width = ctx_t.shape[0]
    for n, distance in enumerate(ORDER):
        dest = [(i * NY + (y + distance) % NY) * NC + core for i in range(NZ)]
        g = jnp.concatenate([g_ref[:, pl.ds(pl.multiple_of(d * UNIT, UNIT), UNIT)] for d in dest], axis=1)
        part = dot(ctx_t, g, ((1,), (0,))).astype(jnp.bfloat16)
        for i in range(NZ):
            out_ref[pl.ds((n * NZ + i) * width, width), :] = part[:, i * UNIT : (i + 1) * UNIT]


def partial_grad(other, stay, came, grad_out):
    shape = (NY * NZ * stay.shape[0], UNIT)
    return pl.pallas_call(
        functools.partial(partial_kernel, other),
        in_specs=[VMEM, VMEM, VMEM],
        out_specs=VMEM,
        out_shape=jax.ShapeDtypeStruct(shape, jnp.bfloat16),
        compiler_params=PARAMS,
    )(stay, came, grad_out)


def grad_context_kernel(g_ref, w_ref, out_ref):
    step = 1024
    acc = jnp.zeros(out_ref.shape, jnp.float32)
    for i in range(0, g_ref.shape[1], step):
        acc += dot(g_ref[:, i : i + step], w_ref[:, i : i + step], ((1,), (1,)))
    out_ref[...] = acc.astype(jnp.bfloat16)


def grad_context(grad_out, out_weight):
    shape = (grad_out.shape[0], out_weight.shape[0])
    return pl.pallas_call(
        grad_context_kernel,
        in_specs=[VMEM] * 2,
        out_specs=VMEM,
        out_shape=jax.ShapeDtypeStruct(shape, jnp.bfloat16),
        compiler_params=PARAMS,
    )(grad_out, out_weight)


def backward_kernel(same_ref, stays_ref, q_ref, k_ref, v_ref, g_ref, back_ref, dq_ref, dk_ref, dv_ref):
    for h in range(q_ref.shape[1] // HD):
        cols = pl.ds(h * HD, HD)
        k, v = k_ref[:, cols], v_ref[:, cols]
        dk = jnp.zeros(k.shape, jnp.float32)
        dv = jnp.zeros(v.shape, jnp.float32)
        for u in range(q_ref.shape[0] // UNIT):
            rows = pl.ds(u * UNIT, UNIT)
            q = q_ref[rows, cols]
            w = unit_weights(q, k, same_ref[u : u + 1, :] != 0)
            stays = stays_ref[u : u + 1, :] != 0
            g = jnp.where(stays, g_ref[rows, cols].astype(jnp.float32), back_ref[:, cols].astype(jnp.float32))
            g = g.astype(jnp.bfloat16)
            dv += dot(w.astype(jnp.bfloat16), g, ((0,), (0,)))
            dw = dot(g, v, ((1,), (1,)))
            ds = (w * (dw - jnp.sum(w * dw, axis=-1, keepdims=True))).astype(jnp.bfloat16)
            dq_ref[rows, cols] = (dot(ds, k, ((1,), (0,))) * HD**-0.5).astype(jnp.bfloat16)
            dk += dot(ds, q, ((0,), (0,)))
        dk_ref[:, cols] = (dk * HD**-0.5).astype(jnp.bfloat16)
        dv_ref[:, cols] = dv.astype(jnp.bfloat16)


def backward(same, stays, q, k, v, g, back):
    return pl.pallas_call(
        backward_kernel,
        in_specs=[VMEM] * 7,
        out_specs=[VMEM] * 3,
        out_shape=[jax.ShapeDtypeStruct(q.shape, jnp.bfloat16)] * 3,
        compiler_params=PARAMS,
    )(same, stays, q, k, v, g, back)


PLACES = [(z, y, c) for z in range(NZ) for y in range(NY) for c in range(NC)]


def index(z, y, c):
    return (z % NZ * NY + y % NY) * NC + c


def send(block, to):
    return lax.ppermute(block, "dp", [(index(*p), index(*to(*p))) for p in PLACES])


def along_y(step):
    return lambda z, y, c: (z, y + step, c)


def apart_y(step):
    return lambda z, y, c: (z, y + step * (1 - 2 * c), c)


def same_place():
    return [[index(z, y, c) for z in range(NZ)] for y in range(NY) for c in range(NC)]


def sibling(z, y, c):
    return (z, y, 1 - c)


def total(*terms):
    return sum(t.astype(jnp.float32) for t in terms)


def rounded_total(*terms):
    return total(*terms).astype(jnp.bfloat16)


def local(queries, key_rows, value_rows, image_ids, send_slot, out_weight, grad_out):
    row_count, width = queries.shape
    ranks = lax.axis_size("dp")
    leave, same, stays, q, k, v = leaving_context(image_ids, send_slot, queries, key_rows, value_rows)
    came = lax.ppermute(leave, "dp", [(i, (i + 1) % ranks) for i in range(ranks)])
    stay, g_near = staying_context(same, stays, q, k, v, grad_out)
    grad_ctx = grad_context(g_near, out_weight)
    stay, grad_ctx = lax.optimization_barrier((stay, grad_ctx))

    size = NZ * width

    def cut(x):
        return [x[i : i + size] for i in range(0, x.shape[0], size)]

    got = send(partial_grad(True, stay, came, g_near), sibling)
    own = partial_grad(False, stay, came, g_near)
    parts = [rounded_total(*pair) for pair in zip(cut(own), cut(got), strict=True)]
    part = dict(zip(ORDER, lax.optimization_barrier(parts), strict=True))
    far, up, down = send(part[4], apart_y(2)), send(part[3], along_y(1)), send(part[5], along_y(-1))

    core = lax.axis_index("dp") % NC
    none = jnp.zeros_like(far)
    up = rounded_total(part[2], up, jnp.where(core == 0, far, none))
    down = rounded_total(part[6], down, jnp.where(core == 1, far, none))
    near = part[1], part[7]
    up, down, *near = lax.optimization_barrier((up, down, *near))
    up, down = send(up, along_y(2)), send(down, along_y(-2))
    near = send(near[0], along_y(1)), send(near[1], along_y(-1))
    sums = rounded_total(part[0], up, down, *near).reshape(NZ, -1, UNIT)
    sums, tail = lax.optimization_barrier((sums, grad_ctx[row_count:]))
    sums = lax.all_to_all(sums, "dp", 0, 0, axis_index_groups=same_place())
    back = lax.ppermute(tail, "dp", [((i + 1) % ranks, i) for i in range(ranks)])
    grads = backward(same, stays, queries, key_rows, value_rows, grad_ctx, back)
    grad_weight = total(*sums)
    return (*grads, grad_weight)


def solution(mesh):
    placed = (
        P("dp", "fsdp"),
        P("dp", "fsdp"),
        P("dp", "fsdp"),
        P("dp"),
        P("dp"),
        P("fsdp", None),
        P("dp", None),
    )
    return jax.shard_map(
        local,
        mesh=mesh,
        in_specs=placed,
        out_specs=(P("dp", "fsdp"), P("dp", "fsdp"), P("dp", "fsdp"), P("fsdp", "dp")),
        check_vma=False,
    )
```

```python
import functools

import jax
import jax.numpy as jnp
from jax import lax
from jax.experimental import pallas as pl
from jax.experimental.pallas import tpu as pltpu
from jax.sharding import PartitionSpec as P

HD = 128
UNIT = 128
NZ, NY, NC = 3, 8, 2
ORDER = (4, 3, 5, 2, 6, 1, 7, 0)
VMEM = pl.BlockSpec(memory_space=pltpu.VMEM)
PARAMS = pltpu.CompilerParams(vmem_limit_bytes=8 * 1024 * 1024)


def dot(a, b, dims):
    return lax.dot_general(a, b, (dims, ((), ())), preferred_element_type=jnp.float32)


def softmax(scores):
    expo = jnp.exp(scores - jnp.max(scores, axis=-1, keepdims=True))
    return expo / jnp.sum(expo, axis=-1, keepdims=True)


def unit_weights(q, k, mask):
    return softmax(jnp.where(mask, dot(q, k, ((1,), (1,))) * HD**-0.5, -jnp.inf))


def leaving_kernel(ids_hbm, slot_hbm, q_hbm, k_hbm, v_hbm, leave_ref, same_ref, stays_ref, q_ref, k_ref, v_ref,
                   ids_ref, slot_ref, sems):
    pairs = [(ids_hbm, ids_ref), (slot_hbm, slot_ref), (q_hbm, q_ref), (k_hbm, k_ref), (v_hbm, v_ref)]
    copies = [pltpu.make_async_copy(src, dst, sems.at[i]) for i, (src, dst) in enumerate(pairs)]
    for copy in copies:
        copy.start()
    for copy in copies:
        copy.wait()
    rows, width = q_ref.shape
    units = rows // UNIT
    stays = [slot_ref[u * UNIT] < rows for u in range(units)]
    first = jnp.int32(0)
    for u in range(1, units):
        first = jnp.where(stays[u], first, u * UNIT)
    moves = slot_ref[first] >= rows
    moved = pl.ds(pl.multiple_of(first, UNIT), UNIT)
    for h in range(width // HD):
        cols = pl.ds(h * HD, HD)
        w = softmax(dot(q_ref[moved, cols], k_ref[moved, cols], ((1,), (1,))) * HD**-0.5)
        ctx = dot(v_ref[moved, cols].T, w.astype(jnp.bfloat16), ((1,), (1,)))
        leave_ref[cols, :] = jnp.where(moves, ctx, 0.0).astype(jnp.bfloat16)
    lane_unit = lax.broadcasted_iota(jnp.int32, (1, rows), 1) // UNIT
    lane_ids = jnp.full((1, rows), ids_ref[0], jnp.int32)
    for u in range(1, units):
        lane_ids = jnp.where(lane_unit == u, ids_ref[u * UNIT], lane_ids)
    for u in range(units):
        same_ref[pl.ds(u, 1), :] = (lane_ids == ids_ref[u * UNIT]).astype(jnp.int32)
        stays_ref[pl.ds(u, 1), :] = jnp.full((1, UNIT), stays[u].astype(jnp.int32), jnp.int32)


def leaving_context(image_ids, send_slot, q, k, v):
    rows, width = q.shape
    shapes = [
        jax.ShapeDtypeStruct((width, UNIT), jnp.bfloat16),
        jax.ShapeDtypeStruct((8, rows), jnp.int32),
        jax.ShapeDtypeStruct((8, UNIT), jnp.int32),
    ] + [jax.ShapeDtypeStruct(q.shape, jnp.bfloat16)] * 3
    return pl.pallas_call(
        leaving_kernel,
        in_specs=[pl.BlockSpec(memory_space=pltpu.HBM)] * 5,
        out_specs=[VMEM] * 6,
        out_shape=shapes,
        scratch_shapes=[
            pltpu.SMEM(image_ids.shape, jnp.int32),
            pltpu.SMEM(send_slot.shape, jnp.int32),
            pltpu.SemaphoreType.DMA((5,)),
        ],
        compiler_params=PARAMS,
    )(*[in_hbm(x) for x in (image_ids, send_slot, q, k, v)])


def context_kernel(same_ref, stays_ref, q_ref, k_ref, v_ref, g_hbm, stay_ref, g_ref, sem):
    copy = pltpu.make_async_copy(g_hbm, g_ref, sem)
    copy.start()
    for h in range(q_ref.shape[1] // HD):
        cols = pl.ds(h * HD, HD)
        v_t = v_ref[:, cols].T
        for u in range(q_ref.shape[0] // UNIT):
            rows = pl.ds(u * UNIT, UNIT)
            w = unit_weights(q_ref[rows, cols], k_ref[:, cols], same_ref[u : u + 1, :] != 0)
            ctx = dot(v_t, w.astype(jnp.bfloat16), ((1,), (1,)))
            stay_ref[cols, rows] = jnp.where(stays_ref[u : u + 1, :] != 0, ctx, 0.0).astype(jnp.bfloat16)
    copy.wait()


def staying_context(same, stays, q, k, v, grad_out):
    shapes = [q.shape[::-1], grad_out.shape]
    return pl.pallas_call(
        context_kernel,
        in_specs=[VMEM] * 5 + [pl.BlockSpec(memory_space=pltpu.HBM)],
        out_specs=[VMEM] * 2,
        out_shape=[jax.ShapeDtypeStruct(shape, jnp.bfloat16) for shape in shapes],
        scratch_shapes=[pltpu.SemaphoreType.DMA],
        compiler_params=PARAMS,
    )(same, stays, q, k, v, in_hbm(grad_out))


def in_hbm(x):
    return pltpu.with_memory_space_constraint(x, pltpu.HBM)


def partial_kernel(other, stay_ref, came_ref, g_ref, out_ref):
    me = lax.axis_index("dp")
    y, c = (me // NC) % NY, me % NC
    core = 1 - c if other else c
    ctx_t = jnp.concatenate([stay_ref[...], came_ref[...]], axis=1)
    width = ctx_t.shape[0]
    for n, distance in enumerate(ORDER):
        dest = [(i * NY + (y + distance) % NY) * NC + core for i in range(NZ)]
        g = jnp.concatenate([g_ref[:, pl.ds(pl.multiple_of(d * UNIT, UNIT), UNIT)] for d in dest], axis=1)
        part = dot(ctx_t, g, ((1,), (0,))).astype(jnp.bfloat16)
        for i in range(NZ):
            out_ref[pl.ds((n * NZ + i) * width, width), :] = part[:, i * UNIT : (i + 1) * UNIT]


def partial_grad(other, stay, came, grad_out):
    shape = (NY * NZ * stay.shape[0], UNIT)
    return pl.pallas_call(
        functools.partial(partial_kernel, other),
        in_specs=[VMEM, VMEM, VMEM],
        out_specs=VMEM,
        out_shape=jax.ShapeDtypeStruct(shape, jnp.bfloat16),
        compiler_params=PARAMS,
    )(stay, came, grad_out)


def grad_context_kernel(g_ref, w_ref, out_ref):
    step = 1024
    acc = jnp.zeros(out_ref.shape, jnp.float32)
    for i in range(0, g_ref.shape[1], step):
        acc += dot(g_ref[:, i : i + step], w_ref[:, i : i + step], ((1,), (1,)))
    out_ref[...] = acc.astype(jnp.bfloat16)


def grad_context(grad_out, out_weight):
    shape = (grad_out.shape[0], out_weight.shape[0])
    return pl.pallas_call(
        grad_context_kernel,
        in_specs=[VMEM] * 2,
        out_specs=VMEM,
        out_shape=jax.ShapeDtypeStruct(shape, jnp.bfloat16),
        compiler_params=PARAMS,
    )(grad_out, out_weight)


def backward_kernel(same_ref, stays_ref, q_ref, k_ref, v_ref, g_ref, back_ref, dq_ref, dk_ref, dv_ref):
    for h in range(q_ref.shape[1] // HD):
        cols = pl.ds(h * HD, HD)
        k, v = k_ref[:, cols], v_ref[:, cols]
        dk = jnp.zeros(k.shape, jnp.float32)
        dv = jnp.zeros(v.shape, jnp.float32)
        for u in range(q_ref.shape[0] // UNIT):
            rows = pl.ds(u * UNIT, UNIT)
            q = q_ref[rows, cols]
            w = unit_weights(q, k, same_ref[u : u + 1, :] != 0)
            stays = stays_ref[u : u + 1, :] != 0
            g = jnp.where(stays, g_ref[rows, cols].astype(jnp.float32), back_ref[:, cols].astype(jnp.float32))
            g = g.astype(jnp.bfloat16)
            dv += dot(w.astype(jnp.bfloat16), g, ((0,), (0,)))
            dw = dot(g, v, ((1,), (1,)))
            ds = (w * (dw - jnp.sum(w * dw, axis=-1, keepdims=True))).astype(jnp.bfloat16)
            dq_ref[rows, cols] = (dot(ds, k, ((1,), (0,))) * HD**-0.5).astype(jnp.bfloat16)
            dk += dot(ds, q, ((0,), (0,)))
        dk_ref[:, cols] = (dk * HD**-0.5).astype(jnp.bfloat16)
        dv_ref[:, cols] = dv.astype(jnp.bfloat16)


def backward(same, stays, q, k, v, g, back):
    return pl.pallas_call(
        backward_kernel,
        in_specs=[VMEM] * 7,
        out_specs=[VMEM] * 3,
        out_shape=[jax.ShapeDtypeStruct(q.shape, jnp.bfloat16)] * 3,
        compiler_params=PARAMS,
    )(same, stays, q, k, v, g, back)


PLACES = [(z, y, c) for z in range(NZ) for y in range(NY) for c in range(NC)]


def index(z, y, c):
    return (z % NZ * NY + y % NY) * NC + c


def send(block, to):
    return lax.ppermute(block, "dp", [(index(*p), index(*to(*p))) for p in PLACES])


def along_y(step):
    return lambda z, y, c: (z, y + step, c)


def apart_y(step):
    return lambda z, y, c: (z, y + step * (1 - 2 * c), c)


def same_place():
    return [[index(z, y, c) for z in range(NZ)] for y in range(NY) for c in range(NC)]


def sibling(z, y, c):
    return (z, y, 1 - c)


def total(*terms):
    return sum(t.astype(jnp.float32) for t in terms)


def rounded_total(*terms):
    return total(*terms).astype(jnp.bfloat16)


def local(queries, key_rows, value_rows, image_ids, send_slot, out_weight, grad_out):
    row_count, width = queries.shape
    ranks = lax.axis_size("dp")
    leave, same, stays, q, k, v = leaving_context(image_ids, send_slot, queries, key_rows, value_rows)
    came = lax.ppermute(leave, "dp", [(i, (i + 1) % ranks) for i in range(ranks)])
    stay, g_near = staying_context(same, stays, q, k, v, grad_out)
    grad_ctx = grad_context(g_near, out_weight)
    stay, grad_ctx = lax.optimization_barrier((stay, grad_ctx))

    size = NZ * width

    def cut(x):
        return [x[i : i + size] for i in range(0, x.shape[0], size)]

    got = send(partial_grad(True, stay, came, g_near), sibling)
    own = partial_grad(False, stay, came, g_near)
    parts = [rounded_total(*pair) for pair in zip(cut(own), cut(got), strict=True)]
    part = dict(zip(ORDER, lax.optimization_barrier(parts), strict=True))
    far, up, down = send(part[4], apart_y(2)), send(part[3], along_y(1)), send(part[5], along_y(-1))
    near = send(part[1], along_y(1)), send(part[7], along_y(-1))

    core = lax.axis_index("dp") % NC
    none = jnp.zeros_like(far)
    up = rounded_total(part[2], up, jnp.where(core == 0, far, none))
    down = rounded_total(part[6], down, jnp.where(core == 1, far, none))
    up, down, tail = lax.optimization_barrier((up, down, grad_ctx[row_count:]))
    up, down = send(up, along_y(2)), send(down, along_y(-2))
    back = lax.ppermute(tail, "dp", [((i + 1) % ranks, i) for i in range(ranks)])
    sums = rounded_total(part[0], up, down, *near).reshape(NZ, -1, UNIT)
    sums, back = lax.optimization_barrier((sums, back))
    sums = lax.all_to_all(sums, "dp", 0, 0, axis_index_groups=same_place())
    grads = backward(same, stays, queries, key_rows, value_rows, grad_ctx, back)
    grad_weight = total(*sums)
    return (*grads, grad_weight)


def solution(mesh):
    placed = (
        P("dp", "fsdp"),
        P("dp", "fsdp"),
        P("dp", "fsdp"),
        P("dp"),
        P("dp"),
        P("fsdp", None),
        P("dp", None),
    )
    return jax.shard_map(
        local,
        mesh=mesh,
        in_specs=placed,
        out_specs=(P("dp", "fsdp"), P("dp", "fsdp"), P("dp", "fsdp"), P("fsdp", "dp")),
        check_vma=False,
    )
```

```python
import functools

import jax
import jax.numpy as jnp
from jax import lax
from jax.experimental import pallas as pl
from jax.experimental.pallas import tpu as pltpu
from jax.sharding import PartitionSpec as P

HD = 128
UNIT = 128
NZ, NY, NC = 3, 8, 2
ORDER = (4, 3, -3, 2, -2, 1, -1, 0)
VMEM = pl.BlockSpec(memory_space=pltpu.VMEM)
PARAMS = pltpu.CompilerParams(vmem_limit_bytes=8 * 1024 * 1024)


def dot(a, b, dims):
    return lax.dot_general(a, b, (dims, ((), ())), preferred_element_type=jnp.float32)


def softmax(scores):
    expo = jnp.exp(scores - jnp.max(scores, axis=-1, keepdims=True))
    return expo / jnp.sum(expo, axis=-1, keepdims=True)


def unit_weights(q, k, mask):
    return softmax(jnp.where(mask, dot(q, k, ((1,), (1,))) * HD**-0.5, -jnp.inf))


def leaving_kernel(ids_hbm, slot_hbm, q_hbm, k_hbm, v_hbm, leave_ref, same_ref, stays_ref, q_ref, k_ref, v_ref,
                   ids_ref, slot_ref, sems):
    pairs = [(ids_hbm, ids_ref), (slot_hbm, slot_ref), (q_hbm, q_ref), (k_hbm, k_ref), (v_hbm, v_ref)]
    copies = [pltpu.make_async_copy(src, dst, sems.at[i]) for i, (src, dst) in enumerate(pairs)]
    for copy in copies:
        copy.start()
    for copy in copies:
        copy.wait()
    rows, width = q_ref.shape
    units = rows // UNIT
    stays = [slot_ref[u * UNIT] < rows for u in range(units)]
    first = jnp.int32(0)
    for u in range(1, units):
        first = jnp.where(stays[u], first, u * UNIT)
    moves = slot_ref[first] >= rows
    moved = pl.ds(pl.multiple_of(first, UNIT), UNIT)
    for h in range(width // HD):
        cols = pl.ds(h * HD, HD)
        w = softmax(dot(q_ref[moved, cols], k_ref[moved, cols], ((1,), (1,))) * HD**-0.5)
        ctx = dot(v_ref[moved, cols].T, w.astype(jnp.bfloat16), ((1,), (1,)))
        leave_ref[cols, :] = jnp.where(moves, ctx, 0.0).astype(jnp.bfloat16)
    lane_unit = lax.broadcasted_iota(jnp.int32, (1, rows), 1) // UNIT
    lane_ids = jnp.full((1, rows), ids_ref[0], jnp.int32)
    for u in range(1, units):
        lane_ids = jnp.where(lane_unit == u, ids_ref[u * UNIT], lane_ids)
    for u in range(units):
        same_ref[pl.ds(u, 1), :] = (lane_ids == ids_ref[u * UNIT]).astype(jnp.int32)
        stays_ref[pl.ds(u, 1), :] = jnp.full((1, UNIT), stays[u].astype(jnp.int32), jnp.int32)


def leaving_context(image_ids, send_slot, q, k, v):
    rows, width = q.shape
    shapes = [
        jax.ShapeDtypeStruct((width, UNIT), jnp.bfloat16),
        jax.ShapeDtypeStruct((8, rows), jnp.int32),
        jax.ShapeDtypeStruct((8, UNIT), jnp.int32),
    ] + [jax.ShapeDtypeStruct(q.shape, jnp.bfloat16)] * 3
    return pl.pallas_call(
        leaving_kernel,
        in_specs=[pl.BlockSpec(memory_space=pltpu.HBM)] * 5,
        out_specs=[VMEM] * 6,
        out_shape=shapes,
        scratch_shapes=[
            pltpu.SMEM(image_ids.shape, jnp.int32),
            pltpu.SMEM(send_slot.shape, jnp.int32),
            pltpu.SemaphoreType.DMA((5,)),
        ],
        compiler_params=PARAMS,
    )(*[in_hbm(x) for x in (image_ids, send_slot, q, k, v)])


def context_kernel(same_ref, stays_ref, q_ref, k_ref, v_ref, g_hbm, stay_ref, g_ref, sem):
    copy = pltpu.make_async_copy(g_hbm, g_ref, sem)
    copy.start()
    for h in range(q_ref.shape[1] // HD):
        cols = pl.ds(h * HD, HD)
        v_t = v_ref[:, cols].T
        for u in range(q_ref.shape[0] // UNIT):
            rows = pl.ds(u * UNIT, UNIT)
            w = unit_weights(q_ref[rows, cols], k_ref[:, cols], same_ref[u : u + 1, :] != 0)
            ctx = dot(v_t, w.astype(jnp.bfloat16), ((1,), (1,)))
            stay_ref[cols, rows] = jnp.where(stays_ref[u : u + 1, :] != 0, ctx, 0.0).astype(jnp.bfloat16)
    copy.wait()


def staying_context(same, stays, q, k, v, grad_out):
    shapes = [q.shape[::-1], grad_out.shape]
    return pl.pallas_call(
        context_kernel,
        in_specs=[VMEM] * 5 + [pl.BlockSpec(memory_space=pltpu.HBM)],
        out_specs=[VMEM] * 2,
        out_shape=[jax.ShapeDtypeStruct(shape, jnp.bfloat16) for shape in shapes],
        scratch_shapes=[pltpu.SemaphoreType.DMA],
        compiler_params=PARAMS,
    )(same, stays, q, k, v, in_hbm(grad_out))


def in_hbm(x):
    return pltpu.with_memory_space_constraint(x, pltpu.HBM)


def partial_kernel(other, stay_ref, came_ref, g_ref, out_ref):
    me = lax.axis_index("dp")
    y, c = (me // NC) % NY, me % NC
    core = 1 - c if other else c
    ctx_t = jnp.concatenate([stay_ref[...], came_ref[...]], axis=1)
    width = ctx_t.shape[0]
    for n, distance in enumerate(ORDER):
        y_to = (y + NY + distance * (1 - 2 * core)) % NY
        dest = [(i * NY + y_to) * NC + core for i in range(NZ)]
        g = jnp.concatenate([g_ref[:, pl.ds(pl.multiple_of(d * UNIT, UNIT), UNIT)] for d in dest], axis=1)
        part = dot(ctx_t, g, ((1,), (0,))).astype(jnp.bfloat16)
        for i in range(NZ):
            out_ref[pl.ds((n * NZ + i) * width, width), :] = part[:, i * UNIT : (i + 1) * UNIT]


def partial_grad(other, stay, came, grad_out):
    shape = (NY * NZ * stay.shape[0], UNIT)
    return pl.pallas_call(
        functools.partial(partial_kernel, other),
        in_specs=[VMEM, VMEM, VMEM],
        out_specs=VMEM,
        out_shape=jax.ShapeDtypeStruct(shape, jnp.bfloat16),
        compiler_params=PARAMS,
    )(stay, came, grad_out)


def grad_context_kernel(g_ref, w_ref, out_ref):
    step = 1024
    acc = jnp.zeros(out_ref.shape, jnp.float32)
    for i in range(0, g_ref.shape[1], step):
        acc += dot(g_ref[:, i : i + step], w_ref[:, i : i + step], ((1,), (1,)))
    out_ref[...] = acc.astype(jnp.bfloat16)


def grad_context(grad_out, out_weight):
    shape = (grad_out.shape[0], out_weight.shape[0])
    return pl.pallas_call(
        grad_context_kernel,
        in_specs=[VMEM] * 2,
        out_specs=VMEM,
        out_shape=jax.ShapeDtypeStruct(shape, jnp.bfloat16),
        compiler_params=PARAMS,
    )(grad_out, out_weight)


def backward_kernel(same_ref, stays_ref, q_ref, k_ref, v_ref, g_ref, back_ref, dq_ref, dk_ref, dv_ref):
    for h in range(q_ref.shape[1] // HD):
        cols = pl.ds(h * HD, HD)
        k, v = k_ref[:, cols], v_ref[:, cols]
        dk = jnp.zeros(k.shape, jnp.float32)
        dv = jnp.zeros(v.shape, jnp.float32)
        for u in range(q_ref.shape[0] // UNIT):
            rows = pl.ds(u * UNIT, UNIT)
            q = q_ref[rows, cols]
            w = unit_weights(q, k, same_ref[u : u + 1, :] != 0)
            stays = stays_ref[u : u + 1, :] != 0
            g = jnp.where(stays, g_ref[rows, cols].astype(jnp.float32), back_ref[:, cols].astype(jnp.float32))
            g = g.astype(jnp.bfloat16)
            dv += dot(w.astype(jnp.bfloat16), g, ((0,), (0,)))
            dw = dot(g, v, ((1,), (1,)))
            ds = (w * (dw - jnp.sum(w * dw, axis=-1, keepdims=True))).astype(jnp.bfloat16)
            dq_ref[rows, cols] = (dot(ds, k, ((1,), (0,))) * HD**-0.5).astype(jnp.bfloat16)
            dk += dot(ds, q, ((0,), (0,)))
        dk_ref[:, cols] = (dk * HD**-0.5).astype(jnp.bfloat16)
        dv_ref[:, cols] = dv.astype(jnp.bfloat16)


def backward(same, stays, q, k, v, g, back):
    return pl.pallas_call(
        backward_kernel,
        in_specs=[VMEM] * 7,
        out_specs=[VMEM] * 3,
        out_shape=[jax.ShapeDtypeStruct(q.shape, jnp.bfloat16)] * 3,
        compiler_params=PARAMS,
    )(same, stays, q, k, v, g, back)


PLACES = [(z, y, c) for z in range(NZ) for y in range(NY) for c in range(NC)]


def index(z, y, c):
    return (z % NZ * NY + y % NY) * NC + c


def send(block, to):
    return lax.ppermute(block, "dp", [(index(*p), index(*to(*p))) for p in PLACES])


def along_y(step):
    return lambda z, y, c: (z, y + step * (1 - 2 * c), c)


def same_place():
    return [[index(z, y, c) for z in range(NZ)] for y in range(NY) for c in range(NC)]


def sibling(z, y, c):
    return (z, y, 1 - c)


def total(*terms):
    return sum(t.astype(jnp.float32) for t in terms)


def rounded_total(*terms):
    return total(*terms).astype(jnp.bfloat16)


def local(queries, key_rows, value_rows, image_ids, send_slot, out_weight, grad_out):
    row_count, width = queries.shape
    ranks = lax.axis_size("dp")
    leave, same, stays, q, k, v = leaving_context(image_ids, send_slot, queries, key_rows, value_rows)
    came = lax.ppermute(leave, "dp", [(i, (i + 1) % ranks) for i in range(ranks)])
    stay, g_near = staying_context(same, stays, q, k, v, grad_out)
    grad_ctx = grad_context(g_near, out_weight)
    stay, grad_ctx = lax.optimization_barrier((stay, grad_ctx))

    size = NZ * width

    def cut(x):
        return [x[i : i + size] for i in range(0, x.shape[0], size)]

    got = send(partial_grad(True, stay, came, g_near), sibling)
    own = partial_grad(False, stay, came, g_near)
    parts = [rounded_total(*pair) for pair in zip(cut(own), cut(got), strict=True)]
    part = dict(zip(ORDER, lax.optimization_barrier(parts), strict=True))
    far, up, down = send(part[4], along_y(2)), send(part[3], along_y(1)), send(part[-3], along_y(-1))
    near = send(part[1], along_y(1)), send(part[-1], along_y(-1))

    up, down = rounded_total(part[2], up, far), rounded_total(part[-2], down)
    up, down, tail = lax.optimization_barrier((up, down, grad_ctx[row_count:]))
    up, down = send(up, along_y(2)), send(down, along_y(-2))
    back = lax.ppermute(tail, "dp", [((i + 1) % ranks, i) for i in range(ranks)])
    sums = rounded_total(part[0], up, down, *near).reshape(NZ, -1, UNIT)
    sums, back = lax.optimization_barrier((sums, back))
    sums = lax.all_to_all(sums, "dp", 0, 0, axis_index_groups=same_place())
    grads = backward(same, stays, queries, key_rows, value_rows, grad_ctx, back)
    grad_weight = total(*sums)
    return (*grads, grad_weight)


def solution(mesh):
    placed = (
        P("dp", "fsdp"),
        P("dp", "fsdp"),
        P("dp", "fsdp"),
        P("dp"),
        P("dp"),
        P("fsdp", None),
        P("dp", None),
    )
    return jax.shard_map(
        local,
        mesh=mesh,
        in_specs=placed,
        out_specs=(P("dp", "fsdp"), P("dp", "fsdp"), P("dp", "fsdp"), P("fsdp", "dp")),
        check_vma=False,
    )
```

```python
import functools

import jax
import jax.numpy as jnp
from jax import lax
from jax.experimental import pallas as pl
from jax.experimental.pallas import tpu as pltpu
from jax.sharding import PartitionSpec as P

HD = 128
UNIT = 128
NZ, NY, NC = 3, 8, 2
ORDER = (4, 3, -3, 2, -2, 1, -1, 0)
VMEM = pl.BlockSpec(memory_space=pltpu.VMEM)
PARAMS = pltpu.CompilerParams(vmem_limit_bytes=8 * 1024 * 1024)


def dot(a, b, dims):
    return lax.dot_general(a, b, (dims, ((), ())), preferred_element_type=jnp.float32)


def softmax(scores):
    expo = jnp.exp(scores - jnp.max(scores, axis=-1, keepdims=True))
    return expo / jnp.sum(expo, axis=-1, keepdims=True)


def unit_weights(q, k, mask):
    return softmax(jnp.where(mask, dot(q, k, ((1,), (1,))) * HD**-0.5, -jnp.inf))


def leaving_kernel(ids_hbm, slot_hbm, q_hbm, k_hbm, v_hbm, leave_ref, same_ref, stays_ref, q_ref, k_ref, v_ref,
                   ids_ref, slot_ref, sems):
    pairs = [(ids_hbm, ids_ref), (slot_hbm, slot_ref), (q_hbm, q_ref), (k_hbm, k_ref), (v_hbm, v_ref)]
    copies = [pltpu.make_async_copy(src, dst, sems.at[i]) for i, (src, dst) in enumerate(pairs)]
    for copy in copies:
        copy.start()
    for copy in copies:
        copy.wait()
    rows, width = q_ref.shape
    units = rows // UNIT
    stays = [slot_ref[u * UNIT] < rows for u in range(units)]
    first = jnp.int32(0)
    for u in range(1, units):
        first = jnp.where(stays[u], first, u * UNIT)
    moves = slot_ref[first] >= rows
    moved = pl.ds(pl.multiple_of(first, UNIT), UNIT)
    for h in range(width // HD):
        cols = pl.ds(h * HD, HD)
        w = softmax(dot(q_ref[moved, cols], k_ref[moved, cols], ((1,), (1,))) * HD**-0.5)
        ctx = dot(v_ref[moved, cols].T, w.astype(jnp.bfloat16), ((1,), (1,)))
        leave_ref[cols, :] = jnp.where(moves, ctx, 0.0).astype(jnp.bfloat16)
    lane_unit = lax.broadcasted_iota(jnp.int32, (1, rows), 1) // UNIT
    lane_ids = jnp.full((1, rows), ids_ref[0], jnp.int32)
    for u in range(1, units):
        lane_ids = jnp.where(lane_unit == u, ids_ref[u * UNIT], lane_ids)
    for u in range(units):
        same_ref[pl.ds(u, 1), :] = (lane_ids == ids_ref[u * UNIT]).astype(jnp.int32)
        stays_ref[pl.ds(u, 1), :] = jnp.full((1, UNIT), stays[u].astype(jnp.int32), jnp.int32)


def leaving_context(image_ids, send_slot, q, k, v):
    rows, width = q.shape
    shapes = [
        jax.ShapeDtypeStruct((width, UNIT), jnp.bfloat16),
        jax.ShapeDtypeStruct((8, rows), jnp.int32),
        jax.ShapeDtypeStruct((8, UNIT), jnp.int32),
    ] + [jax.ShapeDtypeStruct(q.shape, jnp.bfloat16)] * 3
    return pl.pallas_call(
        leaving_kernel,
        in_specs=[pl.BlockSpec(memory_space=pltpu.HBM)] * 5,
        out_specs=[VMEM] * 6,
        out_shape=shapes,
        scratch_shapes=[
            pltpu.SMEM(image_ids.shape, jnp.int32),
            pltpu.SMEM(send_slot.shape, jnp.int32),
            pltpu.SemaphoreType.DMA((5,)),
        ],
        compiler_params=PARAMS,
    )(*[in_hbm(x) for x in (image_ids, send_slot, q, k, v)])


def context_kernel(same_ref, stays_ref, q_ref, k_ref, v_ref, g_hbm, stay_ref, g_ref, sem):
    copy = pltpu.make_async_copy(g_hbm, g_ref, sem)
    copy.start()
    for h in range(q_ref.shape[1] // HD):
        cols = pl.ds(h * HD, HD)
        v_t = v_ref[:, cols].T
        for u in range(q_ref.shape[0] // UNIT):
            rows = pl.ds(u * UNIT, UNIT)
            w = unit_weights(q_ref[rows, cols], k_ref[:, cols], same_ref[u : u + 1, :] != 0)
            ctx = dot(v_t, w.astype(jnp.bfloat16), ((1,), (1,)))
            stay_ref[cols, rows] = jnp.where(stays_ref[u : u + 1, :] != 0, ctx, 0.0).astype(jnp.bfloat16)
    copy.wait()


def staying_context(same, stays, q, k, v, grad_out):
    shapes = [q.shape[::-1], grad_out.shape]
    return pl.pallas_call(
        context_kernel,
        in_specs=[VMEM] * 5 + [pl.BlockSpec(memory_space=pltpu.HBM)],
        out_specs=[VMEM] * 2,
        out_shape=[jax.ShapeDtypeStruct(shape, jnp.bfloat16) for shape in shapes],
        scratch_shapes=[pltpu.SemaphoreType.DMA],
        compiler_params=PARAMS,
    )(same, stays, q, k, v, in_hbm(grad_out))


def in_hbm(x):
    return pltpu.with_memory_space_constraint(x, pltpu.HBM)


def partial_kernel(other, stay_ref, came_ref, g_ref, out_ref):
    me = lax.axis_index("dp")
    y, c = (me // NC) % NY, me % NC
    core = 1 - c if other else c
    ctx_t = jnp.concatenate([stay_ref[...], came_ref[...]], axis=1)
    width = ctx_t.shape[0]
    for n, distance in enumerate(ORDER):
        y_to = (y + NY + distance * (1 - 2 * core)) % NY
        dest = [(i * NY + y_to) * NC + core for i in range(NZ)]
        g = jnp.concatenate([g_ref[:, pl.ds(pl.multiple_of(d * UNIT, UNIT), UNIT)] for d in dest], axis=1)
        part = dot(ctx_t, g, ((1,), (0,))).astype(jnp.bfloat16)
        for i in range(NZ):
            out_ref[pl.ds((n * NZ + i) * width, width), :] = part[:, i * UNIT : (i + 1) * UNIT]


def partial_grad(other, stay, came, grad_out):
    shape = (NY * NZ * stay.shape[0], UNIT)
    return pl.pallas_call(
        functools.partial(partial_kernel, other),
        in_specs=[VMEM, VMEM, VMEM],
        out_specs=VMEM,
        out_shape=jax.ShapeDtypeStruct(shape, jnp.bfloat16),
        compiler_params=PARAMS,
    )(stay, came, grad_out)


def grad_context_kernel(g_ref, w_ref, out_ref):
    step = 1024
    acc = jnp.zeros(out_ref.shape, jnp.float32)
    for i in range(0, g_ref.shape[1], step):
        acc += dot(g_ref[:, i : i + step], w_ref[:, i : i + step], ((1,), (1,)))
    out_ref[...] = acc.astype(jnp.bfloat16)


def grad_context(grad_out, out_weight):
    shape = (grad_out.shape[0], out_weight.shape[0])
    return pl.pallas_call(
        grad_context_kernel,
        in_specs=[VMEM] * 2,
        out_specs=VMEM,
        out_shape=jax.ShapeDtypeStruct(shape, jnp.bfloat16),
        compiler_params=PARAMS,
    )(grad_out, out_weight)


def backward_kernel(same_ref, stays_ref, q_ref, k_ref, v_ref, g_ref, back_ref, dq_ref, dk_ref, dv_ref):
    for h in range(q_ref.shape[1] // HD):
        cols = pl.ds(h * HD, HD)
        k, v = k_ref[:, cols], v_ref[:, cols]
        dk = jnp.zeros(k.shape, jnp.float32)
        dv = jnp.zeros(v.shape, jnp.float32)
        for u in range(q_ref.shape[0] // UNIT):
            rows = pl.ds(u * UNIT, UNIT)
            q = q_ref[rows, cols]
            w = unit_weights(q, k, same_ref[u : u + 1, :] != 0)
            stays = stays_ref[u : u + 1, :] != 0
            g = jnp.where(stays, g_ref[rows, cols].astype(jnp.float32), back_ref[:, cols].astype(jnp.float32))
            g = g.astype(jnp.bfloat16)
            dv += dot(w.astype(jnp.bfloat16), g, ((0,), (0,)))
            dw = dot(g, v, ((1,), (1,)))
            ds = (w * (dw - jnp.sum(w * dw, axis=-1, keepdims=True))).astype(jnp.bfloat16)
            dq_ref[rows, cols] = (dot(ds, k, ((1,), (0,))) * HD**-0.5).astype(jnp.bfloat16)
            dk += dot(ds, q, ((0,), (0,)))
        dk_ref[:, cols] = (dk * HD**-0.5).astype(jnp.bfloat16)
        dv_ref[:, cols] = dv.astype(jnp.bfloat16)


def backward(same, stays, q, k, v, g, back):
    return pl.pallas_call(
        backward_kernel,
        in_specs=[VMEM] * 7,
        out_specs=[VMEM] * 3,
        out_shape=[jax.ShapeDtypeStruct(q.shape, jnp.bfloat16)] * 3,
        compiler_params=PARAMS,
    )(same, stays, q, k, v, g, back)


PLACES = [(z, y, c) for z in range(NZ) for y in range(NY) for c in range(NC)]


def index(z, y, c):
    return (z % NZ * NY + y % NY) * NC + c


def send(block, to):
    return lax.ppermute(block, "dp", [(index(*p), index(*to(*p))) for p in PLACES])


def along_y(step):
    return lambda z, y, c: (z, y + step * (1 - 2 * c), c)


def same_place():
    return [[index(z, y, c) for z in range(NZ)] for y in range(NY) for c in range(NC)]


def sibling(z, y, c):
    return (z, y, 1 - c)


def total(*terms):
    return sum(t.astype(jnp.float32) for t in terms)


def rounded_total(*terms):
    return total(*terms).astype(jnp.bfloat16)


def local(queries, key_rows, value_rows, image_ids, send_slot, out_weight, grad_out):
    row_count, width = queries.shape
    ranks = lax.axis_size("dp")
    leave, same, stays, q, k, v = leaving_context(image_ids, send_slot, queries, key_rows, value_rows)
    came = lax.ppermute(leave, "dp", [(i, (i + 1) % ranks) for i in range(ranks)])
    stay, g_near = staying_context(same, stays, q, k, v, grad_out)
    grad_ctx = grad_context(g_near, out_weight)
    stay, grad_ctx = lax.optimization_barrier((stay, grad_ctx))

    size = NZ * width

    def cut(x):
        return [x[i : i + size] for i in range(0, x.shape[0], size)]

    got = send(partial_grad(True, stay, came, g_near), sibling)
    own = partial_grad(False, stay, came, g_near)
    parts = [rounded_total(*pair) for pair in zip(cut(own), cut(got), strict=True)]
    *parts, tail = lax.optimization_barrier((*parts, grad_ctx[row_count:]))
    part = dict(zip(ORDER, parts, strict=True))
    far, up, down = send(part[4], along_y(2)), send(part[3], along_y(1)), send(part[-3], along_y(-1))
    near = send(part[1], along_y(1)), send(part[-1], along_y(-1))
    back = lax.ppermute(tail, "dp", [((i + 1) % ranks, i) for i in range(ranks)])

    up, down = rounded_total(part[2], up, far), rounded_total(part[-2], down)
    down, back = lax.optimization_barrier((down, back))
    up, down = send(up, along_y(2)), send(down, along_y(-2))
    sums = rounded_total(part[0], up, down, *near).reshape(NZ, -1, UNIT)
    grads = backward(same, stays, queries, key_rows, value_rows, grad_ctx, back)
    sums, *grads = lax.optimization_barrier((sums, *grads))
    sums = lax.all_to_all(sums, "dp", 0, 0, axis_index_groups=same_place())
    grad_weight = total(*sums)
    return (*grads, grad_weight)


def solution(mesh):
    placed = (
        P("dp", "fsdp"),
        P("dp", "fsdp"),
        P("dp", "fsdp"),
        P("dp"),
        P("dp"),
        P("fsdp", None),
        P("dp", None),
    )
    return jax.shard_map(
        local,
        mesh=mesh,
        in_specs=placed,
        out_specs=(P("dp", "fsdp"), P("dp", "fsdp"), P("dp", "fsdp"), P("fsdp", "dp")),
        check_vma=False,
    )
```

```python
import functools

import jax
import jax.numpy as jnp
from jax import lax
from jax.experimental import pallas as pl
from jax.experimental.pallas import tpu as pltpu
from jax.sharding import PartitionSpec as P

HD = 128
UNIT = 128
NZ, NY, NC = 3, 8, 2
ORDER = (4, 3, 1, -3, -1, 2, -2, 0)
VMEM = pl.BlockSpec(memory_space=pltpu.VMEM)
PARAMS = pltpu.CompilerParams(vmem_limit_bytes=8 * 1024 * 1024)


def dot(a, b, dims):
    return lax.dot_general(a, b, (dims, ((), ())), preferred_element_type=jnp.float32)


def softmax(scores):
    expo = jnp.exp(scores - jnp.max(scores, axis=-1, keepdims=True))
    return expo / jnp.sum(expo, axis=-1, keepdims=True)


def unit_weights(q, k, mask):
    return softmax(jnp.where(mask, dot(q, k, ((1,), (1,))) * HD**-0.5, -jnp.inf))


def leaving_kernel(ids_hbm, slot_hbm, q_hbm, k_hbm, v_hbm, leave_ref, same_ref, stays_ref, q_ref, k_ref, v_ref,
                   ids_ref, slot_ref, sems):
    pairs = [(ids_hbm, ids_ref), (slot_hbm, slot_ref), (q_hbm, q_ref), (k_hbm, k_ref), (v_hbm, v_ref)]
    copies = [pltpu.make_async_copy(src, dst, sems.at[i]) for i, (src, dst) in enumerate(pairs)]
    for copy in copies:
        copy.start()
    for copy in copies:
        copy.wait()
    rows, width = q_ref.shape
    units = rows // UNIT
    stays = [slot_ref[u * UNIT] < rows for u in range(units)]
    first = jnp.int32(0)
    for u in range(1, units):
        first = jnp.where(stays[u], first, u * UNIT)
    moves = slot_ref[first] >= rows
    moved = pl.ds(pl.multiple_of(first, UNIT), UNIT)
    for h in range(width // HD):
        cols = pl.ds(h * HD, HD)
        w = softmax(dot(q_ref[moved, cols], k_ref[moved, cols], ((1,), (1,))) * HD**-0.5)
        ctx = dot(v_ref[moved, cols].T, w.astype(jnp.bfloat16), ((1,), (1,)))
        leave_ref[cols, :] = jnp.where(moves, ctx, 0.0).astype(jnp.bfloat16)
    lane_unit = lax.broadcasted_iota(jnp.int32, (1, rows), 1) // UNIT
    lane_ids = jnp.full((1, rows), ids_ref[0], jnp.int32)
    for u in range(1, units):
        lane_ids = jnp.where(lane_unit == u, ids_ref[u * UNIT], lane_ids)
    for u in range(units):
        same_ref[pl.ds(u, 1), :] = (lane_ids == ids_ref[u * UNIT]).astype(jnp.int32)
        stays_ref[pl.ds(u, 1), :] = jnp.full((1, UNIT), stays[u].astype(jnp.int32), jnp.int32)


def leaving_context(image_ids, send_slot, q, k, v):
    rows, width = q.shape
    shapes = [
        jax.ShapeDtypeStruct((width, UNIT), jnp.bfloat16),
        jax.ShapeDtypeStruct((8, rows), jnp.int32),
        jax.ShapeDtypeStruct((8, UNIT), jnp.int32),
    ] + [jax.ShapeDtypeStruct(q.shape, jnp.bfloat16)] * 3
    return pl.pallas_call(
        leaving_kernel,
        in_specs=[pl.BlockSpec(memory_space=pltpu.HBM)] * 5,
        out_specs=[VMEM] * 6,
        out_shape=shapes,
        scratch_shapes=[
            pltpu.SMEM(image_ids.shape, jnp.int32),
            pltpu.SMEM(send_slot.shape, jnp.int32),
            pltpu.SemaphoreType.DMA((5,)),
        ],
        compiler_params=PARAMS,
    )(*[in_hbm(x) for x in (image_ids, send_slot, q, k, v)])


def context_kernel(same_ref, stays_ref, q_ref, k_ref, v_ref, g_hbm, stay_ref, g_ref, sem):
    copy = pltpu.make_async_copy(g_hbm, g_ref, sem)
    copy.start()
    for h in range(q_ref.shape[1] // HD):
        cols = pl.ds(h * HD, HD)
        v_t = v_ref[:, cols].T
        for u in range(q_ref.shape[0] // UNIT):
            rows = pl.ds(u * UNIT, UNIT)
            w = unit_weights(q_ref[rows, cols], k_ref[:, cols], same_ref[u : u + 1, :] != 0)
            ctx = dot(v_t, w.astype(jnp.bfloat16), ((1,), (1,)))
            stay_ref[cols, rows] = jnp.where(stays_ref[u : u + 1, :] != 0, ctx, 0.0).astype(jnp.bfloat16)
    copy.wait()


def staying_context(same, stays, q, k, v, grad_out):
    shapes = [q.shape[::-1], grad_out.shape]
    return pl.pallas_call(
        context_kernel,
        in_specs=[VMEM] * 5 + [pl.BlockSpec(memory_space=pltpu.HBM)],
        out_specs=[VMEM] * 2,
        out_shape=[jax.ShapeDtypeStruct(shape, jnp.bfloat16) for shape in shapes],
        scratch_shapes=[pltpu.SemaphoreType.DMA],
        compiler_params=PARAMS,
    )(same, stays, q, k, v, in_hbm(grad_out))


def in_hbm(x):
    return pltpu.with_memory_space_constraint(x, pltpu.HBM)


def partial_kernel(other, stay_ref, came_ref, g_ref, out_ref):
    me = lax.axis_index("dp")
    y, c = (me // NC) % NY, me % NC
    core = 1 - c if other else c
    ctx_t = jnp.concatenate([stay_ref[...], came_ref[...]], axis=1)
    width = ctx_t.shape[0]
    for n, distance in enumerate(ORDER):
        y_to = (y + NY + distance * (1 - 2 * core)) % NY
        dest = [(i * NY + y_to) * NC + core for i in range(NZ)]
        g = jnp.concatenate([g_ref[:, pl.ds(pl.multiple_of(d * UNIT, UNIT), UNIT)] for d in dest], axis=1)
        part = dot(ctx_t, g, ((1,), (0,))).astype(jnp.bfloat16)
        for i in range(NZ):
            out_ref[pl.ds((n * NZ + i) * width, width), :] = part[:, i * UNIT : (i + 1) * UNIT]


def partial_grad(other, stay, came, grad_out):
    shape = (NY * NZ * stay.shape[0], UNIT)
    return pl.pallas_call(
        functools.partial(partial_kernel, other),
        in_specs=[VMEM, VMEM, VMEM],
        out_specs=VMEM,
        out_shape=jax.ShapeDtypeStruct(shape, jnp.bfloat16),
        compiler_params=PARAMS,
    )(stay, came, grad_out)


def grad_context_kernel(g_ref, w_ref, out_ref):
    step = 1024
    acc = jnp.zeros(out_ref.shape, jnp.float32)
    for i in range(0, g_ref.shape[1], step):
        acc += dot(g_ref[:, i : i + step], w_ref[:, i : i + step], ((1,), (1,)))
    out_ref[...] = acc.astype(jnp.bfloat16)


def grad_context(grad_out, out_weight):
    shape = (grad_out.shape[0], out_weight.shape[0])
    return pl.pallas_call(
        grad_context_kernel,
        in_specs=[VMEM] * 2,
        out_specs=VMEM,
        out_shape=jax.ShapeDtypeStruct(shape, jnp.bfloat16),
        compiler_params=PARAMS,
    )(grad_out, out_weight)


def backward_kernel(same_ref, stays_ref, q_ref, k_ref, v_ref, g_ref, back_ref, dq_ref, dk_ref, dv_ref):
    for h in range(q_ref.shape[1] // HD):
        cols = pl.ds(h * HD, HD)
        k, v = k_ref[:, cols], v_ref[:, cols]
        dk = jnp.zeros(k.shape, jnp.float32)
        dv = jnp.zeros(v.shape, jnp.float32)
        for u in range(q_ref.shape[0] // UNIT):
            rows = pl.ds(u * UNIT, UNIT)
            q = q_ref[rows, cols]
            w = unit_weights(q, k, same_ref[u : u + 1, :] != 0)
            stays = stays_ref[u : u + 1, :] != 0
            g = jnp.where(stays, g_ref[rows, cols].astype(jnp.float32), back_ref[:, cols].astype(jnp.float32))
            g = g.astype(jnp.bfloat16)
            dv += dot(w.astype(jnp.bfloat16), g, ((0,), (0,)))
            dw = dot(g, v, ((1,), (1,)))
            ds = (w * (dw - jnp.sum(w * dw, axis=-1, keepdims=True))).astype(jnp.bfloat16)
            dq_ref[rows, cols] = (dot(ds, k, ((1,), (0,))) * HD**-0.5).astype(jnp.bfloat16)
            dk += dot(ds, q, ((0,), (0,)))
        dk_ref[:, cols] = (dk * HD**-0.5).astype(jnp.bfloat16)
        dv_ref[:, cols] = dv.astype(jnp.bfloat16)


def backward(same, stays, q, k, v, g, back):
    return pl.pallas_call(
        backward_kernel,
        in_specs=[VMEM] * 7,
        out_specs=[VMEM] * 3,
        out_shape=[jax.ShapeDtypeStruct(q.shape, jnp.bfloat16)] * 3,
        compiler_params=PARAMS,
    )(same, stays, q, k, v, g, back)


PLACES = [(z, y, c) for z in range(NZ) for y in range(NY) for c in range(NC)]


def index(z, y, c):
    return (z % NZ * NY + y % NY) * NC + c


def send(block, to):
    return lax.ppermute(block, "dp", [(index(*p), index(*to(*p))) for p in PLACES])


def along_y(step):
    return lambda z, y, c: (z, y + step * (1 - 2 * c), c)


def same_place():
    return [[index(z, y, c) for z in range(NZ)] for y in range(NY) for c in range(NC)]


def sibling(z, y, c):
    return (z, y, 1 - c)


def total(*terms):
    return sum(t.astype(jnp.float32) for t in terms)


def rounded_total(*terms):
    return total(*terms).astype(jnp.bfloat16)


def local(queries, key_rows, value_rows, image_ids, send_slot, out_weight, grad_out):
    row_count, width = queries.shape
    ranks = lax.axis_size("dp")
    leave, same, stays, q, k, v = leaving_context(image_ids, send_slot, queries, key_rows, value_rows)
    came = lax.ppermute(leave, "dp", [(i, (i + 1) % ranks) for i in range(ranks)])
    stay, g_near = staying_context(same, stays, q, k, v, grad_out)
    grad_ctx = grad_context(g_near, out_weight)
    stay, grad_ctx = lax.optimization_barrier((stay, grad_ctx))

    size = NZ * width

    got = send(partial_grad(True, stay, came, g_near), sibling)
    own = partial_grad(False, stay, came, g_near)
    parts = []
    for first, last in ((4, 4), (3, 1), (-3, -1), (2, 2), (-2, -2), (0, 0)):
        rows = slice(ORDER.index(first) * size, (ORDER.index(last) + 1) * size)
        parts.append(rounded_total(own[rows], got[rows]))
    far, up, down, up2, down2, here = lax.optimization_barrier(parts)
    far, up, down = send(far, along_y(2)), send(up, along_y(1)), send(down, along_y(-1))
    near = up[size:], down[size:]

    up, down = rounded_total(up2, up[:size], far), rounded_total(down2, down[:size])
    up, down, tail = lax.optimization_barrier((up, down, grad_ctx[row_count:]))
    up, down = send(up, along_y(2)), send(down, along_y(-2))
    back = lax.ppermute(tail, "dp", [((i + 1) % ranks, i) for i in range(ranks)])
    sums = rounded_total(here, up, down, *near).reshape(NZ, -1, UNIT)
    sums, back = lax.optimization_barrier((sums, back))
    sums = lax.all_to_all(sums, "dp", 0, 0, axis_index_groups=same_place())
    grads = backward(same, stays, queries, key_rows, value_rows, grad_ctx, back)
    grad_weight = total(*sums)
    return (*grads, grad_weight)


def solution(mesh):
    placed = (
        P("dp", "fsdp"),
        P("dp", "fsdp"),
        P("dp", "fsdp"),
        P("dp"),
        P("dp"),
        P("fsdp", None),
        P("dp", None),
    )
    return jax.shard_map(
        local,
        mesh=mesh,
        in_specs=placed,
        out_specs=(P("dp", "fsdp"), P("dp", "fsdp"), P("dp", "fsdp"), P("fsdp", "dp")),
        check_vma=False,
    )
```

```python
import functools

import jax
import jax.numpy as jnp
from jax import lax
from jax.experimental import pallas as pl
from jax.experimental.pallas import tpu as pltpu
from jax.sharding import PartitionSpec as P

HD = 128
UNIT = 128
NZ, NY, NC = 3, 8, 2
ORDER = (4, 3, -3, 2, -2, 1, -1, 0)
VMEM = pl.BlockSpec(memory_space=pltpu.VMEM)
PARAMS = pltpu.CompilerParams(vmem_limit_bytes=8 * 1024 * 1024)


def dot(a, b, dims):
    return lax.dot_general(a, b, (dims, ((), ())), preferred_element_type=jnp.float32)


def softmax(scores):
    expo = jnp.exp(scores - jnp.max(scores, axis=-1, keepdims=True))
    return expo / jnp.sum(expo, axis=-1, keepdims=True)


def unit_weights(q, k, mask):
    return softmax(jnp.where(mask, dot(q, k, ((1,), (1,))) * HD**-0.5, -jnp.inf))


def leaving_kernel(ids_hbm, slot_hbm, q_hbm, k_hbm, v_hbm, leave_ref, same_ref, stays_ref, q_ref, k_ref, v_ref,
                   ids_ref, slot_ref, sems):
    pairs = [(ids_hbm, ids_ref), (slot_hbm, slot_ref), (q_hbm, q_ref), (k_hbm, k_ref), (v_hbm, v_ref)]
    copies = [pltpu.make_async_copy(src, dst, sems.at[i]) for i, (src, dst) in enumerate(pairs)]
    for copy in copies:
        copy.start()
    for copy in copies:
        copy.wait()
    rows, width = q_ref.shape
    units = rows // UNIT
    stays = [slot_ref[u * UNIT] < rows for u in range(units)]
    first = jnp.int32(0)
    for u in range(1, units):
        first = jnp.where(stays[u], first, u * UNIT)
    moves = slot_ref[first] >= rows
    moved = pl.ds(pl.multiple_of(first, UNIT), UNIT)
    for h in range(width // HD):
        cols = pl.ds(h * HD, HD)
        w = softmax(dot(q_ref[moved, cols], k_ref[moved, cols], ((1,), (1,))) * HD**-0.5)
        ctx = dot(v_ref[moved, cols].T, w.astype(jnp.bfloat16), ((1,), (1,)))
        leave_ref[cols, :] = jnp.where(moves, ctx, 0.0).astype(jnp.bfloat16)
    lane_unit = lax.broadcasted_iota(jnp.int32, (1, rows), 1) // UNIT
    lane_ids = jnp.full((1, rows), ids_ref[0], jnp.int32)
    for u in range(1, units):
        lane_ids = jnp.where(lane_unit == u, ids_ref[u * UNIT], lane_ids)
    for u in range(units):
        same_ref[pl.ds(u, 1), :] = (lane_ids == ids_ref[u * UNIT]).astype(jnp.int32)
        stays_ref[pl.ds(u, 1), :] = jnp.full((1, UNIT), stays[u].astype(jnp.int32), jnp.int32)


def leaving_context(image_ids, send_slot, q, k, v):
    rows, width = q.shape
    shapes = [
        jax.ShapeDtypeStruct((width, UNIT), jnp.bfloat16),
        jax.ShapeDtypeStruct((8, rows), jnp.int32),
        jax.ShapeDtypeStruct((8, UNIT), jnp.int32),
    ] + [jax.ShapeDtypeStruct(q.shape, jnp.bfloat16)] * 3
    return pl.pallas_call(
        leaving_kernel,
        in_specs=[pl.BlockSpec(memory_space=pltpu.HBM)] * 5,
        out_specs=[VMEM] * 6,
        out_shape=shapes,
        scratch_shapes=[
            pltpu.SMEM(image_ids.shape, jnp.int32),
            pltpu.SMEM(send_slot.shape, jnp.int32),
            pltpu.SemaphoreType.DMA((5,)),
        ],
        compiler_params=PARAMS,
    )(*[in_hbm(x) for x in (image_ids, send_slot, q, k, v)])


def context_kernel(same_ref, stays_ref, q_ref, k_ref, v_ref, g_hbm, stay_ref, g_ref, sem):
    copy = pltpu.make_async_copy(g_hbm, g_ref, sem)
    copy.start()
    for h in range(q_ref.shape[1] // HD):
        cols = pl.ds(h * HD, HD)
        v_t = v_ref[:, cols].T
        for u in range(q_ref.shape[0] // UNIT):
            rows = pl.ds(u * UNIT, UNIT)
            w = unit_weights(q_ref[rows, cols], k_ref[:, cols], same_ref[u : u + 1, :] != 0)
            ctx = dot(v_t, w.astype(jnp.bfloat16), ((1,), (1,)))
            stay_ref[cols, rows] = jnp.where(stays_ref[u : u + 1, :] != 0, ctx, 0.0).astype(jnp.bfloat16)
    copy.wait()


def staying_context(same, stays, q, k, v, grad_out):
    shapes = [q.shape[::-1], grad_out.shape]
    return pl.pallas_call(
        context_kernel,
        in_specs=[VMEM] * 5 + [pl.BlockSpec(memory_space=pltpu.HBM)],
        out_specs=[VMEM] * 2,
        out_shape=[jax.ShapeDtypeStruct(shape, jnp.bfloat16) for shape in shapes],
        scratch_shapes=[pltpu.SemaphoreType.DMA],
        compiler_params=PARAMS,
    )(same, stays, q, k, v, in_hbm(grad_out))


def in_hbm(x):
    return pltpu.with_memory_space_constraint(x, pltpu.HBM)


def partial_kernel(other, stay_ref, came_ref, g_ref, out_ref):
    me = lax.axis_index("dp")
    y, c = (me // NC) % NY, me % NC
    core = 1 - c if other else c
    ctx_t = jnp.concatenate([stay_ref[...], came_ref[...]], axis=1)
    width = ctx_t.shape[0]
    for n, distance in enumerate(ORDER):
        y_to = (y + NY + distance * (1 - 2 * core)) % NY
        dest = [(i * NY + y_to) * NC + core for i in range(NZ)]
        g = jnp.concatenate([g_ref[:, pl.ds(pl.multiple_of(d * UNIT, UNIT), UNIT)] for d in dest], axis=1)
        part = dot(ctx_t, g, ((1,), (0,))).astype(jnp.bfloat16)
        for i in range(NZ):
            out_ref[pl.ds((n * NZ + i) * width, width), :] = part[:, i * UNIT : (i + 1) * UNIT]


def partial_grad(other, stay, came, grad_out):
    shape = (NY * NZ * stay.shape[0], UNIT)
    return pl.pallas_call(
        functools.partial(partial_kernel, other),
        in_specs=[VMEM, VMEM, VMEM],
        out_specs=VMEM,
        out_shape=jax.ShapeDtypeStruct(shape, jnp.bfloat16),
        compiler_params=PARAMS,
    )(stay, came, grad_out)


def grad_context_kernel(g_ref, w_ref, out_ref):
    step = 1024
    acc = jnp.zeros(out_ref.shape, jnp.float32)
    for i in range(0, g_ref.shape[1], step):
        acc += dot(g_ref[:, i : i + step], w_ref[:, i : i + step], ((1,), (1,)))
    out_ref[...] = acc.astype(jnp.bfloat16)


def grad_context(grad_out, out_weight):
    shape = (grad_out.shape[0], out_weight.shape[0])
    return pl.pallas_call(
        grad_context_kernel,
        in_specs=[VMEM] * 2,
        out_specs=VMEM,
        out_shape=jax.ShapeDtypeStruct(shape, jnp.bfloat16),
        compiler_params=PARAMS,
    )(grad_out, out_weight)


def backward_kernel(same_ref, stays_ref, q_ref, k_ref, v_ref, g_ref, back_ref, dq_ref, dk_ref, dv_ref):
    for h in range(q_ref.shape[1] // HD):
        cols = pl.ds(h * HD, HD)
        k, v = k_ref[:, cols], v_ref[:, cols]
        dk = jnp.zeros(k.shape, jnp.float32)
        dv = jnp.zeros(v.shape, jnp.float32)
        for u in range(q_ref.shape[0] // UNIT):
            rows = pl.ds(u * UNIT, UNIT)
            q = q_ref[rows, cols]
            w = unit_weights(q, k, same_ref[u : u + 1, :] != 0)
            stays = stays_ref[u : u + 1, :] != 0
            g = jnp.where(stays, g_ref[rows, cols].astype(jnp.float32), back_ref[:, cols].astype(jnp.float32))
            g = g.astype(jnp.bfloat16)
            dv += dot(w.astype(jnp.bfloat16), g, ((0,), (0,)))
            dw = dot(g, v, ((1,), (1,)))
            ds = (w * (dw - jnp.sum(w * dw, axis=-1, keepdims=True))).astype(jnp.bfloat16)
            dq_ref[rows, cols] = (dot(ds, k, ((1,), (0,))) * HD**-0.5).astype(jnp.bfloat16)
            dk += dot(ds, q, ((0,), (0,)))
        dk_ref[:, cols] = (dk * HD**-0.5).astype(jnp.bfloat16)
        dv_ref[:, cols] = dv.astype(jnp.bfloat16)


def backward(same, stays, q, k, v, g, back):
    return pl.pallas_call(
        backward_kernel,
        in_specs=[VMEM] * 7,
        out_specs=[VMEM] * 3,
        out_shape=[jax.ShapeDtypeStruct(q.shape, jnp.bfloat16)] * 3,
        compiler_params=PARAMS,
    )(same, stays, q, k, v, g, back)


PLACES = [(z, y, c) for z in range(NZ) for y in range(NY) for c in range(NC)]


def index(z, y, c):
    return (z % NZ * NY + y % NY) * NC + c


def send(block, to):
    return lax.ppermute(block, "dp", [(index(*p), index(*to(*p))) for p in PLACES])


def along_y(step):
    return lambda z, y, c: (z, y + step * (1 - 2 * c), c)


def same_place():
    return [[index(z, y, c) for z in range(NZ)] for y in range(NY) for c in range(NC)]


def sibling(z, y, c):
    return (z, y, 1 - c)


def total(*terms):
    return sum(t.astype(jnp.float32) for t in terms)


def rounded_total(*terms):
    return total(*terms).astype(jnp.bfloat16)


def local(queries, key_rows, value_rows, image_ids, send_slot, out_weight, grad_out):
    row_count, width = queries.shape
    ranks = lax.axis_size("dp")
    leave, same, stays, q, k, v = leaving_context(image_ids, send_slot, queries, key_rows, value_rows)
    came = lax.ppermute(leave, "dp", [(i, (i + 1) % ranks) for i in range(ranks)])
    stay, g_near = staying_context(same, stays, q, k, v, grad_out)
    grad_ctx = grad_context(g_near, out_weight)
    stay, grad_ctx = lax.optimization_barrier((stay, grad_ctx))

    size = NZ * width

    def cut(x):
        return [x[i : i + size] for i in range(0, x.shape[0], size)]

    got = send(partial_grad(True, stay, came, g_near), sibling)
    own = partial_grad(False, stay, came, g_near)
    parts = [rounded_total(*pair) for pair in zip(cut(own), cut(got), strict=True)]
    part = dict(zip(ORDER, lax.optimization_barrier(parts), strict=True))
    far, up, down = send(part[4], along_y(2)), send(part[3], along_y(1)), send(part[-3], along_y(-1))
    near = send(part[1], along_y(1))

    up, down = rounded_total(part[2], up, far), rounded_total(part[-2], down)
    up, down, other, tail = lax.optimization_barrier((up, down, part[-1], grad_ctx[row_count:]))
    up, down, other = send(up, along_y(2)), send(down, along_y(-2)), send(other, along_y(-1))
    back = lax.ppermute(tail, "dp", [((i + 1) % ranks, i) for i in range(ranks)])
    sums = rounded_total(part[0], up, down, near, other).reshape(NZ, -1, UNIT)
    sums, back = lax.optimization_barrier((sums, back))
    sums = lax.all_to_all(sums, "dp", 0, 0, axis_index_groups=same_place())
    grads = backward(same, stays, queries, key_rows, value_rows, grad_ctx, back)
    grad_weight = total(*sums)
    return (*grads, grad_weight)


def solution(mesh):
    placed = (
        P("dp", "fsdp"),
        P("dp", "fsdp"),
        P("dp", "fsdp"),
        P("dp"),
        P("dp"),
        P("fsdp", None),
        P("dp", None),
    )
    return jax.shard_map(
        local,
        mesh=mesh,
        in_specs=placed,
        out_specs=(P("dp", "fsdp"), P("dp", "fsdp"), P("dp", "fsdp"), P("fsdp", "dp")),
        check_vma=False,
    )
```

```python
import functools

import jax
import jax.numpy as jnp
from jax import lax
from jax.experimental import pallas as pl
from jax.experimental.pallas import tpu as pltpu
from jax.sharding import PartitionSpec as P

HD = 128
UNIT = 128
NZ, NY, NC = 3, 8, 2
ORDER = (4, -3, 3, -2, 2, -1, 1, 0)
VMEM = pl.BlockSpec(memory_space=pltpu.VMEM)
PARAMS = pltpu.CompilerParams(vmem_limit_bytes=8 * 1024 * 1024)


def dot(a, b, dims):
    return lax.dot_general(a, b, (dims, ((), ())), preferred_element_type=jnp.float32)


def softmax(scores):
    expo = jnp.exp(scores - jnp.max(scores, axis=-1, keepdims=True))
    return expo / jnp.sum(expo, axis=-1, keepdims=True)


def unit_weights(q, k, mask):
    return softmax(jnp.where(mask, dot(q, k, ((1,), (1,))) * HD**-0.5, -jnp.inf))


def leaving_kernel(ids_hbm, slot_hbm, q_hbm, k_hbm, v_hbm, leave_ref, same_ref, stays_ref, q_ref, k_ref, v_ref,
                   ids_ref, slot_ref, sems):
    pairs = [(ids_hbm, ids_ref), (slot_hbm, slot_ref), (q_hbm, q_ref), (k_hbm, k_ref), (v_hbm, v_ref)]
    copies = [pltpu.make_async_copy(src, dst, sems.at[i]) for i, (src, dst) in enumerate(pairs)]
    for copy in copies:
        copy.start()
    for copy in copies:
        copy.wait()
    rows, width = q_ref.shape
    units = rows // UNIT
    stays = [slot_ref[u * UNIT] < rows for u in range(units)]
    first = jnp.int32(0)
    for u in range(1, units):
        first = jnp.where(stays[u], first, u * UNIT)
    moves = slot_ref[first] >= rows
    moved = pl.ds(pl.multiple_of(first, UNIT), UNIT)
    for h in range(width // HD):
        cols = pl.ds(h * HD, HD)
        w = softmax(dot(q_ref[moved, cols], k_ref[moved, cols], ((1,), (1,))) * HD**-0.5)
        ctx = dot(v_ref[moved, cols].T, w.astype(jnp.bfloat16), ((1,), (1,)))
        leave_ref[cols, :] = jnp.where(moves, ctx, 0.0).astype(jnp.bfloat16)
    lane_unit = lax.broadcasted_iota(jnp.int32, (1, rows), 1) // UNIT
    lane_ids = jnp.full((1, rows), ids_ref[0], jnp.int32)
    for u in range(1, units):
        lane_ids = jnp.where(lane_unit == u, ids_ref[u * UNIT], lane_ids)
    for u in range(units):
        same_ref[pl.ds(u, 1), :] = (lane_ids == ids_ref[u * UNIT]).astype(jnp.int32)
        stays_ref[pl.ds(u, 1), :] = jnp.full((1, UNIT), stays[u].astype(jnp.int32), jnp.int32)


def leaving_context(image_ids, send_slot, q, k, v):
    rows, width = q.shape
    shapes = [
        jax.ShapeDtypeStruct((width, UNIT), jnp.bfloat16),
        jax.ShapeDtypeStruct((8, rows), jnp.int32),
        jax.ShapeDtypeStruct((8, UNIT), jnp.int32),
    ] + [jax.ShapeDtypeStruct(q.shape, jnp.bfloat16)] * 3
    return pl.pallas_call(
        leaving_kernel,
        in_specs=[pl.BlockSpec(memory_space=pltpu.HBM)] * 5,
        out_specs=[VMEM] * 6,
        out_shape=shapes,
        scratch_shapes=[
            pltpu.SMEM(image_ids.shape, jnp.int32),
            pltpu.SMEM(send_slot.shape, jnp.int32),
            pltpu.SemaphoreType.DMA((5,)),
        ],
        compiler_params=PARAMS,
    )(*[in_hbm(x) for x in (image_ids, send_slot, q, k, v)])


def context_kernel(same_ref, stays_ref, q_ref, k_ref, v_ref, g_hbm, stay_ref, g_ref, sem):
    copy = pltpu.make_async_copy(g_hbm, g_ref, sem)
    copy.start()
    for h in range(q_ref.shape[1] // HD):
        cols = pl.ds(h * HD, HD)
        v_t = v_ref[:, cols].T
        for u in range(q_ref.shape[0] // UNIT):
            rows = pl.ds(u * UNIT, UNIT)
            w = unit_weights(q_ref[rows, cols], k_ref[:, cols], same_ref[u : u + 1, :] != 0)
            ctx = dot(v_t, w.astype(jnp.bfloat16), ((1,), (1,)))
            stay_ref[cols, rows] = jnp.where(stays_ref[u : u + 1, :] != 0, ctx, 0.0).astype(jnp.bfloat16)
    copy.wait()


def staying_context(same, stays, q, k, v, grad_out):
    shapes = [q.shape[::-1], grad_out.shape]
    return pl.pallas_call(
        context_kernel,
        in_specs=[VMEM] * 5 + [pl.BlockSpec(memory_space=pltpu.HBM)],
        out_specs=[VMEM] * 2,
        out_shape=[jax.ShapeDtypeStruct(shape, jnp.bfloat16) for shape in shapes],
        scratch_shapes=[pltpu.SemaphoreType.DMA],
        compiler_params=PARAMS,
    )(same, stays, q, k, v, in_hbm(grad_out))


def in_hbm(x):
    return pltpu.with_memory_space_constraint(x, pltpu.HBM)


def partial_kernel(other, stay_ref, came_ref, g_ref, out_ref):
    me = lax.axis_index("dp")
    y, c = (me // NC) % NY, me % NC
    core = 1 - c if other else c
    ctx_t = jnp.concatenate([stay_ref[...], came_ref[...]], axis=1)
    width = ctx_t.shape[0]
    for n, distance in enumerate(ORDER):
        y_to = (y + NY + distance * (1 - 2 * core)) % NY
        dest = [(i * NY + y_to) * NC + core for i in range(NZ)]
        g = jnp.concatenate([g_ref[:, pl.ds(pl.multiple_of(d * UNIT, UNIT), UNIT)] for d in dest], axis=1)
        part = dot(ctx_t, g, ((1,), (0,))).astype(jnp.bfloat16)
        for i in range(NZ):
            out_ref[pl.ds((n * NZ + i) * width, width), :] = part[:, i * UNIT : (i + 1) * UNIT]


def partial_grad(other, stay, came, grad_out):
    shape = (NY * NZ * stay.shape[0], UNIT)
    return pl.pallas_call(
        functools.partial(partial_kernel, other),
        in_specs=[VMEM, VMEM, VMEM],
        out_specs=VMEM,
        out_shape=jax.ShapeDtypeStruct(shape, jnp.bfloat16),
        compiler_params=PARAMS,
    )(stay, came, grad_out)


def grad_context_kernel(g_ref, w_ref, out_ref):
    step = 1024
    acc = jnp.zeros(out_ref.shape, jnp.float32)
    for i in range(0, g_ref.shape[1], step):
        acc += dot(g_ref[:, i : i + step], w_ref[:, i : i + step], ((1,), (1,)))
    out_ref[...] = acc.astype(jnp.bfloat16)


def grad_context(grad_out, out_weight):
    shape = (grad_out.shape[0], out_weight.shape[0])
    return pl.pallas_call(
        grad_context_kernel,
        in_specs=[VMEM] * 2,
        out_specs=VMEM,
        out_shape=jax.ShapeDtypeStruct(shape, jnp.bfloat16),
        compiler_params=PARAMS,
    )(grad_out, out_weight)


def backward_kernel(same_ref, stays_ref, q_ref, k_ref, v_ref, g_ref, back_ref, dq_ref, dk_ref, dv_ref):
    for h in range(q_ref.shape[1] // HD):
        cols = pl.ds(h * HD, HD)
        k, v = k_ref[:, cols], v_ref[:, cols]
        dk = jnp.zeros(k.shape, jnp.float32)
        dv = jnp.zeros(v.shape, jnp.float32)
        for u in range(q_ref.shape[0] // UNIT):
            rows = pl.ds(u * UNIT, UNIT)
            q = q_ref[rows, cols]
            w = unit_weights(q, k, same_ref[u : u + 1, :] != 0)
            stays = stays_ref[u : u + 1, :] != 0
            g = jnp.where(stays, g_ref[rows, cols].astype(jnp.float32), back_ref[:, cols].astype(jnp.float32))
            g = g.astype(jnp.bfloat16)
            dv += dot(w.astype(jnp.bfloat16), g, ((0,), (0,)))
            dw = dot(g, v, ((1,), (1,)))
            ds = (w * (dw - jnp.sum(w * dw, axis=-1, keepdims=True))).astype(jnp.bfloat16)
            dq_ref[rows, cols] = (dot(ds, k, ((1,), (0,))) * HD**-0.5).astype(jnp.bfloat16)
            dk += dot(ds, q, ((0,), (0,)))
        dk_ref[:, cols] = (dk * HD**-0.5).astype(jnp.bfloat16)
        dv_ref[:, cols] = dv.astype(jnp.bfloat16)


def backward(same, stays, q, k, v, g, back):
    return pl.pallas_call(
        backward_kernel,
        in_specs=[VMEM] * 7,
        out_specs=[VMEM] * 3,
        out_shape=[jax.ShapeDtypeStruct(q.shape, jnp.bfloat16)] * 3,
        compiler_params=PARAMS,
    )(same, stays, q, k, v, g, back)


PLACES = [(z, y, c) for z in range(NZ) for y in range(NY) for c in range(NC)]


def index(z, y, c):
    return (z % NZ * NY + y % NY) * NC + c


def send(block, to):
    return lax.ppermute(block, "dp", [(index(*p), index(*to(*p))) for p in PLACES])


def along_y(step):
    return lambda z, y, c: (z, y + step * (1 - 2 * c), c)


def same_place():
    return [[index(z, y, c) for z in range(NZ)] for y in range(NY) for c in range(NC)]


def sibling(z, y, c):
    return (z, y, 1 - c)


def total(*terms):
    return sum(t.astype(jnp.float32) for t in terms)


def rounded_total(*terms):
    return total(*terms).astype(jnp.bfloat16)


def local(queries, key_rows, value_rows, image_ids, send_slot, out_weight, grad_out):
    row_count, width = queries.shape
    ranks = lax.axis_size("dp")
    leave, same, stays, q, k, v = leaving_context(image_ids, send_slot, queries, key_rows, value_rows)
    came = lax.ppermute(leave, "dp", [(i, (i + 1) % ranks) for i in range(ranks)])
    stay, g_near = staying_context(same, stays, q, k, v, grad_out)
    grad_ctx = grad_context(g_near, out_weight)
    stay, grad_ctx = lax.optimization_barrier((stay, grad_ctx))

    size = NZ * width

    def cut(x):
        return [x[i : i + size] for i in range(0, x.shape[0], size)]

    got = send(partial_grad(True, stay, came, g_near), sibling)
    own = partial_grad(False, stay, came, g_near)
    parts = [rounded_total(*pair) for pair in zip(cut(own), cut(got), strict=True)]
    part = dict(zip(ORDER, lax.optimization_barrier(parts), strict=True))
    up, down = send(part[4], along_y(1)), send(part[-3], along_y(-1))
    up, down = send(rounded_total(part[3], up), along_y(1)), send(rounded_total(part[-2], down), along_y(-1))
    up, tail = lax.optimization_barrier((rounded_total(part[2], up), grad_ctx[row_count:]))
    up, down = send(up, along_y(1)), send(rounded_total(part[-1], down), along_y(-1))
    back = lax.ppermute(tail, "dp", [((i + 1) % ranks, i) for i in range(ranks)])
    up = send(rounded_total(part[1], up), along_y(1))
    sums = rounded_total(part[0], up, down).reshape(NZ, -1, UNIT)
    sums, back = lax.optimization_barrier((sums, back))
    sums = lax.all_to_all(sums, "dp", 0, 0, axis_index_groups=same_place())
    grads = backward(same, stays, queries, key_rows, value_rows, grad_ctx, back)
    grad_weight = total(*sums)
    return (*grads, grad_weight)


def solution(mesh):
    placed = (
        P("dp", "fsdp"),
        P("dp", "fsdp"),
        P("dp", "fsdp"),
        P("dp"),
        P("dp"),
        P("fsdp", None),
        P("dp", None),
    )
    return jax.shard_map(
        local,
        mesh=mesh,
        in_specs=placed,
        out_specs=(P("dp", "fsdp"), P("dp", "fsdp"), P("dp", "fsdp"), P("fsdp", "dp")),
        check_vma=False,
    )
```

```python
import functools

import jax
import jax.numpy as jnp
from jax import lax
from jax.experimental import pallas as pl
from jax.experimental.pallas import tpu as pltpu
from jax.sharding import PartitionSpec as P

HD = 128
UNIT = 128
NZ, NY, NC = 3, 8, 2
ORDER = (4, 3, -3, 2, -2, 1, -1, 0)
VMEM = pl.BlockSpec(memory_space=pltpu.VMEM)
PARAMS = pltpu.CompilerParams(vmem_limit_bytes=8 * 1024 * 1024)


def dot(a, b, dims):
    return lax.dot_general(a, b, (dims, ((), ())), preferred_element_type=jnp.float32)


def softmax(scores):
    expo = jnp.exp(scores - jnp.max(scores, axis=-1, keepdims=True))
    return expo / jnp.sum(expo, axis=-1, keepdims=True)


def unit_weights(q, k, mask):
    return softmax(jnp.where(mask, dot(q, k, ((1,), (1,))) * HD**-0.5, -jnp.inf))


def leaving_kernel(ids_hbm, slot_hbm, q_hbm, k_hbm, v_hbm, leave_ref, same_ref, stays_ref, q_ref, k_ref, v_ref,
                   ids_ref, slot_ref, sems):
    pairs = [(ids_hbm, ids_ref), (slot_hbm, slot_ref), (q_hbm, q_ref), (k_hbm, k_ref), (v_hbm, v_ref)]
    copies = [pltpu.make_async_copy(src, dst, sems.at[i]) for i, (src, dst) in enumerate(pairs)]
    for copy in copies:
        copy.start()
    for copy in copies:
        copy.wait()
    rows, width = q_ref.shape
    units = rows // UNIT
    stays = [slot_ref[u * UNIT] < rows for u in range(units)]
    first = jnp.int32(0)
    for u in range(1, units):
        first = jnp.where(stays[u], first, u * UNIT)
    moves = slot_ref[first] >= rows
    moved = pl.ds(pl.multiple_of(first, UNIT), UNIT)
    for h in range(width // HD):
        cols = pl.ds(h * HD, HD)
        w = softmax(dot(q_ref[moved, cols], k_ref[moved, cols], ((1,), (1,))) * HD**-0.5)
        ctx = dot(v_ref[moved, cols].T, w.astype(jnp.bfloat16), ((1,), (1,)))
        leave_ref[cols, :] = jnp.where(moves, ctx, 0.0).astype(jnp.bfloat16)
    lane_unit = lax.broadcasted_iota(jnp.int32, (1, rows), 1) // UNIT
    lane_ids = jnp.full((1, rows), ids_ref[0], jnp.int32)
    for u in range(1, units):
        lane_ids = jnp.where(lane_unit == u, ids_ref[u * UNIT], lane_ids)
    for u in range(units):
        same_ref[pl.ds(u, 1), :] = (lane_ids == ids_ref[u * UNIT]).astype(jnp.int32)
        stays_ref[pl.ds(u, 1), :] = jnp.full((1, UNIT), stays[u].astype(jnp.int32), jnp.int32)


def leaving_context(image_ids, send_slot, q, k, v):
    rows, width = q.shape
    shapes = [
        jax.ShapeDtypeStruct((width, UNIT), jnp.bfloat16),
        jax.ShapeDtypeStruct((8, rows), jnp.int32),
        jax.ShapeDtypeStruct((8, UNIT), jnp.int32),
    ] + [jax.ShapeDtypeStruct(q.shape, jnp.bfloat16)] * 3
    return pl.pallas_call(
        leaving_kernel,
        in_specs=[pl.BlockSpec(memory_space=pltpu.HBM)] * 5,
        out_specs=[VMEM] * 6,
        out_shape=shapes,
        scratch_shapes=[
            pltpu.SMEM(image_ids.shape, jnp.int32),
            pltpu.SMEM(send_slot.shape, jnp.int32),
            pltpu.SemaphoreType.DMA((5,)),
        ],
        compiler_params=PARAMS,
    )(*[in_hbm(x) for x in (image_ids, send_slot, q, k, v)])


def context_kernel(same_ref, stays_ref, q_ref, k_ref, v_ref, g_hbm, stay_ref, g_ref, sem):
    copy = pltpu.make_async_copy(g_hbm, g_ref, sem)
    copy.start()
    for h in range(q_ref.shape[1] // HD):
        cols = pl.ds(h * HD, HD)
        v_t = v_ref[:, cols].T
        for u in range(q_ref.shape[0] // UNIT):
            rows = pl.ds(u * UNIT, UNIT)
            w = unit_weights(q_ref[rows, cols], k_ref[:, cols], same_ref[u : u + 1, :] != 0)
            ctx = dot(v_t, w.astype(jnp.bfloat16), ((1,), (1,)))
            stay_ref[cols, rows] = jnp.where(stays_ref[u : u + 1, :] != 0, ctx, 0.0).astype(jnp.bfloat16)
    copy.wait()


def staying_context(same, stays, q, k, v, grad_out):
    shapes = [q.shape[::-1], grad_out.shape]
    return pl.pallas_call(
        context_kernel,
        in_specs=[VMEM] * 5 + [pl.BlockSpec(memory_space=pltpu.HBM)],
        out_specs=[VMEM] * 2,
        out_shape=[jax.ShapeDtypeStruct(shape, jnp.bfloat16) for shape in shapes],
        scratch_shapes=[pltpu.SemaphoreType.DMA],
        compiler_params=PARAMS,
    )(same, stays, q, k, v, in_hbm(grad_out))


def in_hbm(x):
    return pltpu.with_memory_space_constraint(x, pltpu.HBM)


def partial_kernel(other, stay_ref, came_ref, g_ref, out_ref):
    me = lax.axis_index("dp")
    y, c = (me // NC) % NY, me % NC
    core = 1 - c if other else c
    ctx_t = jnp.concatenate([stay_ref[...], came_ref[...]], axis=1)
    width = ctx_t.shape[0]
    for n, distance in enumerate(ORDER):
        y_to = (y + NY + distance * (1 - 2 * core)) % NY
        dest = [(i * NY + y_to) * NC + core for i in range(NZ)]
        g = jnp.concatenate([g_ref[:, pl.ds(pl.multiple_of(d * UNIT, UNIT), UNIT)] for d in dest], axis=1)
        part = dot(ctx_t, g, ((1,), (0,))).astype(jnp.bfloat16)
        for i in range(NZ):
            out_ref[pl.ds((n * NZ + i) * width, width), :] = part[:, i * UNIT : (i + 1) * UNIT]


def partial_grad(other, stay, came, grad_out):
    shape = (NY * NZ * stay.shape[0], UNIT)
    return pl.pallas_call(
        functools.partial(partial_kernel, other),
        in_specs=[VMEM, VMEM, VMEM],
        out_specs=VMEM,
        out_shape=jax.ShapeDtypeStruct(shape, jnp.bfloat16),
        compiler_params=PARAMS,
    )(stay, came, grad_out)


def grad_context_kernel(g_ref, w_ref, out_ref):
    step = 1024
    acc = jnp.zeros(out_ref.shape, jnp.float32)
    for i in range(0, g_ref.shape[1], step):
        acc += dot(g_ref[:, i : i + step], w_ref[:, i : i + step], ((1,), (1,)))
    out_ref[...] = acc.astype(jnp.bfloat16)


def grad_context(grad_out, out_weight):
    shape = (grad_out.shape[0], out_weight.shape[0])
    return pl.pallas_call(
        grad_context_kernel,
        in_specs=[VMEM] * 2,
        out_specs=VMEM,
        out_shape=jax.ShapeDtypeStruct(shape, jnp.bfloat16),
        compiler_params=PARAMS,
    )(grad_out, out_weight)


def backward_kernel(same_ref, stays_ref, q_ref, k_ref, v_ref, g_ref, back_ref, dq_ref, dk_ref, dv_ref):
    for h in range(q_ref.shape[1] // HD):
        cols = pl.ds(h * HD, HD)
        k, v = k_ref[:, cols], v_ref[:, cols]
        dk = jnp.zeros(k.shape, jnp.float32)
        dv = jnp.zeros(v.shape, jnp.float32)
        for u in range(q_ref.shape[0] // UNIT):
            rows = pl.ds(u * UNIT, UNIT)
            q = q_ref[rows, cols]
            w = unit_weights(q, k, same_ref[u : u + 1, :] != 0)
            stays = stays_ref[u : u + 1, :] != 0
            g = jnp.where(stays, g_ref[rows, cols].astype(jnp.float32), back_ref[:, cols].astype(jnp.float32))
            g = g.astype(jnp.bfloat16)
            dv += dot(w.astype(jnp.bfloat16), g, ((0,), (0,)))
            dw = dot(g, v, ((1,), (1,)))
            ds = (w * (dw - jnp.sum(w * dw, axis=-1, keepdims=True))).astype(jnp.bfloat16)
            dq_ref[rows, cols] = (dot(ds, k, ((1,), (0,))) * HD**-0.5).astype(jnp.bfloat16)
            dk += dot(ds, q, ((0,), (0,)))
        dk_ref[:, cols] = (dk * HD**-0.5).astype(jnp.bfloat16)
        dv_ref[:, cols] = dv.astype(jnp.bfloat16)


def backward(same, stays, q, k, v, g, back):
    return pl.pallas_call(
        backward_kernel,
        in_specs=[VMEM] * 7,
        out_specs=[VMEM] * 3,
        out_shape=[jax.ShapeDtypeStruct(q.shape, jnp.bfloat16)] * 3,
        compiler_params=PARAMS,
    )(same, stays, q, k, v, g, back)


PLACES = [(z, y, c) for z in range(NZ) for y in range(NY) for c in range(NC)]


def index(z, y, c):
    return (z % NZ * NY + y % NY) * NC + c


def send(block, to):
    return lax.ppermute(block, "dp", [(index(*p), index(*to(*p))) for p in PLACES])


def along_y(step):
    return lambda z, y, c: (z, y + step * (1 - 2 * c), c)


def same_place():
    return [[index(z, y, c) for z in range(NZ)] for y in range(NY) for c in range(NC)]


def sibling(z, y, c):
    return (z, y, 1 - c)


def total(*terms):
    return sum(t.astype(jnp.float32) for t in terms)


def rounded_total(*terms):
    return total(*terms).astype(jnp.bfloat16)


def local(queries, key_rows, value_rows, image_ids, send_slot, out_weight, grad_out):
    row_count, width = queries.shape
    ranks = lax.axis_size("dp")
    leave, same, stays, q, k, v = leaving_context(image_ids, send_slot, queries, key_rows, value_rows)
    came = lax.ppermute(leave, "dp", [(i, (i + 1) % ranks) for i in range(ranks)])
    stay, g_near = staying_context(same, stays, q, k, v, grad_out)
    grad_ctx = grad_context(g_near, out_weight)
    stay, grad_ctx = lax.optimization_barrier((stay, grad_ctx))

    size = NZ * width

    def cut(x):
        return [x[i : i + size] for i in range(0, x.shape[0], size)]

    got = send(partial_grad(True, stay, came, g_near), sibling)
    own = partial_grad(False, stay, came, g_near)
    parts = [rounded_total(*pair) for pair in zip(cut(own), cut(got), strict=True)]
    part = dict(zip(ORDER, lax.optimization_barrier(parts), strict=True))
    far, up, down = send(part[4], along_y(2)), send(part[3], along_y(1)), send(part[-3], along_y(-1))
    near = send(part[1], along_y(1)), send(part[-1], along_y(-1))
    far, up, down = lax.optimization_barrier((far, up, down))

    up, down = rounded_total(part[2], up, far), rounded_total(part[-2], down)
    up, down, tail = lax.optimization_barrier((up, down, grad_ctx[row_count:]))
    up, down = send(up, along_y(2)), send(down, along_y(-2))
    back = lax.ppermute(tail, "dp", [((i + 1) % ranks, i) for i in range(ranks)])
    sums = rounded_total(part[0], up, down, *near).reshape(NZ, -1, UNIT)
    sums, back = lax.optimization_barrier((sums, back))
    sums = lax.all_to_all(sums, "dp", 0, 0, axis_index_groups=same_place())
    grads = backward(same, stays, queries, key_rows, value_rows, grad_ctx, back)
    grad_weight = total(*sums)
    return (*grads, grad_weight)


def solution(mesh):
    placed = (
        P("dp", "fsdp"),
        P("dp", "fsdp"),
        P("dp", "fsdp"),
        P("dp"),
        P("dp"),
        P("fsdp", None),
        P("dp", None),
    )
    return jax.shard_map(
        local,
        mesh=mesh,
        in_specs=placed,
        out_specs=(P("dp", "fsdp"), P("dp", "fsdp"), P("dp", "fsdp"), P("fsdp", "dp")),
        check_vma=False,
    )
```

```python
import functools

import jax
import jax.numpy as jnp
from jax import lax
from jax.experimental import pallas as pl
from jax.experimental.pallas import tpu as pltpu
from jax.sharding import PartitionSpec as P

HD = 128
UNIT = 128
NZ, NY, NC = 3, 8, 2
ORDER = (4, 3, -3, 2, -2, 1, -1, 0)
VMEM = pl.BlockSpec(memory_space=pltpu.VMEM)
PARAMS = pltpu.CompilerParams(vmem_limit_bytes=8 * 1024 * 1024)


def dot(a, b, dims):
    return lax.dot_general(a, b, (dims, ((), ())), preferred_element_type=jnp.float32)


def softmax(scores):
    expo = jnp.exp(scores - jnp.max(scores, axis=-1, keepdims=True))
    return expo / jnp.sum(expo, axis=-1, keepdims=True)


def unit_weights(q, k, mask):
    return softmax(jnp.where(mask, dot(q, k, ((1,), (1,))) * HD**-0.5, -jnp.inf))


def leaving_kernel(ids_hbm, slot_hbm, q_hbm, k_hbm, v_hbm, leave_ref, same_ref, stays_ref, q_ref, k_ref, v_ref,
                   ids_ref, slot_ref, sems):
    pairs = [(ids_hbm, ids_ref), (slot_hbm, slot_ref), (q_hbm, q_ref), (k_hbm, k_ref), (v_hbm, v_ref)]
    copies = [pltpu.make_async_copy(src, dst, sems.at[i]) for i, (src, dst) in enumerate(pairs)]
    for copy in copies:
        copy.start()
    for copy in copies:
        copy.wait()
    rows, width = q_ref.shape
    units = rows // UNIT
    stays = [slot_ref[u * UNIT] < rows for u in range(units)]
    first = jnp.int32(0)
    for u in range(1, units):
        first = jnp.where(stays[u], first, u * UNIT)
    moves = slot_ref[first] >= rows
    moved = pl.ds(pl.multiple_of(first, UNIT), UNIT)
    for h in range(width // HD):
        cols = pl.ds(h * HD, HD)
        w = softmax(dot(q_ref[moved, cols], k_ref[moved, cols], ((1,), (1,))) * HD**-0.5)
        ctx = dot(v_ref[moved, cols].T, w.astype(jnp.bfloat16), ((1,), (1,)))
        leave_ref[cols, :] = jnp.where(moves, ctx, 0.0).astype(jnp.bfloat16)
    lane_unit = lax.broadcasted_iota(jnp.int32, (1, rows), 1) // UNIT
    lane_ids = jnp.full((1, rows), ids_ref[0], jnp.int32)
    for u in range(1, units):
        lane_ids = jnp.where(lane_unit == u, ids_ref[u * UNIT], lane_ids)
    for u in range(units):
        same_ref[pl.ds(u, 1), :] = (lane_ids == ids_ref[u * UNIT]).astype(jnp.int32)
        stays_ref[pl.ds(u, 1), :] = jnp.full((1, UNIT), stays[u].astype(jnp.int32), jnp.int32)


def leaving_context(image_ids, send_slot, q, k, v):
    rows, width = q.shape
    shapes = [
        jax.ShapeDtypeStruct((width, UNIT), jnp.bfloat16),
        jax.ShapeDtypeStruct((8, rows), jnp.int32),
        jax.ShapeDtypeStruct((8, UNIT), jnp.int32),
    ] + [jax.ShapeDtypeStruct(q.shape, jnp.bfloat16)] * 3
    return pl.pallas_call(
        leaving_kernel,
        in_specs=[pl.BlockSpec(memory_space=pltpu.HBM)] * 5,
        out_specs=[VMEM] * 6,
        out_shape=shapes,
        scratch_shapes=[
            pltpu.SMEM(image_ids.shape, jnp.int32),
            pltpu.SMEM(send_slot.shape, jnp.int32),
            pltpu.SemaphoreType.DMA((5,)),
        ],
        compiler_params=PARAMS,
    )(*[in_hbm(x) for x in (image_ids, send_slot, q, k, v)])


def context_kernel(same_ref, stays_ref, q_ref, k_ref, v_ref, g_hbm, stay_ref, g_ref, sem):
    copy = pltpu.make_async_copy(g_hbm, g_ref, sem)
    copy.start()
    for h in range(q_ref.shape[1] // HD):
        cols = pl.ds(h * HD, HD)
        v_t = v_ref[:, cols].T
        for u in range(q_ref.shape[0] // UNIT):
            rows = pl.ds(u * UNIT, UNIT)
            w = unit_weights(q_ref[rows, cols], k_ref[:, cols], same_ref[u : u + 1, :] != 0)
            ctx = dot(v_t, w.astype(jnp.bfloat16), ((1,), (1,)))
            stay_ref[cols, rows] = jnp.where(stays_ref[u : u + 1, :] != 0, ctx, 0.0).astype(jnp.bfloat16)
    copy.wait()


def staying_context(same, stays, q, k, v, grad_out):
    shapes = [q.shape[::-1], grad_out.shape]
    return pl.pallas_call(
        context_kernel,
        in_specs=[VMEM] * 5 + [pl.BlockSpec(memory_space=pltpu.HBM)],
        out_specs=[VMEM] * 2,
        out_shape=[jax.ShapeDtypeStruct(shape, jnp.bfloat16) for shape in shapes],
        scratch_shapes=[pltpu.SemaphoreType.DMA],
        compiler_params=PARAMS,
    )(same, stays, q, k, v, in_hbm(grad_out))


def in_hbm(x):
    return pltpu.with_memory_space_constraint(x, pltpu.HBM)


def partial_kernel(other, stay_ref, came_ref, g_ref, out_ref):
    me = lax.axis_index("dp")
    y, c = (me // NC) % NY, me % NC
    core = 1 - c if other else c
    ctx_t = jnp.concatenate([stay_ref[...], came_ref[...]], axis=1)
    width = ctx_t.shape[0]
    for n, distance in enumerate(ORDER):
        y_to = (y + NY + distance * (1 - 2 * core)) % NY
        dest = [(i * NY + y_to) * NC + core for i in range(NZ)]
        g = jnp.concatenate([g_ref[:, pl.ds(pl.multiple_of(d * UNIT, UNIT), UNIT)] for d in dest], axis=1)
        part = dot(ctx_t, g, ((1,), (0,))).astype(jnp.bfloat16)
        for i in range(NZ):
            out_ref[pl.ds((n * NZ + i) * width, width), :] = part[:, i * UNIT : (i + 1) * UNIT]


def partial_grad(other, stay, came, grad_out):
    shape = (NY * NZ * stay.shape[0], UNIT)
    return pl.pallas_call(
        functools.partial(partial_kernel, other),
        in_specs=[VMEM, VMEM, VMEM],
        out_specs=VMEM,
        out_shape=jax.ShapeDtypeStruct(shape, jnp.bfloat16),
        compiler_params=PARAMS,
    )(stay, came, grad_out)


def grad_context_kernel(g_ref, w_ref, out_ref):
    step = 1024
    acc = jnp.zeros(out_ref.shape, jnp.float32)
    for i in range(0, g_ref.shape[1], step):
        acc += dot(g_ref[:, i : i + step], w_ref[:, i : i + step], ((1,), (1,)))
    out_ref[...] = acc.astype(jnp.bfloat16)


def grad_context(grad_out, out_weight):
    shape = (grad_out.shape[0], out_weight.shape[0])
    return pl.pallas_call(
        grad_context_kernel,
        in_specs=[VMEM] * 2,
        out_specs=VMEM,
        out_shape=jax.ShapeDtypeStruct(shape, jnp.bfloat16),
        compiler_params=PARAMS,
    )(grad_out, out_weight)


def backward_kernel(same_ref, stays_ref, q_ref, k_ref, v_ref, g_ref, back_ref, dq_ref, dk_ref, dv_ref):
    for h in range(q_ref.shape[1] // HD):
        cols = pl.ds(h * HD, HD)
        k, v = k_ref[:, cols], v_ref[:, cols]
        dk = jnp.zeros(k.shape, jnp.float32)
        dv = jnp.zeros(v.shape, jnp.float32)
        for u in range(q_ref.shape[0] // UNIT):
            rows = pl.ds(u * UNIT, UNIT)
            q = q_ref[rows, cols]
            w = unit_weights(q, k, same_ref[u : u + 1, :] != 0)
            stays = stays_ref[u : u + 1, :] != 0
            g = jnp.where(stays, g_ref[rows, cols].astype(jnp.float32), back_ref[:, cols].astype(jnp.float32))
            g = g.astype(jnp.bfloat16)
            dv += dot(w.astype(jnp.bfloat16), g, ((0,), (0,)))
            dw = dot(g, v, ((1,), (1,)))
            ds = (w * (dw - jnp.sum(w * dw, axis=-1, keepdims=True))).astype(jnp.bfloat16)
            dq_ref[rows, cols] = (dot(ds, k, ((1,), (0,))) * HD**-0.5).astype(jnp.bfloat16)
            dk += dot(ds, q, ((0,), (0,)))
        dk_ref[:, cols] = (dk * HD**-0.5).astype(jnp.bfloat16)
        dv_ref[:, cols] = dv.astype(jnp.bfloat16)


def backward(same, stays, q, k, v, g, back):
    return pl.pallas_call(
        backward_kernel,
        in_specs=[VMEM] * 7,
        out_specs=[VMEM] * 3,
        out_shape=[jax.ShapeDtypeStruct(q.shape, jnp.bfloat16)] * 3,
        compiler_params=PARAMS,
    )(same, stays, q, k, v, g, back)


PLACES = [(z, y, c) for z in range(NZ) for y in range(NY) for c in range(NC)]


def index(z, y, c):
    return (z % NZ * NY + y % NY) * NC + c


def send(block, to):
    return lax.ppermute(block, "dp", [(index(*p), index(*to(*p))) for p in PLACES])


def along_y(step):
    return lambda z, y, c: (z, y + step * (1 - 2 * c), c)


def same_place():
    return [[index(z, y, c) for z in range(NZ)] for y in range(NY) for c in range(NC)]


def sibling(z, y, c):
    return (z, y, 1 - c)


def total(*terms):
    return sum(t.astype(jnp.float32) for t in terms)


def rounded_total(*terms):
    return total(*terms).astype(jnp.bfloat16)


def local(queries, key_rows, value_rows, image_ids, send_slot, out_weight, grad_out):
    row_count, width = queries.shape
    ranks = lax.axis_size("dp")
    leave, same, stays, q, k, v = leaving_context(image_ids, send_slot, queries, key_rows, value_rows)
    came = lax.ppermute(leave, "dp", [(i, (i + 1) % ranks) for i in range(ranks)])
    stay, g_near = staying_context(same, stays, q, k, v, grad_out)
    grad_ctx = grad_context(g_near, out_weight)
    stay, grad_ctx = lax.optimization_barrier((stay, grad_ctx))

    size = NZ * width

    def cut(x):
        return [x[i : i + size] for i in range(0, x.shape[0], size)]

    got = send(partial_grad(True, stay, came, g_near), sibling)
    own = partial_grad(False, stay, came, g_near)
    parts = [rounded_total(*pair) for pair in zip(cut(own), cut(got), strict=True)]
    *parts, tail = lax.optimization_barrier((*parts, grad_ctx[row_count:]))
    part = dict(zip(ORDER, parts, strict=True))
    far, up, down = send(part[4], along_y(2)), send(part[3], along_y(1)), send(part[-3], along_y(-1))
    near = send(part[1], along_y(1)), send(part[-1], along_y(-1))
    back = lax.ppermute(tail, "dp", [((i + 1) % ranks, i) for i in range(ranks)])

    up, down = rounded_total(part[2], up, far), rounded_total(part[-2], down)
    up, down = send(up, along_y(2)), send(down, along_y(-2))
    sums = rounded_total(part[0], up, down, *near).reshape(NZ, -1, UNIT)
    grads = backward(same, stays, queries, key_rows, value_rows, grad_ctx, back)
    sums, *grads = lax.optimization_barrier((sums, *grads))
    sums = lax.all_to_all(sums, "dp", 0, 0, axis_index_groups=same_place())
    grad_weight = total(*sums)
    return (*grads, grad_weight)


def solution(mesh):
    placed = (
        P("dp", "fsdp"),
        P("dp", "fsdp"),
        P("dp", "fsdp"),
        P("dp"),
        P("dp"),
        P("fsdp", None),
        P("dp", None),
    )
    return jax.shard_map(
        local,
        mesh=mesh,
        in_specs=placed,
        out_specs=(P("dp", "fsdp"), P("dp", "fsdp"), P("dp", "fsdp"), P("fsdp", "dp")),
        check_vma=False,
    )
```
